32 devices in a mesh: seq: 4 (over z), mp: 8 (over y, x, core).
Axes of the slice: x: 2, y: 2, z: 4, core: 2. Of those that a mesh axis runs over, the one named last changes fastest.
Arguments:
- residual: bfloat16 [4096, 2048], P('seq', 'mp'), may hold values from -6 to 6
- attn_gain: float32 [2048], replicated, may hold values from 0.5 to 1.5
- w_mixer: bfloat16 [2048, 16, 768], P('seq', 'mp'), may hold values from -0.125 to 0.125
- w_gates: bfloat16 [2048, 16, 2], P('seq', 'mp'), may hold values from -0.125 to 0.125
- conv_taps: float32 [4, 16, 512], P(None, 'mp'), may hold values from -2.5 to 2.5
- decay_scale: float32 [16], P('mp'), may hold values from 0.00012207031 to 0.03
- dt_bias: float32 [16], P('mp'), may hold values from -1 to 1
- head_gain: float32 [16, 256], P('mp'), may hold values from 0.5 to 1.5
- w_out: bfloat16 [4096, 2048], P('mp', 'seq'), may hold values from -0.09375 to 0.09375
- ffn_gain: float32 [2048], replicated, may hold values from 0.5 to 1.5
- w_gate: bfloat16 [2048, 5504], P('seq', 'mp'), may hold values from -0.125 to 0.125
- w_up: bfloat16 [2048, 5504], P('seq', 'mp'), may hold values from -0.125 to 0.125
- w_down: bfloat16 [5504, 2048], P('mp', 'seq'), may hold values from -0.078125 to 0.078125
- out_grad: bfloat16 [4096, 2048], P('seq', 'mp'), may hold values from -6 to 6
- doc_ids: int32 [4096], replicated, may hold values from 0 to 2, as said below
Outputs:
- output: bfloat16 [4096, 2048], P('seq', 'mp')
- grad_residual: float32 [4096, 2048], P('seq', 'mp')
- grad_attn_gain: float32 [2048], replicated
- grad_w_mixer: float32 [2048, 16, 768], P('seq', 'mp')
- grad_w_gates: float32 [2048, 16, 2], P('seq', 'mp')
- grad_conv_taps: float32 [4, 16, 512], P(None, 'mp')
- grad_decay_scale: float32 [16], P('mp')
- grad_dt_bias: float32 [16], P('mp')
- grad_head_gain: float32 [16, 256], P('mp')
- grad_w_out: float32 [4096, 2048], P('mp', 'seq')
- grad_ffn_gain: float32 [2048], replicated
- grad_w_gate: float32 [2048, 5504], P('seq', 'mp')
- grad_w_up: float32 [2048, 5504], P('seq', 'mp')
- grad_w_down: float32 [5504, 2048], P('mp', 'seq')
The draws below stay inside these ranges and needn't reach their ends.
Inputs may be any that keep to these rules, and one draw needn't show every extreme that they name: doc_ids never falls, starts at 0 and rises by at most 1 from one token to the next; there are three documents, the second begins among the first 1024 tokens and ends among the last 1024.
All inputs are finite; a program needn't handle non-finite values.
Results may differ from the reference program's by a relative error of at most 0.012.
The reference program's roundings to bfloat16 on the way (of `normed`, `mixed`, `normed2` and `hidden`) count: a program that leaves them out, or rounds other values in their place, can miss the bound.
Values may be sent and summed in bfloat16 or wider, within the bound.
No kernel may reach another device: no remote copies, remote signals or barrier semaphores. Data moves between devices by JAX's collectives and lax.ppermute only.
A program may use at most 256 MiB of HBM per device.

```python
import math
import jax
import jax.numpy as jnp
from jax import lax

D = 2048
H = 16
DK = 128
DV = 256
FF = 5504
SPAN = 64
TOK_DEV = 1024
TOKENS = 4096


def draw_doc_ids(key, part):
    key = jax.random.fold_in(key, 7)
    first_key, last_key = jax.random.split(key, 2)
    opening = jax.random.randint(first_key, (), 1, TOK_DEV)
    closing = jax.random.randint(last_key, (), TOKENS - TOK_DEV, TOKENS - 1)
    places = jnp.arange(TOKENS)
    starts = (places == opening) | (places == closing + 1)
    return jnp.cumsum(starts.astype(jnp.int32)).astype(jnp.int32)


def block_scale(own_key, dims, cuts, smallest, largest):
    def one(position, parts):
        heights = jax.random.uniform(jax.random.fold_in(jax.random.fold_in(own_key, 6), position), (parts,), jnp.float32, smallest / len(cuts), largest / len(cuts))
        return jnp.repeat(jnp.exp(heights), dims[position] // parts).reshape((-1,) + (1,) * (len(dims) - position - 1))

    factor_of = one(*cuts[0])
    for cut in cuts[1:]:
        factor_of = factor_of * one(*cut)
    return factor_of


def normal_values(own_key, dims, deviation, most, cuts=(), kind=jnp.bfloat16):
    array = jax.random.normal(own_key, dims, jnp.float32) * deviation
    if len(cuts) > 0:
        array = block_scale(own_key, dims, cuts, -0.22, 0.18) * array
    return jnp.clip(array, min=-most, max=most).astype(kind)


def setup_inputs(seed: int = 0) -> dict:
    arg_keys = jax.random.split(jax.random.key(seed), 16)
    residual = normal_values(arg_keys[0], (TOKENS, D), 1.0, 6.0, ((0, 4), (1, 8)))
    attn_gain = jnp.clip(1.0 + 0.1 * jax.random.normal(arg_keys[1], (D,), jnp.float32), 0.5, 1.5)
    w_mixer = normal_values(arg_keys[2], (D, H, 2 * DK + 2 * DV), D ** -0.5, 0.125, ((0, 4), (1, 8)))
    w_gates = normal_values(arg_keys[3], (D, H, 2), D ** -0.5, 0.125, ((0, 4), (1, 8)))
    conv_taps = normal_values(arg_keys[4], (4, H, 2 * DK + DV), 0.5, 2.5, ((1, 8),), jnp.float32)
    decay_scale = jnp.clip(jnp.exp(math.log(0.03) - 5.5043554 * jax.random.uniform(arg_keys[5], (H,), jnp.float32) ** block_scale(arg_keys[5], (H,), ((0, 8),), -0.2, 0.2)), 0.00012207031, 0.03)
    dt_bias = jnp.clip(jax.random.uniform(arg_keys[6], (H,), jnp.float32, -1.0, 1.0) * block_scale(arg_keys[6], (H,), ((0, 8),), -0.4, 0.0), -1.0, 1.0)
    head_gain = jnp.clip(1.0 + 0.1 * jax.random.normal(arg_keys[7], (H, DV), jnp.float32), 0.5, 1.5)
    w_out = normal_values(arg_keys[8], (H * DV, D), (H * DV) ** -0.5, 0.09375, ((0, 8), (1, 4)))
    ffn_gain = jnp.clip(1.0 + 0.1 * jax.random.normal(arg_keys[9], (D,), jnp.float32), 0.5, 1.5)
    w_gate = normal_values(arg_keys[10], (D, FF), D ** -0.5, 0.125, ((0, 4), (1, 8)))
    w_up = normal_values(arg_keys[11], (D, FF), D ** -0.5, 0.125, ((0, 4), (1, 8)))
    w_down = normal_values(arg_keys[12], (FF, D), FF ** -0.5, 0.078125, ((0, 8), (1, 4)))
    out_grad = normal_values(arg_keys[13], (TOKENS, D), 1.0, 6.0, ((0, 4), (1, 8)))
    doc_ids = draw_doc_ids(jax.random.fold_in(arg_keys[15], 71), 0)
    return {"residual": residual, "attn_gain": attn_gain, "w_mixer": w_mixer, "w_gates": w_gates, "conv_taps": conv_taps, "decay_scale": decay_scale, "dt_bias": dt_bias, "head_gain": head_gain, "w_out": w_out, "ffn_gain": ffn_gain, "w_gate": w_gate, "w_up": w_up, "w_down": w_down, "out_grad": out_grad, "doc_ids": doc_ids}


@jax.custom_vjp
def low(v):
    return lax.optimization_barrier(v.astype(jnp.bfloat16)).astype(jnp.float32)

@jax.custom_vjp
def low_back(v):
    return v

def low_keep(v):
    return (low(v), None)

def low_pass(kept, grad):
    return (grad,)

def back_keep(v):
    return (v, None)

def back_low(kept, grad):
    return (low(grad),)
low.defvjp(low_keep, low_pass)
low_back.defvjp(back_keep, back_low)

def matmul(left_mat, right_mat):
    return jnp.dot(left_mat, right_mat, precision=lax.Precision.HIGHEST)

def rms_norm(values, gain_row):
    return values * lax.rsqrt(lax.optimization_barrier(jnp.mean(values * values, axis=-1, keepdims=True)) + 1e-05) * gain_row

def gated_norm(head_vals, gate_cols, gain_row):
    inverse = lax.rsqrt(lax.optimization_barrier(jnp.mean(head_vals * head_vals, axis=-1, keepdims=True)) + 1e-05)
    return head_vals * inverse * gain_row * jax.nn.silu(gate_cols)

def conv_gates(extended, extended_ids, gate_vals, tap_weights, scales, biases):
    tok_rows = gate_vals.shape[0]
    convolved = jnp.zeros((tok_rows,) + extended.shape[1:], jnp.float32)
    for offset in range(4):
        lagged = extended[3 - offset:3 - offset + tok_rows]
        same_doc = (extended_ids[3 - offset:3 - offset + tok_rows] == extended_ids[3:]).astype(jnp.float32)
        convolved = convolved + tap_weights[offset] * lagged * same_doc[:, None, None]
    activated = jax.nn.silu(convolved)
    queries = activated[..., :DK]
    key_rows = activated[..., DK:2 * DK]
    value_rows = activated[..., 2 * DK:]
    queries = queries * lax.rsqrt(lax.optimization_barrier(jnp.sum(queries * queries, axis=-1, keepdims=True)) + 1e-06) * DK ** (-0.5)
    key_rows = key_rows * lax.rsqrt(lax.optimization_barrier(jnp.sum(key_rows * key_rows, axis=-1, keepdims=True)) + 1e-06)
    log_decay = -scales * jax.nn.softplus(gate_vals[..., 0] + biases)
    beta_gates = jax.nn.sigmoid(gate_vals[..., 1])
    return (queries, key_rows, value_rows, log_decay, beta_gates)

def solve_lower(system, right_side):
    return lax.linalg.triangular_solve(system, right_side, left_side=True, lower=True, unit_diagonal=True)

def span_prep(queries, key_rows, value_rows, log_decay, beta_gates, span_ids, prior_id):
    span_len = queries.shape[0]
    cumulative = jnp.cumsum(log_decay)
    row_index = lax.broadcasted_iota(jnp.int32, (span_len, span_len), 0)
    col_index = lax.broadcasted_iota(jnp.int32, (span_len, span_len), 1)
    same_doc = span_ids[:, None] == span_ids[None, :]
    inside = (row_index >= col_index) & same_doc
    strict = (row_index > col_index) & same_doc
    spread = jnp.where(inside, cumulative[:, None] - cumulative[None, :], 0.0)
    decays = jnp.where(inside, jnp.exp(spread), 0.0)
    carried = jnp.exp(cumulative) * (span_ids == prior_id).astype(jnp.float32)
    lower_part = jnp.where(strict, decays * matmul(key_rows, key_rows.T), 0.0) * beta_gates[:, None]
    system = jnp.eye(span_len, dtype=jnp.float32) + lower_part
    weighted_keys = solve_lower(system, (beta_gates * carried)[:, None] * key_rows)
    weighted_vals = solve_lower(system, beta_gates[:, None] * value_rows)
    scores = decays * matmul(queries, key_rows.T)
    return (weighted_keys, weighted_vals, scores, carried[:, None] * queries, decays[-1][:, None] * key_rows, carried[-1])

def state_step(carried_state, prepared):
    weighted_keys, weighted_vals, scores, decayed_q, end_keys, end_gain = prepared
    pseudo_vals = weighted_vals - matmul(weighted_keys, carried_state.T)
    outputs = matmul(decayed_q, carried_state.T) + matmul(scores, pseudo_vals)
    next_state = end_gain * carried_state + matmul(pseudo_vals.T, end_keys)
    return (next_state, outputs)

def delta_rule(queries, key_rows, value_rows, log_decay, beta_gates, doc_ids):
    span_count = queries.shape[0] // SPAN

    def by_span(tensor):
        return tensor.reshape((span_count, SPAN) + tensor.shape[1:])
    padded = jnp.concatenate([jnp.full((1,), -1, jnp.int32), doc_ids])
    priors = padded[:-1].reshape(span_count, SPAN)[:, 0]

    def advance(carried_state, pieces):
        return state_step(carried_state, span_prep(*pieces))
    start_state = jnp.zeros((value_rows.shape[-1], key_rows.shape[-1]), jnp.float32)
    ignored, outputs = lax.scan(jax.checkpoint(advance), start_state, (by_span(queries), by_span(key_rows), by_span(value_rows), by_span(log_decay), by_span(beta_gates), by_span(doc_ids), priors))
    return outputs.reshape(-1, value_rows.shape[-1])

def layer_forward(residual, attn_gain, w_mixer, w_gates, conv_taps, decay_scale, dt_bias, head_gain, w_out, ffn_gain, w_gate, w_up, w_down, doc_ids):
    tok_rows, model_width = residual.shape
    head_count = w_mixer.shape[1]
    normed = low(rms_norm(residual, attn_gain))
    projected = low_back(matmul(normed, w_mixer.reshape(model_width, -1))).reshape(tok_rows, head_count, -1)
    gate_pre = low_back(matmul(normed, w_gates.reshape(model_width, -1))).reshape(tok_rows, head_count, 2)
    conv_width = 2 * DK + DV
    extended = jnp.concatenate([jnp.zeros((3, head_count, conv_width), jnp.float32), projected[..., :conv_width]], axis=0)
    extended_ids = jnp.concatenate([jnp.full((3,), -1, jnp.int32), doc_ids])
    queries, key_rows, value_rows, log_decay, beta_gates = conv_gates(extended, extended_ids, gate_pre, conv_taps, decay_scale, dt_bias)
    head_vals = jax.vmap(delta_rule, in_axes=(1, 1, 1, 1, 1, None), out_axes=1)(queries, key_rows, value_rows, log_decay, beta_gates, doc_ids)
    mixed = low(gated_norm(head_vals, projected[..., conv_width:], head_gain)).reshape(tok_rows, -1)
    middle = residual + low_back(matmul(mixed, w_out))
    normed2 = low(rms_norm(middle, ffn_gain))
    gate_val = low_back(matmul(normed2, w_gate))
    up_val = low_back(matmul(normed2, w_up))
    hidden = low(jax.nn.silu(gate_val) * up_val)
    return middle + matmul(hidden, w_down)

def reference(residual, attn_gain, w_mixer, w_gates, conv_taps, decay_scale, dt_bias, head_gain, w_out, ffn_gain, w_gate, w_up, w_down, out_grad, doc_ids):
    weights = tuple((weight_arr.astype(jnp.float32) for weight_arr in (residual, attn_gain, w_mixer, w_gates, conv_taps, decay_scale, dt_bias, head_gain, w_out, ffn_gain, w_gate, w_up, w_down)))
    doc_numbers = doc_ids.astype(jnp.int32)

    def forward(*inputs):
        return layer_forward(*inputs, doc_numbers)
    result, pullback = jax.vjp(forward, *weights)
    gradients = pullback(out_grad.astype(jnp.float32))
    return (result.astype(jnp.bfloat16), gradients[0], gradients[1], gradients[2], gradients[3], gradients[4], gradients[5], gradients[6], gradients[7], gradients[8], gradients[9], gradients[10], gradients[11], gradients[12])
```

```python
import functools
import jax
import jax.numpy as jnp
from jax import lax
from jax.experimental import pallas as pl
from jax.experimental.pallas import tpu as pltpu
from jax.sharding import PartitionSpec as P

DK = 128
DV = 256
CHUNK = 128
GATE_LANES = 8
F32 = jnp.float32
BF16 = jnp.bfloat16
NN = (((1,), (0,)), ((), ()))
NT = (((1,), (1,)), ((), ()))
VMEM_LIMIT = 48 * 1024 * 1024


def d1(left, right, dims=NN):
    return lax.dot_general(
        left.astype(BF16), right.astype(BF16), dims, preferred_element_type=F32
    )


def dx(left, right, dims=NN):
    if left.dtype == BF16 and right.dtype == BF16:
        return d1(left, right, dims)
    return d3(left.astype(F32), right.astype(F32), dims)


def split(value):
    high = value.astype(BF16)
    return high, (value - high.astype(F32)).astype(BF16)


def d3(left, right, dims=NN):
    lh, ll = split(left)
    rh, rl = split(right)
    return d1(lh, rh, dims) + (d1(lh, rl, dims) + d1(ll, rh, dims))


def params():
    return pltpu.CompilerParams(vmem_limit_bytes=VMEM_LIMIT)


def cost(flops, nbytes):
    return pl.CostEstimate(flops=int(flops), bytes_accessed=int(nbytes), transcendentals=0)


def spec(shape, index_map):
    return pl.BlockSpec(shape, index_map)


def rows_cols():
    row = lax.broadcasted_iota(jnp.int32, (CHUNK, CHUNK), 0)
    col = lax.broadcasted_iota(jnp.int32, (CHUNK, CHUNK), 1)
    return row, col


def to_row(column, row, col):
    return jnp.sum(jnp.where(row == col, column, 0.0), axis=0, keepdims=True)


def to_col(line, row, col):
    return jnp.sum(jnp.where(row == col, line, 0.0), axis=1, keepdims=True)


def decay_parts(gates, row, col):
    log_decay, beta, ids, prior = (gates[:, i : i + 1] for i in range(4))
    cum_row = jnp.sum(jnp.where(row <= col, log_decay, 0.0), axis=0, keepdims=True)
    cum_col = to_col(cum_row, row, col)
    same = ids == to_row(ids, row, col)
    inside = (row >= col) & same
    decays = jnp.where(inside, jnp.exp(jnp.where(inside, cum_col - cum_row, 0.0)), 0.0)
    carried = jnp.where(ids == prior, jnp.exp(cum_col), 0.0)
    last_ids = ids[CHUNK - 1 : CHUNK]
    last_cum = cum_col[CHUNK - 1 : CHUNK]
    to_end = jnp.where(ids == last_ids, jnp.exp(last_cum - cum_col), 0.0)
    return beta, decays, carried, to_end


def invert(lowers, row, col):
    eye = jnp.where(row == col, 1.0, 0.0)
    found = None
    shift = 0
    while (1 << shift) < CHUNK:
        mask = ((row >> (shift + 1)) == (col >> (shift + 1))) & (
            (row >> shift) > (col >> shift)
        )
        masked = [jnp.where(mask, lower, 0.0) for lower in lowers]
        if found is None:
            found = [eye - m for m in masked]
        else:
            low = [x.astype(BF16) for x in found]
            inner = [d1(m, x) for m, x in zip(masked, low)]
            outer = [d1(x, y) for x, y in zip(low, inner)]
            found = [x - y for x, y in zip(found, outer)]
        shift += 1
    rest = [d3(lower, x) for lower, x in zip(lowers, found)]
    rest = [(eye - x) - r for x, r in zip(found, rest)]
    return [x + d1(x, r) for x, r in zip(found, rest)]


def prep_kernel(
    group, qk_ref, gt_ref, t_ref, tt_ref, a_ref, at_ref, lk_ref, w_ref, p_ref, pt_ref, m_ref, mt_ref
):
    row, col = rows_cols()
    queries, keys, parts = [], [], []
    for c in range(group):
        block = qk_ref[c * CHUNK : (c + 1) * CHUNK, :]
        queries.append(block[:, :DK])
        keys.append(block[:, DK:])
        parts.append(decay_parts(gt_ref[0, c * CHUNK : (c + 1) * CHUNK, :], row, col))
    gram = [d3(k, k, NT) for k in keys]
    scores = [dx(q, k, NT) for q, k in zip(queries, keys)]
    kept = [jnp.where(row > col, p[1] * g, 0.0) for p, g in zip(parts, gram)]
    lowers = [x * p[0] for x, p in zip(kept, parts)]
    inverses = invert(lowers, row, col)
    eye = jnp.where(row == col, 1.0, 0.0)
    for c in range(group):
        beta, decays, carried, to_end = parts[c]
        inverse = inverses[c]
        t_ref[0, c] = inverse
        tt_ref[0, c] = inverses[c].T
        score = decays * scores[c]
        a_ref[0, c] = score
        at_ref[0, c] = score.T
        lk_ref[0, c] = kept[c]
        wkeys = dx(inverse, (beta * carried) * keys[c])
        w_ref[0, c] = wkeys
        reach = carried * queries[c] - dx(score, wkeys)
        p_ref[0, c] = reach
        pt_ref[0, c] = reach.T
        end_keys = to_end * keys[c]
        step = carried[CHUNK - 1 : CHUNK] * eye - dx(end_keys.T, wkeys)
        m_ref[0, c] = step
        mt_ref[0, c] = step.T


def delta_prep(qk, gates):
    heads, tokens, _ = gates.shape
    count = tokens // CHUNK
    group = min(4, count)
    rows = group * CHUNK
    low = jax.ShapeDtypeStruct((heads, count, CHUNK, CHUNK), F32)
    wide = jax.ShapeDtypeStruct((heads, count, DK, DK), F32)
    out_spec = spec((1, group, CHUNK, CHUNK), lambda h, g: (h, g, 0, 0))
    return pl.pallas_call(
        functools.partial(prep_kernel, group),
        grid=(heads, count // group),
        in_specs=[
            spec((rows, 2 * DK), lambda h, g: (g, 2 * h)),
            spec((1, rows, GATE_LANES), lambda h, g: (h, g, 0)),
        ],
        out_specs=[out_spec] * 10,
        out_shape=[low] * 8 + [wide] * 2,
        compiler_params=params(),
        cost_estimate=cost(heads * count * 40 * 2 * CHUNK**3 * 8, heads * count * CHUNK * CHUNK * 24),
        name="delta_prep",
    )(qk, gates)


def trans_kernel(heads, count, m_ref, mt_ref, fwd_ref, back_ref):
    row, col = rows_cols()
    eye = jnp.where(row == col, 1.0, 0.0)
    fwd = [eye] * heads
    back = [eye] * heads
    for h in range(heads):
        fwd_ref[h, 0] = eye
        back_ref[h, count] = eye
    for c in range(count):
        if c == 0:
            fwd = [m_ref[h, 0] for h in range(heads)]
            back = [mt_ref[h, count - 1] for h in range(heads)]
        else:
            fwd = [d3(m_ref[h, c], fwd[h]) for h in range(heads)]
            back = [d3(mt_ref[h, count - 1 - c], back[h]) for h in range(heads)]
        for h in range(heads):
            fwd_ref[h, c + 1] = fwd[h]
            back_ref[h, count - 1 - c] = back[h]


def delta_trans(steps, steps_turned):
    heads, count = steps.shape[:2]
    shape = jax.ShapeDtypeStruct((heads, count + 1, DK, DK), F32)
    return pl.pallas_call(
        functools.partial(trans_kernel, heads, count),
        out_shape=[shape, shape],
        compiler_params=params(),
        cost_estimate=cost(heads * count * 6 * 2 * DK**3 * 8, heads * count * DK * DK * 16),
        name="delta_trans",
    )(steps, steps_turned)


def values_kernel(
    heads, group, qkv_ref, gt_ref, t_ref, a_ref, m_ref, ut_ref, o_ref, s_ref, end_ref, state
):
    @pl.when(pl.program_id(0) == 0)
    def _():
        state[...] = jnp.zeros_like(state)

    row, col = rows_cols()
    pairs = [(h, c) for c in range(group) for h in range(heads)]
    offsets = {}
    for h, c in pairs:
        at = slice(c * CHUNK, (c + 1) * CHUNK)
        beta, _, _, to_end = decay_parts(gt_ref[h, at, :], row, col)
        pseudo = dx(t_ref[h, c], beta * qkv_ref[at, (2 * h + 1) * DV : (2 * h + 2) * DV])
        ut_ref[h, c] = pseudo
        o_ref[at, h * DV : (h + 1) * DV] = dx(a_ref[h, c], pseudo)
        end_keys = to_end * qkv_ref[at, (4 * h + 1) * DK : (4 * h + 2) * DK]
        offsets[h, c] = dx(end_keys.T, pseudo)
    held = [state[h] for h in range(heads)]
    for c in range(group):
        for h in range(heads):
            s_ref[h, c] = held[h]
        held = [d3(m_ref[h, c], held[h]) + offsets[h, c] for h in range(heads)]
    for h in range(heads):
        state[h] = held[h]
        end_ref[h] = held[h]


def delta_values(qkv, gates, inverse, scores, steps):
    heads, tokens, _ = gates.shape
    count = tokens // CHUNK
    group = min(4, count)
    rows = group * CHUNK
    square = spec((heads, group, CHUNK, CHUNK), lambda g: (0, g, 0, 0))
    tall = spec((heads, group, CHUNK, DV), lambda g: (0, g, 0, 0))
    return pl.pallas_call(
        functools.partial(values_kernel, heads, group),
        grid=(count // group,),
        in_specs=[
            spec((rows, heads * 2 * DV), lambda g: (g, 0)),
            spec((heads, rows, GATE_LANES), lambda g: (0, g, 0)),
            square,
            square,
            square,
        ],
        out_specs=[
            tall,
            spec((rows, heads * DV), lambda g: (g, 0)),
            tall,
            spec((heads, DK, DV), lambda g: (0, 0, 0)),
        ],
        out_shape=[
            jax.ShapeDtypeStruct((heads, count, CHUNK, DV), F32),
            jax.ShapeDtypeStruct((tokens, heads * DV), F32),
            jax.ShapeDtypeStruct((heads, count, DK, DV), F32),
            jax.ShapeDtypeStruct((heads, DK, DV), F32),
        ],
        scratch_shapes=[pltpu.VMEM((heads, DK, DV), F32)],
        compiler_params=params(),
        cost_estimate=cost(heads * count * 12 * 2 * CHUNK**3 * 8, heads * count * CHUNK * 4000),
        name="delta_values",
    )(qkv, gates, inverse, scores, steps)


def output_kernel(
    heads, group, start_ref, s0_ref, tc_ref, p_ref, w_ref, ut_ref, o0_ref, gain_ref, *refs
):
    g_refs, (mixed_ref, o_ref, s_ref, u_ref) = refs[:heads], refs[heads:]
    for c in range(group):
        for h in range(heads):
            at = slice(c * CHUNK, (c + 1) * CHUNK)
            cols = slice(h * DV, (h + 1) * DV)
            held = s0_ref[h, c] + d3(tc_ref[h, c], start_ref[h])
            low = held
            s_ref[h, c] = low
            u_ref[h, c] = (ut_ref[h, c].astype(F32) - dx(w_ref[h, c], low))
            out = o0_ref[at, cols] + dx(p_ref[h, c], low)
            o_ref[at, cols] = out
            gate = g_refs[h][at, :]
            inv = lax.rsqrt(jnp.mean(out * out, axis=-1, keepdims=True) + 1e-05)
            mixed = out * inv * gain_ref[h : h + 1, :] * (gate * jax.nn.sigmoid(gate))
            mixed_ref[at, cols] = mixed.astype(BF16)


def gate_specs(heads, rows, place):
    return [
        spec((rows, DV), functools.partial(lambda h, g: (place(g), 3 * h + 2), h))
        for h in range(heads)
    ]


def delta_output(start, states, trans, reach, wkeys, pseudo, local_out, raw, gain):
    heads, count = states.shape[:2]
    tokens = count * CHUNK
    group = min(2, count)
    rows = group * CHUNK
    square = spec((heads, group, CHUNK, CHUNK), lambda g: (0, g, 0, 0))
    tall = spec((heads, group, CHUNK, DV), lambda g: (0, g, 0, 0))
    flat = spec((rows, heads * DV), lambda g: (g, 0))
    low = jax.ShapeDtypeStruct((heads, count, CHUNK, DV), F32)
    return pl.pallas_call(
        functools.partial(output_kernel, heads, group),
        grid=(count // group,),
        in_specs=[
            spec((heads, DK, DV), lambda g: (0, 0, 0)),
            tall,
            square,
            square,
            square,
            tall,
            flat,
            spec((heads, DV), lambda g: (0, 0)),
        ]
        + gate_specs(heads, rows, lambda g: g),
        out_specs=[flat, flat, tall, tall],
        out_shape=[
            jax.ShapeDtypeStruct((tokens, heads * DV), BF16),
            jax.ShapeDtypeStruct((tokens, heads * DV), F32),
            low,
            low,
        ],
        compiler_params=params(),
        cost_estimate=cost(heads * count * 10 * 2 * CHUNK**3 * 8, heads * count * CHUNK * 6000),
        name="delta_output",
    )(start, states, trans, reach, wkeys, pseudo, local_out, gain, *([raw] * heads))


def tail_kernel(
    heads, group, dm_ref, o_ref, gain_ref, pt_ref, mt_ref, *refs
):
    g_refs = refs[:heads]
    do_ref, dg_ref, dgain_ref, ds_ref, dstart_ref, state = refs[heads:]

    @pl.when(pl.program_id(0) == 0)
    def _():
        state[...] = jnp.zeros_like(state)
        dgain_ref[...] = jnp.zeros_like(dgain_ref)

    pushed = {}
    for c in range(group):
        for h in range(heads):
            at = slice(c * CHUNK, (c + 1) * CHUNK)
            cols = slice(h * DV, (h + 1) * DV)
            out = o_ref[at, cols]
            gate = g_refs[h][at, :]
            back = dm_ref[at, cols]
            gain = gain_ref[h : h + 1, :]
            sig = jax.nn.sigmoid(gate)
            silu = gate * sig
            inv = lax.rsqrt(jnp.mean(out * out, axis=-1, keepdims=True) + 1e-05)
            hat = out * inv
            dgain_ref[h : h + 1, :] += jnp.sum(back * hat * silu, axis=0, keepdims=True)
            scaled = back * gain
            dg_ref[at, cols] = (scaled * hat * (sig * (1.0 + gate * (1.0 - sig)))).astype(BF16)
            dhat = scaled * silu
            dout = inv * (dhat - hat * jnp.mean(dhat * hat, axis=-1, keepdims=True))
            low = dout
            do_ref[at, cols] = low
            pushed[h, c] = dx(pt_ref[h, c], low)
    held = [state[h] for h in range(heads)]
    for c in reversed(range(group)):
        for h in range(heads):
            ds_ref[h, c] = held[h]
        held = [d3(mt_ref[h, c], held[h]) + pushed[h, c] for h in range(heads)]
    for h in range(heads):
        state[h] = held[h]
        dstart_ref[h] = held[h]


def delta_tail(grad_mixed, outs, raw, gain, reach_turned, steps_turned):
    heads, count = steps_turned.shape[:2]
    tokens = count * CHUNK
    group = min(2, count)
    rows = group * CHUNK
    last = count // group - 1
    square = spec((heads, group, CHUNK, CHUNK), lambda g: (0, last - g, 0, 0))
    tall = spec((heads, group, CHUNK, DV), lambda g: (0, last - g, 0, 0))
    flat = spec((rows, heads * DV), lambda g: (last - g, 0))
    return pl.pallas_call(
        functools.partial(tail_kernel, heads, group),
        grid=(count // group,),
        in_specs=[flat, flat, spec((heads, DV), lambda g: (0, 0)), square, square]
        + gate_specs(heads, rows, lambda g: last - g),
        out_specs=[
            flat,
            flat,
            spec((heads, DV), lambda g: (0, 0)),
            tall,
            spec((heads, DK, DV), lambda g: (0, 0, 0)),
        ],
        out_shape=[
            jax.ShapeDtypeStruct((tokens, heads * DV), F32),
            jax.ShapeDtypeStruct((tokens, heads * DV), BF16),
            jax.ShapeDtypeStruct((heads, DV), F32),
            jax.ShapeDtypeStruct((heads, count, DK, DV), F32),
            jax.ShapeDtypeStruct((heads, DK, DV), F32),
        ],
        scratch_shapes=[pltpu.VMEM((heads, DK, DV), F32)],
        compiler_params=params(),
        cost_estimate=cost(heads * count * 10 * 2 * CHUNK**3 * 8, heads * count * CHUNK * 6000),
        name="delta_tail",
    )(grad_mixed, outs, gain, reach_turned, steps_turned, *([raw] * heads))


def grads_kernel(
    heads, group, end_ref, qkv_ref, gt_ref, tt_ref, a_ref, at_ref, lk_ref, u_ref, s_ref,
    ds_ref, back_ref, do_ref, dqkv_ref, dgt_ref,
):
    row, col = rows_cols()
    lane = lax.broadcasted_iota(jnp.int32, (CHUNK, GATE_LANES), 1)
    pairs = [(h, c) for c in range(group) for h in range(heads)]
    at = {(h, c): slice(c * CHUNK, (c + 1) * CHUNK) for h, c in pairs}
    parts = {(h, c): decay_parts(gt_ref[h, at[h, c], :], row, col) for h, c in pairs}
    keys = {(h, c): qkv_ref[at[h, c], (4 * h + 1) * DK : (4 * h + 2) * DK] for h, c in pairs}
    queries = {(h, c): qkv_ref[at[h, c], 4 * h * DK : (4 * h + 1) * DK] for h, c in pairs}
    vals = {(h, c): qkv_ref[at[h, c], (2 * h + 1) * DV : (2 * h + 2) * DV] for h, c in pairs}
    douts = {(h, c): do_ref[at[h, c], h * DV : (h + 1) * DV] for h, c in pairs}
    after = {(h, c): ds_ref[h, c] + d3(back_ref[h, c], end_ref[h]) for h, c in pairs}
    after_low = {p: after[p] for p in pairs}
    du = {
        (h, c): dx(at_ref[h, c], douts[h, c])
        + dx(parts[h, c][3] * keys[h, c], after_low[h, c])
        for h, c in pairs
    }
    x = {(h, c): dx(tt_ref[h, c], du[h, c]) for h, c in pairs}
    x_low = {p: x[p] for p in pairs}
    y = {(h, c): -dx(x_low[h, c], s_ref[h, c], NT) for h, c in pairs}
    da = {(h, c): dx(douts[h, c], u_ref[h, c], NT) for h, c in pairs}
    dqd = {(h, c): dx(douts[h, c], s_ref[h, c], NT) for h, c in pairs}
    dke = {(h, c): dx(u_ref[h, c], after_low[h, c], NT) for h, c in pairs}
    dl = {(h, c): dx(x_low[h, c], u_ref[h, c], NT) for h, c in pairs}
    for h, c in pairs:
        p = (h, c)
        beta, decays, carried, to_end = parts[p]
        key, query = keys[p], queries[p]
        kept = lk_ref[h, c].astype(F32)
        low_grad = jnp.where(row > col, -dl[p], 0.0)
        dg = jnp.sum(s_ref[h, c].astype(F32) * after[p], axis=0, keepdims=True)
        dg = jnp.sum(dg, axis=1, keepdims=True)
        yk = jnp.sum(y[p] * key, axis=-1, keepdims=True)
        dbeta = jnp.sum(x[p] * vals[p], axis=-1, keepdims=True) + carried * yk
        dbeta = dbeta + jnp.sum(low_grad * kept, axis=-1, keepdims=True)
        dcarried = beta * yk + jnp.sum(dqd[p] * query, axis=-1, keepdims=True)
        dend = jnp.sum(dke[p] * key, axis=-1, keepdims=True) * to_end
        scaled = low_grad * beta
        gram = scaled * decays
        score = da[p] * decays
        dqkv_ref[at[p], (2 * h + 1) * DV : (2 * h + 2) * DV] = beta * x[p]
        dqkv_ref[at[p], 4 * h * DK : (4 * h + 1) * DK] = carried * dqd[p] + dx(score, key)
        dqkv_ref[at[p], (4 * h + 1) * DK : (4 * h + 2) * DK] = (
            (beta * carried) * y[p]
            + to_end * dke[p]
            + dx(gram + gram.T, key)
            + dx(score.T, query)
        )
        spread = scaled * kept + da[p] * a_ref[h, c].astype(F32)
        dcum = jnp.sum(spread, axis=-1, keepdims=True)
        dcum = dcum - to_col(jnp.sum(spread, axis=0, keepdims=True), row, col)
        dcum = dcum - dend + dcarried * carried
        tail = jnp.sum(dend, axis=0, keepdims=True) + dg * carried[CHUNK - 1 : CHUNK]
        line = jnp.sum(jnp.where(row >= col, dcum, 0.0), axis=0, keepdims=True) + tail
        dlog = to_col(line, row, col)
        dgt_ref[h, at[p], :] = jnp.where(lane == 0, dlog, jnp.where(lane == 1, dbeta, 0.0))


def delta_grads(grad_end, qkv, gates, inv_turned, scores, scores_turned, kept, u, s, ds, back, dout):
    heads, tokens, _ = gates.shape
    count = tokens // CHUNK
    group = min(2, count)
    rows = group * CHUNK
    square = spec((heads, group, CHUNK, CHUNK), lambda g: (0, g, 0, 0))
    tall = spec((heads, group, CHUNK, DV), lambda g: (0, g, 0, 0))
    flat = spec((rows, heads * DV), lambda g: (g, 0))
    gate_spec = spec((heads, rows, GATE_LANES), lambda g: (0, g, 0))
    wide = spec((rows, heads * 2 * DV), lambda g: (g, 0))
    return pl.pallas_call(
        functools.partial(grads_kernel, heads, group),
        grid=(count // group,),
        in_specs=[
            spec((heads, DK, DV), lambda g: (0, 0, 0)),
            wide,
            gate_spec,
            square,
            square,
            square,
            square,
            tall,
            tall,
            tall,
            square,
            flat,
        ],
        out_specs=[wide, gate_spec],
        out_shape=[
            jax.ShapeDtypeStruct((tokens, heads * 2 * DV), F32),
            jax.ShapeDtypeStruct((heads, tokens, GATE_LANES), F32),
        ],
        compiler_params=params(),
        cost_estimate=cost(heads * count * 30 * 2 * CHUNK**3 * 8, heads * count * CHUNK * 12000),
        name="delta_grads",
    )(grad_end, qkv, gates, inv_turned, scores, scores_turned, kept, u, s, ds, back, dout)


def front_act(x, rim, mask_ref, taps, tokens):
    extended = jnp.concatenate([rim, x], axis=0)
    lags = [x]
    for lag in range(1, 4):
        moved = pltpu.roll(extended, lag, 0)[8:]
        lags.append(moved * mask_ref[:, 3 + lag : 4 + lag])
    conv = taps[0:1] * lags[0]
    for lag in range(1, 4):
        conv = conv + taps[lag : lag + 1] * lags[lag]
    return conv, lags


def front_kernel(x_ref, rim_ref, mask_ref, taps_ref, y_ref):
    tokens = x_ref.shape[0]
    conv, _ = front_act(x_ref[...], rim_ref[...], mask_ref, taps_ref[...], tokens)
    act = conv * jax.nn.sigmoid(conv)
    kind = pl.program_id(0) & 3

    @pl.when(kind < 2)
    def _():
        inv = lax.rsqrt(jnp.sum(act * act, axis=-1, keepdims=True) + 1e-06)
        y_ref[...] = act * (inv * jnp.where(kind == 0, DK**-0.5, 1.0))

    @pl.when(kind >= 2)
    def _():
        y_ref[...] = act


def raw_block(c):
    return (c >> 2) * 6 + (c & 3)


def front(raw, rim, masks, taps):
    tokens, cols = raw.shape[0], taps.shape[1]
    block = spec((tokens, DK), lambda c: (0, c))
    return pl.pallas_call(
        front_kernel,
        grid=(cols // DK,),
        in_specs=[
            spec((tokens, DK), lambda c: (0, raw_block(c))),
            spec((8, DK), lambda c: (0, raw_block(c))),
            spec((tokens, 8), lambda c: (0, 0)),
            spec((4, DK), lambda c: (0, c)),
        ],
        out_specs=block,
        out_shape=jax.ShapeDtypeStruct((tokens, cols), F32),
        compiler_params=params(),
        cost_estimate=cost(tokens * cols * 40, tokens * cols * 8),
        name="front",
    )(raw, rim, masks, taps)


def front_back_kernel(
    x_ref, rim_ref, mask_ref, taps_ref, dy_ref, dg_ref, dx_ref, edge_ref, drim_ref, dtaps_ref
):
    tokens = x_ref.shape[0]
    kind = lax.rem(pl.program_id(0), 6)

    @pl.when(kind >= 4)
    def _():
        grad = dg_ref[...]
        dx_ref[...] = grad
        edge_ref[...] = grad[tokens - 16 :].astype(F32)
        drim_ref[...] = jnp.zeros((8, DK), F32)
        dtaps_ref[...] = jnp.zeros((4, DK), F32)

    def through(normalize):
        taps = taps_ref[...]
        conv, lags = front_act(x_ref[...], rim_ref[...], mask_ref, taps, tokens)
        sig = jax.nn.sigmoid(conv)
        back = dy_ref[...]
        if normalize:
            act = conv * sig
            inv = lax.rsqrt(jnp.sum(act * act, axis=-1, keepdims=True) + 1e-06)
            unit = act * inv
            back = back * jnp.where(kind == 0, DK**-0.5, 1.0)
            back = inv * (back - unit * jnp.sum(back * unit, axis=-1, keepdims=True))
        dconv = back * (sig * (1.0 + conv * (1.0 - sig)))
        zeros = jnp.zeros((8, DK), F32)
        total = jnp.concatenate([zeros, taps[0:1] * dconv], axis=0)
        for lag in range(4):
            dtaps_ref[lag : lag + 1, :] = jnp.sum(dconv * lags[lag], axis=0, keepdims=True)
            if lag:
                part = (taps[lag : lag + 1] * dconv) * mask_ref[:, 3 + lag : 4 + lag]
                part = jnp.concatenate([zeros, part], axis=0)
                total = total + pltpu.roll(part, tokens + 8 - lag, 0)
        drim_ref[...] = total[:8]
        dx_ref[...] = total[8:].astype(BF16)
        edge_ref[...] = total[tokens - 8 :]

    @pl.when(kind < 2)
    def _():
        through(True)

    @pl.when((kind >= 2) & (kind < 4))
    def _():
        through(False)


def act_block(c):
    return lax.div(c, 6) * 4 + jnp.minimum(lax.rem(c, 6), 3)


def gate_block(c):
    return lax.div(c, 6) * 2 + jnp.maximum(lax.rem(c, 6) - 4, 0)


def front_back(raw, rim, masks, taps, dqkv, dg):
    tokens, cols = raw.shape
    block = spec((tokens, DK), lambda c: (0, c))
    return pl.pallas_call(
        front_back_kernel,
        grid=(cols // DK,),
        in_specs=[
            block,
            spec((8, DK), lambda c: (0, c)),
            spec((tokens, 8), lambda c: (0, 0)),
            spec((4, DK), lambda c: (0, act_block(c))),
            spec((tokens, DK), lambda c: (0, act_block(c))),
            spec((tokens, DK), lambda c: (0, gate_block(c))),
        ],
        out_specs=[
            block,
            spec((16, DK), lambda c: (0, c)),
            spec((8, DK), lambda c: (0, c)),
            spec((4, DK), lambda c: (0, c)),
        ],
        out_shape=[
            jax.ShapeDtypeStruct((tokens, cols), BF16),
            jax.ShapeDtypeStruct((16, cols), F32),
            jax.ShapeDtypeStruct((8, cols), F32),
            jax.ShapeDtypeStruct((4, cols), F32),
        ],
        compiler_params=params(),
        cost_estimate=cost(tokens * cols * 80, tokens * cols * 10),
        name="front_back",
    )(raw, rim, masks, taps, dqkv, dg)


def flip(value, bit):
    count = lax.axis_size("mp")
    return lax.ppermute(value, "mp", [(i, i ^ (1 << bit)) for i in range(count)])


def bit_count():
    return lax.axis_size("mp").bit_length() - 1


def exchange(values, bits):
    values = lax.optimization_barrier(tuple(values))
    return lax.optimization_barrier(tuple(flip(v, b) for v, b in zip(values, bits)))


def gather_mp(share):
    bits = bit_count()
    half = share.shape[0] // 2
    orders = (list(range(bits - 1, 0, -1)), list(range(1, bits)))
    held = [share[w * half : (w + 1) * half][None] for w in range(2)]
    rels = [[0], [0]]
    for turn in range(bits - 1):
        now = [order[turn] for order in orders]
        got = exchange(held, now)
        held = [jnp.concatenate([h, g], axis=0) for h, g in zip(held, got)]
        rels = [rel + [r | (1 << bit) for r in rel] for rel, bit in zip(rels, now)]
    got = exchange(held, [0, 0])
    return [(h, g, rel) for h, g, rel in zip(held, got, rels)]


def gathered_specs(found, tile, tiles):
    specs = []
    for which, (held, other, rel) in enumerate(found):
        shape = (held.shape[0], tile, held.shape[2])
        if which == 0:
            index = lambda i, m: (0, jnp.minimum(i, tiles - 1), 0)
        else:
            index = lambda i, m: (0, jnp.maximum(i - tiles, 0), 0)
        specs += [spec(shape, index)] * 2
    return specs


def gathered_args(found):
    return [x for held, other, rel in found for x in (held, other)]


def gathered_blocks(found, refs, which):
    held, other = refs[2 * which], refs[2 * which + 1]
    rel = found[which][2]
    blocks = [(r, held[i].astype(F32)) for i, r in enumerate(rel)]
    return blocks + [(r | 1, other[i].astype(F32)) for i, r in enumerate(rel)]


def place(mp_ref, r, cols):
    return pl.ds(pl.multiple_of((mp_ref[0] ^ r) * cols, cols), cols)


def norm_kernel(rels, cols, tiles, mode, *refs):
    mp_ref, refs = refs[0], refs[1:]
    found = [(None, None, rel) for rel in rels]
    if mode == "plain":
        out_ref = refs[4]
    else:
        gain_ref, out_ref, inv_ref = refs[4:7]
    for which in range(2):

        @pl.when((pl.program_id(0) < tiles) == (which == 0))
        def _():
            blocks = gathered_blocks(found, refs, which)
            if mode == "plain":
                for r, x in blocks:
                    out_ref[:, place(mp_ref, r, cols)] = x.astype(BF16)
                return
            total = sum(jnp.sum(x * x, axis=-1, keepdims=True) for _, x in blocks)
            inv = lax.rsqrt(total * (1.0 / (cols * len(blocks))) + 1e-05)
            for r, x in blocks:
                at = place(mp_ref, r, cols)
                out_ref[:, at] = (x * inv * gain_ref[:, at]).astype(BF16)
            inv_ref[...] = jnp.broadcast_to(inv, inv_ref.shape)


def assemble(found, mp_pos, gain=None):
    half, cols = found[0][0].shape[1:]
    rels = [f[2] for f in found]
    width = cols * 2 * len(rels[0])
    tokens = 2 * half
    tile = min(256, half)
    tiles = half // tile
    mode = "plain" if gain is None else "norm"
    row_spec = spec((tile, width), lambda i, m: (i, 0))
    in_specs = gathered_specs(found, tile, tiles)
    out_specs = [row_spec]
    out_shape = [jax.ShapeDtypeStruct((tokens, width), BF16)]
    args = gathered_args(found)
    if gain is not None:
        in_specs.append(spec((1, width), lambda i, m: (0, 0)))
        args.append(gain.reshape(1, width))
        out_specs.append(spec((tile, 128), lambda i, m: (i, 0)))
        out_shape.append(jax.ShapeDtypeStruct((tokens, 128), F32))
    return pl.pallas_call(
        functools.partial(norm_kernel, rels, cols, tiles, mode),
        grid_spec=pltpu.PrefetchScalarGridSpec(
            num_scalar_prefetch=1,
            grid=(2 * tiles,),
            in_specs=in_specs,
            out_specs=out_specs,
        ),
        out_shape=out_shape,
        compiler_params=params(),
        cost_estimate=cost(tokens * width * 10, tokens * width * 4),
        name="assemble",
    )(mp_pos.reshape(1).astype(jnp.int32), *args)


def norm_back_kernel(rels, cols, tiles, *refs):
    mp_ref, refs = refs[0], refs[1:]
    found = [(None, None, rel) for rel in rels]
    grads, mids = refs[:4], refs[4:8]
    up_ref, gain_ref, own_grad_ref, own_mid_ref, out_ref, own_out_ref, dgain_ref = refs[8:]

    @pl.when(pl.program_id(0) == 0)
    def _():
        dgain_ref[...] = jnp.zeros_like(dgain_ref)

    for which in range(2):

        @pl.when((pl.program_id(0) < tiles) == (which == 0))
        def _():
            grad = gathered_blocks(found, grads, which)
            mid = gathered_blocks(found, mids, which)
            scale = 1.0 / (cols * len(grad))
            total = sum(jnp.sum(x * x, axis=-1, keepdims=True) for _, x in mid)
            inv = lax.rsqrt(total * scale + 1e-05)
            scaled = [(r, g * gain_ref[:, place(mp_ref, r, cols)]) for r, g in grad]
            mean = sum(
                jnp.sum(g * x, axis=-1, keepdims=True) for (_, g), (_, x) in zip(scaled, mid)
            )
            shrink = inv * inv * (mean * scale)
            for (r, g), (_, x) in zip(scaled, mid):
                at = place(mp_ref, r, cols)
                out_ref[:, at] = (up_ref[:, at].astype(F32) + inv * (g - x * shrink)).astype(BF16)
            at = place(mp_ref, 0, cols)
            own_grad, own_mid = own_grad_ref[...], own_mid_ref[...]
            own_out_ref[...] = up_ref[:, at].astype(F32) + inv * (
                own_grad * gain_ref[:, at] - own_mid * shrink
            )
            dgain_ref[...] += jnp.sum(own_grad * own_mid * inv, axis=0, keepdims=True)


def norm_back(found_grad, found_mid, full_grad, gain, own_grad, own_mid, mp_pos):
    half, cols = found_grad[0][0].shape[1:]
    rels = [f[2] for f in found_grad]
    tokens, width = full_grad.shape
    tile = min(256, half)
    tiles = half // tile
    row_spec = spec((tile, width), lambda i, m: (i, 0))
    own_spec = spec((tile, cols), lambda i, m: (i, 0))
    return pl.pallas_call(
        functools.partial(norm_back_kernel, rels, cols, tiles),
        grid_spec=pltpu.PrefetchScalarGridSpec(
            num_scalar_prefetch=1,
            grid=(2 * tiles,),
            in_specs=gathered_specs(found_grad, tile, tiles)
            + gathered_specs(found_mid, tile, tiles)
            + [row_spec, spec((1, width), lambda i, m: (0, 0)), own_spec, own_spec],
            out_specs=[row_spec, own_spec, spec((1, cols), lambda i, m: (0, 0))],
        ),
        out_shape=[
            jax.ShapeDtypeStruct((tokens, width), BF16),
            jax.ShapeDtypeStruct((tokens, cols), F32),
            jax.ShapeDtypeStruct((1, cols), F32),
        ],
        compiler_params=params(),
        cost_estimate=cost(tokens * width * 20, tokens * width * 8),
        name="norm_back",
    )(
        mp_pos.reshape(1).astype(jnp.int32),
        *gathered_args(found_grad),
        *gathered_args(found_mid),
        full_grad,
        gain.reshape(1, width),
        own_grad,
        own_mid,
    )


def block_kernel(turns, mp_ref, *refs):
    out_ref = refs[2 * len(turns)]
    total = None
    for i, turned in enumerate(turns):
        part = d1(refs[2 * i][...], refs[2 * i + 1][...], NN if turned is False else NT)
        total = part if total is None else total + part
    out_ref[0] = total.astype(out_ref.dtype)


def right_index(parity, turned, g, m):
    at = (2 * g + parity) ^ m[0]
    return (at, 0) if turned else (0, at)


def spaced_index(parity, cols, rows, g, m):
    at = ((2 * g + parity) ^ m[0]) * cols
    return (pl.multiple_of(at + lax.div(at, rows) * 16, 16), 0)


def block_products(terms, mp_pos, cols, parity):
    tokens = terms[0][0].shape[0]
    count = lax.axis_size("mp") // 2
    in_specs, args, flops = [], [], 0
    for left, right, turned in terms:
        depth = left.shape[1]
        in_specs.append(spec((tokens, depth), lambda g, m: (0, 0)))
        if turned is None:
            rows = right.shape[0] // lax.axis_size("seq") - 16
            index = functools.partial(spaced_index, parity, cols, rows)
            in_specs.append(pl.BlockSpec((pl.Element(cols), pl.Element(depth)), index))
        else:
            index = functools.partial(right_index, parity, turned)
            in_specs.append(spec((cols, depth) if turned else (depth, cols), index))
        args += [left, right]
        flops += 2 * tokens * depth * cols * count
    return pl.pallas_call(
        functools.partial(block_kernel, [t[2] for t in terms]),
        grid_spec=pltpu.PrefetchScalarGridSpec(
            num_scalar_prefetch=1,
            grid=(count,),
            in_specs=in_specs,
            out_specs=spec((1, tokens, cols), lambda g, m: (g, 0, 0)),
        ),
        out_shape=jax.ShapeDtypeStruct((count, tokens, cols), BF16 if parity else F32),
        compiler_params=params(),
        cost_estimate=cost(flops, tokens * cols * count * 4),
        name="block_products",
    )(mp_pos.reshape(1).astype(jnp.int32), *args)


def reduce_mp(terms, mp_pos, cols):
    sent = flip(block_products(terms, mp_pos, cols, 1), 0)
    kept = block_products(terms, mp_pos, cols, 0)
    bits = bit_count()
    half = kept.shape[1] // 2
    orders = (list(range(1, bits)), list(range(bits - 1, 0, -1)))
    rels = [[2 * i for i in range(kept.shape[0])] for _ in orders]
    helds = []
    for which in range(2):
        at = slice(which * half, (which + 1) * half)
        helds.append({r: kept[i, at] + sent[i, at].astype(F32) for i, r in enumerate(rels[which])})
    for turn in range(bits - 1):
        aways = [[r for r in rels[w] if (r >> orders[w][turn]) & 1] for w in range(2)]
        gots = exchange(
            [jnp.stack([helds[w][r].astype(BF16) for r in aways[w]]) for w in range(2)],
            [orders[w][turn] for w in range(2)],
        )
        for w in range(2):
            bit = orders[w][turn]
            rels[w] = [r for r in rels[w] if not (r >> bit) & 1]
            helds[w] = {
                r: helds[w][r] + gots[w][aways[w].index(r | (1 << bit))].astype(F32) for r in rels[w]
            }
    return jnp.concatenate([helds[0][0], helds[1][0]], axis=0)


def sum_mp(value):
    for bit in range(bit_count()):
        value = value + flip(value, bit)
    return value


def sum_seq(value):
    count = lax.axis_size("seq")
    total = value
    for step in range(1, count):
        total = total + lax.ppermute(value, "seq", [(i, (i + step) % count) for i in range(count)])
    return total


def shifted(value, steps):
    count = lax.axis_size("seq")
    first, last = max(0, -steps), min(count, count - steps)
    return lax.ppermute(value, "seq", [(i, i + steps) for i in range(first, last)])


def batched(left, right):
    return jnp.einsum("hde,hev->hdv", left, right, precision=lax.Precision.HIGHEST)


def dot(left, right, dims=NN):
    return lax.dot_general(left, right, dims, preferred_element_type=F32)


TN = (((0,), (0,)), ((), ()))


def first_kernel(heads, count, rows, x_ref, w_ref, mask_ref, scale_ref, bias_ref, raw_ref, pre_ref, gate_ref):
    raw, pre = None, None
    for s in range(count):
        at = s * (rows + 16)
        part = x_ref[:, s * rows : (s + 1) * rows]
        left = d1(part, w_ref[at : at + rows, :])
        right = d1(part, w_ref[at + rows : at + rows + 16, :rows], NT)
        raw = left if raw is None else raw + left
        pre = right if pre is None else pre + right
    raw_ref[...] = raw
    pre_ref[...] = pre
    masks = mask_ref[...]
    lane = lax.broadcasted_iota(jnp.int32, masks.shape, 1)
    for h in range(heads):
        x = pre[:, 2 * h : 2 * h + 1] + bias_ref[h]
        soft = jnp.maximum(x, 0.0) + jnp.log1p(jnp.exp(-jnp.abs(x)))
        beta = jax.nn.sigmoid(pre[:, 2 * h + 1 : 2 * h + 2])
        gate_ref[h] = jnp.where(
            lane == 0, -scale_ref[h] * soft, jnp.where(lane == 1, beta, masks)
        )


def project_first(normed, mixer, masks, scale, bias):
    tokens, width = normed.shape
    count = lax.axis_size("seq")
    rows, cols = mixer.shape[0] // count - 16, mixer.shape[1]
    heads = scale.shape[0]
    tile = 256
    scalar = pl.BlockSpec(memory_space=pltpu.SMEM)
    return pl.pallas_call(
        functools.partial(first_kernel, heads, count, rows),
        grid=(tokens // tile,),
        in_specs=[
            spec((tile, width), lambda i: (i, 0)),
            spec(mixer.shape, lambda i: (0, 0)),
            spec((tile, 8), lambda i: (i, 0)),
            scalar,
            scalar,
        ],
        out_specs=[
            spec((tile, cols), lambda i: (i, 0)),
            spec((tile, 16), lambda i: (i, 0)),
            spec((heads, tile, 8), lambda i: (0, i, 0)),
        ],
        out_shape=[
            jax.ShapeDtypeStruct((tokens, cols), F32),
            jax.ShapeDtypeStruct((tokens, 16), F32),
            jax.ShapeDtypeStruct((heads, tokens, 8), F32),
        ],
        compiler_params=params(),
        cost_estimate=cost(2 * tokens * width * cols, tokens * width * 2 + width * cols * 2),
        name="project_first",
    )(normed, mixer, masks, scale, bias)


def gates_back_kernel(heads, pre_ref, dg_ref, scale_ref, bias_ref, low_ref, sums_ref):
    pre = pre_ref[...]
    lane = lax.broadcasted_iota(jnp.int32, pre.shape, 1)
    line = lax.broadcasted_iota(jnp.int32, (1, 128), 1)
    low = jnp.zeros(pre.shape, F32)
    for h in range(heads):
        x = pre[:, 2 * h : 2 * h + 1] + bias_ref[h]
        soft = jnp.maximum(x, 0.0) + jnp.log1p(jnp.exp(-jnp.abs(x)))
        beta = jax.nn.sigmoid(pre[:, 2 * h + 1 : 2 * h + 2])
        dlog = dg_ref[h][:, 0:1]
        dx = dlog * (-scale_ref[h] * jax.nn.sigmoid(x))
        db = dg_ref[h][:, 1:2] * (beta * (1.0 - beta))
        low = jnp.where(lane == 2 * h, dx, jnp.where(lane == 2 * h + 1, db, low))
        dscale = jnp.sum(-dlog * soft, axis=0, keepdims=True)
        dbias = jnp.sum(dx, axis=0, keepdims=True)
        sums_ref[h : h + 1, :] = jnp.where(line == 0, dscale, jnp.where(line == 1, dbias, 0.0))
    low_ref[...] = low.astype(BF16)


def gates_back(pre, dgates, scale, bias):
    tokens = pre.shape[0]
    heads = scale.shape[0]
    scalar = pl.BlockSpec(memory_space=pltpu.SMEM)
    whole = pl.BlockSpec(memory_space=pltpu.VMEM)
    return pl.pallas_call(
        functools.partial(gates_back_kernel, heads),
        in_specs=[whole, whole, scalar, scalar],
        out_specs=[whole, whole],
        out_shape=[
            jax.ShapeDtypeStruct((tokens, 16), BF16),
            jax.ShapeDtypeStruct((heads, 128), F32),
        ],
        compiler_params=params(),
        cost_estimate=cost(tokens * 1000, tokens * 1024),
        name="gates_back",
    )(pre, dgates, scale, bias)


def ffn_kernel(units, at, x_ref, dy_ref, gu_ref, down_ref, hid_ref, dgu_ref):
    x = x_ref[...]
    gate = d1(x, gu_ref[:, :units])
    up = d1(x, gu_ref[:, at : at + units])
    back = d1(dy_ref[...], down_ref[...], NT)
    sig = jax.nn.sigmoid(gate)
    silu = gate * sig
    hid_ref[...] = (silu * up).astype(BF16)
    dgu_ref[:, units:at] = jnp.zeros((x.shape[0], at - units), BF16)
    dgu_ref[:, :units] = (back * up * sig * (1.0 + gate * (1.0 - sig))).astype(BF16)
    dgu_ref[:, at : at + units] = (back * silu).astype(BF16)


def ffn(normed2, full_grad, gu_full, down_full):
    tokens, width = normed2.shape
    units = down_full.shape[0]
    both = gu_full.shape[1]
    tile = 256
    row_spec = spec((tile, width), lambda i: (i, 0))
    return pl.pallas_call(
        functools.partial(ffn_kernel, units, both - units),
        grid=(tokens // tile,),
        in_specs=[
            row_spec,
            row_spec,
            spec((width, both), lambda i: (0, 0)),
            spec((units, width), lambda i: (0, 0)),
        ],
        out_specs=[
            spec((tile, units), lambda i: (i, 0)),
            spec((tile, both), lambda i: (i, 0)),
        ],
        out_shape=[
            jax.ShapeDtypeStruct((tokens, units), BF16),
            jax.ShapeDtypeStruct((tokens, both), BF16),
        ],
        compiler_params=params(),
        cost_estimate=cost(6 * tokens * width * units, tokens * width * 4 + width * units * 6),
        name="ffn",
    )(normed2, full_grad, gu_full, down_full)


def after(value, *earlier):
    return lax.optimization_barrier((value, earlier))[0]


def ring_gather(value):
    pairs = [(shifted(value, 1), shifted(value, -1))]
    for _ in range(2, lax.axis_size("seq")):
        pairs.append((shifted(pairs[-1][0], 1), shifted(pairs[-1][1], -1)))
    return pairs


def together(*values):
    return lax.optimization_barrier(values)


def join_ring(own, pairs, axis):
    seq_count = lax.axis_size("seq")
    seq_pos = lax.axis_index("seq")
    size = own.shape[axis]
    shape = list(own.shape)
    shape[axis] = size * seq_count
    full = jnp.zeros(tuple(shape), own.dtype)
    full = lax.dynamic_update_slice_in_dim(full, own, seq_pos * size, axis)
    for j in range(1, seq_count):
        piece = jnp.where(seq_pos >= j, pairs[j - 1][0], pairs[seq_count - j - 1][1])
        at = lax.rem(seq_pos - j + seq_count, seq_count) * size
        full = lax.dynamic_update_slice_in_dim(full, piece, at, axis)
    return full


def chain(steps, ends, sign):
    total = shifted(ends.astype(BF16), sign).astype(F32)
    for _ in range(lax.axis_size("seq") - 2):
        total = shifted((batched(steps, total) + ends).astype(BF16), sign).astype(F32)
    return total


def scatter_seq(value, axis):
    return lax.psum_scatter(value, "seq", scatter_dimension=axis, tiled=True).astype(F32)


def shards(
    residual,
    attn_gain,
    w_mixer,
    w_gates,
    conv_taps,
    decay_scale,
    dt_bias,
    head_gain,
    w_out,
    ffn_gain,
    w_gate,
    w_up,
    w_down,
    out_grad,
    doc_ids,
):
    tokens, cols = residual.shape
    seq_count = lax.axis_size("seq")
    mp_count = lax.axis_size("mp")
    seq_pos = lax.axis_index("seq")
    mp_pos = lax.axis_index("mp")
    rows, heads = w_mixer.shape[:2]
    width = rows * seq_count

    padded = jnp.concatenate([jnp.full((3,), -1, jnp.int32), doc_ids])
    window = lax.dynamic_slice_in_dim(padded, seq_pos * tokens, tokens + 3)
    ids = window[3:]
    prior = jnp.repeat(window[2 : 2 + tokens].reshape(-1, CHUNK)[:, 0], CHUNK)
    same = [(window[3 - j : 3 - j + tokens] == ids).astype(F32) for j in range(1, 4)]
    ids_f, prior_f = ids.astype(F32), prior.astype(F32)
    zero = jnp.zeros((tokens,), F32)
    masks = jnp.stack([zero] * 2 + [ids_f, prior_f] + same + [zero], axis=1)

    units = w_gate.shape[1]
    spare = -units % 128
    mix_cols = heads * (2 * DK + 2 * DV)
    gate_part = jnp.pad(
        w_gates.reshape(rows, 2 * heads).T, ((0, 16 - 2 * heads), (0, mix_cols - rows))
    )
    mixer_part = jnp.concatenate([w_mixer.reshape(rows, mix_cols), gate_part])
    do_part = jnp.concatenate([w_out, w_down])
    gu_part = jnp.concatenate([w_gate, jnp.zeros((rows, spare), BF16), w_up], axis=1)
    mixer_full = lax.all_gather(mixer_part, "seq", axis=0, tiled=True)
    found_res = gather_mp(residual)
    do_full = lax.all_gather(after(do_part, found_res[0][0]), "seq", axis=1, tiled=True)

    normed, inv1 = assemble(found_res, mp_pos, attn_gain)
    gu_full = lax.all_gather(after(gu_part, normed), "seq", axis=0, tiled=True)
    found_og = gather_mp(after(out_grad, normed))
    full_grad = assemble(found_og, mp_pos)[0]
    mixer_full = after(mixer_full, full_grad)
    raw, gate_pre, gates = project_first(normed, mixer_full, masks, decay_scale, dt_bias)
    taps = conv_taps.reshape(4, heads * 2 * DV)
    rim = shifted(raw[tokens - 8 :], 1)
    qkv = front(raw, rim, masks, taps)

    inverse, inv_turned, scores, scores_turned, kept, wkeys, reach, reach_turned, steps, steps_turned = (
        delta_prep(qkv, gates)
    )
    trans, back = delta_trans(steps, steps_turned)
    pseudo, local_out, states, state_end = delta_values(qkv, gates, inverse, scores, steps)
    start = chain(trans[:, -1], state_end, 1)
    mixed, outs, held, corrected = delta_output(
        start, states, trans, reach, wkeys, pseudo, local_out, raw, head_gain
    )

    out_full, down_full = do_full[: w_out.shape[0]], do_full[w_out.shape[0] :]
    branch = reduce_mp([(mixed, out_full, False)], mp_pos, cols)
    middle = residual.astype(F32) + branch
    found_mid = gather_mp(middle.astype(BF16))
    normed2, _ = assemble(found_mid, mp_pos, ffn_gain)
    hidden, grad_gu = ffn(normed2, full_grad, gu_full, down_full)
    part_gu = dot(normed2, grad_gu, TN).astype(BF16)
    grad_normed2 = reduce_mp([(grad_gu, gu_full, True)], mp_pos, cols)
    dw_gu = lax.psum_scatter(part_gu, "seq", scatter_dimension=0, tiled=True)
    part_down = dot(hidden, full_grad, TN).astype(BF16)
    grad_normed2 = after(grad_normed2, part_gu)
    found_gn2 = gather_mp(grad_normed2.astype(BF16))

    grad_branch, grad_middle, dffn_gain = norm_back(
        found_gn2, found_mid, full_grad, ffn_gain, grad_normed2, middle, mp_pos
    )
    grad_mixed = dot(grad_branch, out_full, NT)
    part_out = dot(mixed, grad_branch, TN).astype(BF16)
    dw_do = lax.psum_scatter(
        jnp.concatenate([part_out, part_down]), "seq", scatter_dimension=1, tiled=True
    )
    ffn_part = reduce_mp([(after(hidden, grad_branch), down_full, False)], mp_pos, cols)
    output = (middle + ffn_part).astype(BF16)

    dout, dg_raw, dhead_gain, dstates, dstart = delta_tail(
        grad_mixed, outs, raw, head_gain, reach_turned, steps_turned
    )
    grad_end = chain(back[:, 0], dstart, -1)
    grad_end = after(grad_end, output, part_out)
    dqkv, dgates = delta_grads(
        grad_end, qkv, gates, inv_turned, scores, scores_turned, kept, corrected, held,
        dstates, back[:, 1:], dout,
    )
    dproj, edge, drim, dtaps = front_back(raw, rim, masks, taps, dqkv, dg_raw)
    edge = jnp.concatenate([edge[:8], edge[8:] + shifted(drim, -1)])
    dproj = lax.dynamic_update_slice_in_dim(dproj, edge.astype(BF16), tokens - 16, 0)
    dgate_low, gate_sums = gates_back(gate_pre, dgates, decay_scale, dt_bias)

    part_mixer = dot(normed, dproj, TN).astype(BF16)
    dw_mixer = lax.psum_scatter(part_mixer, "seq", scatter_dimension=0, tiled=True)
    part_gates = dot(dgate_low, normed, TN)
    gates_full = jnp.swapaxes(
        mixer_full.reshape(seq_count, rows + 16, mix_cols)[:, rows:, :rows], 0, 1
    ).reshape(16, width)
    grad_normed = reduce_mp(
        [(dproj, mixer_full, None), (dgate_low, gates_full, False)], mp_pos, cols
    )
    own_gain = lax.dynamic_slice_in_dim(attn_gain, mp_pos * cols, cols)
    own_res = residual.astype(F32)
    inv1 = inv1[:, :1]
    scaled = grad_normed * own_gain
    mean = jnp.sum(scaled * own_res, axis=-1).reshape(-1, 128)
    mean = sum_mp(mean).reshape(tokens, 1) * (1.0 / width)
    grad_residual = grad_middle + inv1 * (scaled - own_res * (inv1 * inv1 * mean))
    dattn_gain = jnp.sum(grad_normed * own_res * inv1, axis=0)

    dtaps = dtaps.reshape(4, heads, 2 * DK + 2 * DV)[:, :, : 2 * DK + DV]
    small = [
        dattn_gain, dffn_gain, dhead_gain, gate_sums[:, 0], gate_sums[:, 1], dtaps,
        part_gates[: 2 * heads],
    ]
    packed = jnp.concatenate([value.reshape(-1) for value in small])
    packed = jnp.pad(packed, (0, -packed.shape[0] % 1024)).reshape(-1, 128)
    packed = sum_seq(packed).reshape(-1)
    sums, at = [], 0
    for value in small:
        sums.append(packed[at : at + value.size].reshape(value.shape))
        at += value.size
    gains = jnp.stack([sums[0], sums[1].reshape(-1)])
    gains = lax.dynamic_update_slice(jnp.zeros((2, width), F32), gains, (0, mp_pos * cols))
    gains = sum_mp(gains)
    dw_gates = lax.dynamic_slice_in_dim(sums[6], seq_pos * rows, rows, 1)
    return (
        output,
        grad_residual,
        gains[0],
        dw_mixer.astype(F32).reshape(rows, heads, 2 * DK + 2 * DV),
        dw_gates.T.reshape(rows, heads, 2),
        sums[5],
        sums[3],
        sums[4],
        sums[2],
        dw_do[: w_out.shape[0]].astype(F32),
        gains[1],
        dw_gu[:, :units].astype(F32),
        dw_gu[:, units + spare :].astype(F32),
        dw_do[w_out.shape[0] :].astype(F32),
    )


def solution(mesh):
    in_specs = (
        P("seq", "mp"),
        P(),
        P("seq", "mp", None),
        P("seq", "mp", None),
        P(None, "mp", None),
        P("mp"),
        P("mp"),
        P("mp", None),
        P("mp", "seq"),
        P(),
        P("seq", "mp"),
        P("seq", "mp"),
        P("mp", "seq"),
        P("seq", "mp"),
        P(),
    )
    out_specs = (
        P("seq", "mp"),
        P("seq", "mp"),
        P(),
        P("seq", "mp", None),
        P("seq", "mp", None),
        P(None, "mp", None),
        P("mp"),
        P("mp"),
        P("mp", None),
        P("mp", "seq"),
        P(),
        P("seq", "mp"),
        P("seq", "mp"),
        P("mp", "seq"),
    )
    return jax.shard_map(shards, mesh=mesh, in_specs=in_specs, out_specs=out_specs, check_vma=False)
```

```python
import functools
import jax
import jax.numpy as jnp
from jax import lax
from jax.experimental import pallas as pl
from jax.experimental.pallas import tpu as pltpu
from jax.sharding import PartitionSpec as P

DK = 128
DV = 256
CHUNK = 128
GATE_LANES = 8
F32 = jnp.float32
BF16 = jnp.bfloat16
NN = (((1,), (0,)), ((), ()))
NT = (((1,), (1,)), ((), ()))
VMEM_LIMIT = 48 * 1024 * 1024


def d1(left, right, dims=NN):
    return lax.dot_general(
        left.astype(BF16), right.astype(BF16), dims, preferred_element_type=F32
    )


def dx(left, right, dims=NN):
    if left.dtype == BF16 and right.dtype == BF16:
        return d1(left, right, dims)
    return d3(left.astype(F32), right.astype(F32), dims)


def split(value):
    high = value.astype(BF16)
    return high, (value - high.astype(F32)).astype(BF16)


def d3(left, right, dims=NN):
    lh, ll = split(left)
    rh, rl = split(right)
    return d1(lh, rh, dims) + (d1(lh, rl, dims) + d1(ll, rh, dims))


def params():
    return pltpu.CompilerParams(vmem_limit_bytes=VMEM_LIMIT)


def cost(flops, nbytes):
    return pl.CostEstimate(flops=int(flops) // 100, bytes_accessed=int(nbytes) // 100, transcendentals=0)


def spec(shape, index_map):
    return pl.BlockSpec(shape, index_map)


def rows_cols():
    row = lax.broadcasted_iota(jnp.int32, (CHUNK, CHUNK), 0)
    col = lax.broadcasted_iota(jnp.int32, (CHUNK, CHUNK), 1)
    return row, col


def to_row(column, row, col):
    return jnp.sum(jnp.where(row == col, column, 0.0), axis=0, keepdims=True)


def to_col(line, row, col):
    return jnp.sum(jnp.where(row == col, line, 0.0), axis=1, keepdims=True)


def decay_parts(gates, row, col):
    log_decay, beta, ids, prior = (gates[:, i : i + 1] for i in range(4))
    cum_row = jnp.sum(jnp.where(row <= col, log_decay, 0.0), axis=0, keepdims=True)
    cum_col = to_col(cum_row, row, col)
    same = ids == to_row(ids, row, col)
    inside = (row >= col) & same
    decays = jnp.where(inside, jnp.exp(jnp.where(inside, cum_col - cum_row, 0.0)), 0.0)
    carried = jnp.where(ids == prior, jnp.exp(cum_col), 0.0)
    last_ids = ids[CHUNK - 1 : CHUNK]
    last_cum = cum_col[CHUNK - 1 : CHUNK]
    to_end = jnp.where(ids == last_ids, jnp.exp(last_cum - cum_col), 0.0)
    return beta, decays, carried, to_end


def invert(lowers, row, col):
    eye = jnp.where(row == col, 1.0, 0.0)
    found = None
    shift = 0
    while (1 << shift) < CHUNK:
        mask = ((row >> (shift + 1)) == (col >> (shift + 1))) & (
            (row >> shift) > (col >> shift)
        )
        masked = [jnp.where(mask, lower, 0.0) for lower in lowers]
        if found is None:
            found = [eye - m for m in masked]
        else:
            low = [x.astype(BF16) for x in found]
            inner = [d1(m, x) for m, x in zip(masked, low)]
            outer = [d1(x, y) for x, y in zip(low, inner)]
            found = [x - y for x, y in zip(found, outer)]
        shift += 1
    rest = [d3(lower, x) for lower, x in zip(lowers, found)]
    rest = [(eye - x) - r for x, r in zip(found, rest)]
    return [x + d1(x, r) for x, r in zip(found, rest)]


def prep_kernel(
    group, qk_ref, gt_ref, t_ref, tt_ref, a_ref, at_ref, lk_ref, w_ref, p_ref, pt_ref, m_ref, mt_ref
):
    row, col = rows_cols()
    queries, keys, parts = [], [], []
    for c in range(group):
        block = qk_ref[c * CHUNK : (c + 1) * CHUNK, :]
        queries.append(block[:, :DK])
        keys.append(block[:, DK:])
        parts.append(decay_parts(gt_ref[0, c * CHUNK : (c + 1) * CHUNK, :], row, col))
    gram = [d3(k, k, NT) for k in keys]
    scores = [dx(q, k, NT) for q, k in zip(queries, keys)]
    kept = [jnp.where(row > col, p[1] * g, 0.0) for p, g in zip(parts, gram)]
    lowers = [x * p[0] for x, p in zip(kept, parts)]
    inverses = invert(lowers, row, col)
    eye = jnp.where(row == col, 1.0, 0.0)
    for c in range(group):
        beta, decays, carried, to_end = parts[c]
        inverse = inverses[c]
        t_ref[0, c] = inverse
        tt_ref[0, c] = inverses[c].T
        score = decays * scores[c]
        a_ref[0, c] = score
        at_ref[0, c] = score.T
        lk_ref[0, c] = kept[c]
        wkeys = dx(inverse, (beta * carried) * keys[c])
        w_ref[0, c] = wkeys
        reach = carried * queries[c] - dx(score, wkeys)
        p_ref[0, c] = reach
        pt_ref[0, c] = reach.T
        end_keys = to_end * keys[c]
        step = carried[CHUNK - 1 : CHUNK] * eye - dx(end_keys.T, wkeys)
        m_ref[0, c] = step
        mt_ref[0, c] = step.T


def delta_prep(qk, gates):
    heads, tokens, _ = gates.shape
    count = tokens // CHUNK
    group = min(4, count)
    rows = group * CHUNK
    low = jax.ShapeDtypeStruct((heads, count, CHUNK, CHUNK), F32)
    wide = jax.ShapeDtypeStruct((heads, count, DK, DK), F32)
    out_spec = spec((1, group, CHUNK, CHUNK), lambda h, g: (h, g, 0, 0))
    return pl.pallas_call(
        functools.partial(prep_kernel, group),
        grid=(heads, count // group),
        in_specs=[
            spec((rows, 2 * DK), lambda h, g: (g, 2 * h)),
            spec((1, rows, GATE_LANES), lambda h, g: (h, g, 0)),
        ],
        out_specs=[out_spec] * 10,
        out_shape=[low] * 8 + [wide] * 2,
        compiler_params=params(),
        cost_estimate=cost(heads * count * 40 * 2 * CHUNK**3 * 8, heads * count * CHUNK * CHUNK * 24),
        name="delta_prep",
    )(qk, gates)


def trans_kernel(heads, count, m_ref, mt_ref, fwd_ref, back_ref):
    row, col = rows_cols()
    eye = jnp.where(row == col, 1.0, 0.0)
    fwd = [eye] * heads
    back = [eye] * heads
    for h in range(heads):
        fwd_ref[h, 0] = eye
        back_ref[h, count] = eye
    for c in range(count):
        if c == 0:
            fwd = [m_ref[h, 0] for h in range(heads)]
            back = [mt_ref[h, count - 1] for h in range(heads)]
        else:
            fwd = [d3(m_ref[h, c], fwd[h]) for h in range(heads)]
            back = [d3(mt_ref[h, count - 1 - c], back[h]) for h in range(heads)]
        for h in range(heads):
            fwd_ref[h, c + 1] = fwd[h]
            back_ref[h, count - 1 - c] = back[h]


def delta_trans(steps, steps_turned):
    heads, count = steps.shape[:2]
    shape = jax.ShapeDtypeStruct((heads, count + 1, DK, DK), F32)
    return pl.pallas_call(
        functools.partial(trans_kernel, heads, count),
        out_shape=[shape, shape],
        compiler_params=params(),
        cost_estimate=cost(heads * count * 6 * 2 * DK**3 * 8, heads * count * DK * DK * 16),
        name="delta_trans",
    )(steps, steps_turned)


def values_kernel(
    heads, group, qkv_ref, gt_ref, t_ref, a_ref, m_ref, ut_ref, o_ref, s_ref, end_ref, state
):
    @pl.when(pl.program_id(0) == 0)
    def _():
        state[...] = jnp.zeros_like(state)

    row, col = rows_cols()
    pairs = [(h, c) for c in range(group) for h in range(heads)]
    offsets = {}
    for h, c in pairs:
        at = slice(c * CHUNK, (c + 1) * CHUNK)
        beta, _, _, to_end = decay_parts(gt_ref[h, at, :], row, col)
        pseudo = dx(t_ref[h, c], beta * qkv_ref[at, (2 * h + 1) * DV : (2 * h + 2) * DV])
        ut_ref[h, c] = pseudo
        o_ref[at, h * DV : (h + 1) * DV] = dx(a_ref[h, c], pseudo)
        end_keys = to_end * qkv_ref[at, (4 * h + 1) * DK : (4 * h + 2) * DK]
        offsets[h, c] = dx(end_keys.T, pseudo)
    held = [state[h] for h in range(heads)]
    for c in range(group):
        for h in range(heads):
            s_ref[h, c] = held[h]
        held = [d3(m_ref[h, c], held[h]) + offsets[h, c] for h in range(heads)]
    for h in range(heads):
        state[h] = held[h]
        end_ref[h] = held[h]


def delta_values(qkv, gates, inverse, scores, steps):
    heads, tokens, _ = gates.shape
    count = tokens // CHUNK
    group = min(4, count)
    rows = group * CHUNK
    square = spec((heads, group, CHUNK, CHUNK), lambda g: (0, g, 0, 0))
    tall = spec((heads, group, CHUNK, DV), lambda g: (0, g, 0, 0))
    return pl.pallas_call(
        functools.partial(values_kernel, heads, group),
        grid=(count // group,),
        in_specs=[
            spec((rows, heads * 2 * DV), lambda g: (g, 0)),
            spec((heads, rows, GATE_LANES), lambda g: (0, g, 0)),
            square,
            square,
            square,
        ],
        out_specs=[
            tall,
            spec((rows, heads * DV), lambda g: (g, 0)),
            tall,
            spec((heads, DK, DV), lambda g: (0, 0, 0)),
        ],
        out_shape=[
            jax.ShapeDtypeStruct((heads, count, CHUNK, DV), F32),
            jax.ShapeDtypeStruct((tokens, heads * DV), F32),
            jax.ShapeDtypeStruct((heads, count, DK, DV), F32),
            jax.ShapeDtypeStruct((heads, DK, DV), F32),
        ],
        scratch_shapes=[pltpu.VMEM((heads, DK, DV), F32)],
        compiler_params=params(),
        cost_estimate=cost(heads * count * 12 * 2 * CHUNK**3 * 8, heads * count * CHUNK * 4000),
        name="delta_values",
    )(qkv, gates, inverse, scores, steps)


def output_kernel(
    heads, group, start_ref, s0_ref, tc_ref, p_ref, w_ref, ut_ref, o0_ref, gain_ref, *refs
):
    g_refs, (mixed_ref, o_ref, s_ref, u_ref) = refs[:heads], refs[heads:]
    for c in range(group):
        for h in range(heads):
            at = slice(c * CHUNK, (c + 1) * CHUNK)
            cols = slice(h * DV, (h + 1) * DV)
            held = s0_ref[h, c] + d3(tc_ref[h, c], start_ref[h])
            low = held
            s_ref[h, c] = low
            u_ref[h, c] = (ut_ref[h, c].astype(F32) - dx(w_ref[h, c], low))
            out = o0_ref[at, cols] + dx(p_ref[h, c], low)
            o_ref[at, cols] = out
            gate = g_refs[h][at, :]
            inv = lax.rsqrt(jnp.mean(out * out, axis=-1, keepdims=True) + 1e-05)
            mixed = out * inv * gain_ref[h : h + 1, :] * (gate * jax.nn.sigmoid(gate))
            mixed_ref[at, cols] = mixed.astype(BF16)


def gate_specs(heads, rows, place):
    return [
        spec((rows, DV), functools.partial(lambda h, g: (place(g), 3 * h + 2), h))
        for h in range(heads)
    ]


def delta_output(start, states, trans, reach, wkeys, pseudo, local_out, raw, gain):
    heads, count = states.shape[:2]
    tokens = count * CHUNK
    group = min(2, count)
    rows = group * CHUNK
    square = spec((heads, group, CHUNK, CHUNK), lambda g: (0, g, 0, 0))
    tall = spec((heads, group, CHUNK, DV), lambda g: (0, g, 0, 0))
    flat = spec((rows, heads * DV), lambda g: (g, 0))
    low = jax.ShapeDtypeStruct((heads, count, CHUNK, DV), F32)
    return pl.pallas_call(
        functools.partial(output_kernel, heads, group),
        grid=(count // group,),
        in_specs=[
            spec((heads, DK, DV), lambda g: (0, 0, 0)),
            tall,
            square,
            square,
            square,
            tall,
            flat,
            spec((heads, DV), lambda g: (0, 0)),
        ]
        + gate_specs(heads, rows, lambda g: g),
        out_specs=[flat, flat, tall, tall],
        out_shape=[
            jax.ShapeDtypeStruct((tokens, heads * DV), BF16),
            jax.ShapeDtypeStruct((tokens, heads * DV), F32),
            low,
            low,
        ],
        compiler_params=params(),
        cost_estimate=cost(heads * count * 10 * 2 * CHUNK**3 * 8, heads * count * CHUNK * 6000),
        name="delta_output",
    )(start, states, trans, reach, wkeys, pseudo, local_out, gain, *([raw] * heads))


def tail_kernel(
    heads, group, dm_ref, o_ref, gain_ref, pt_ref, mt_ref, *refs
):
    g_refs = refs[:heads]
    do_ref, dg_ref, dgain_ref, ds_ref, dstart_ref, state = refs[heads:]

    @pl.when(pl.program_id(0) == 0)
    def _():
        state[...] = jnp.zeros_like(state)
        dgain_ref[...] = jnp.zeros_like(dgain_ref)

    pushed = {}
    for c in range(group):
        for h in range(heads):
            at = slice(c * CHUNK, (c + 1) * CHUNK)
            cols = slice(h * DV, (h + 1) * DV)
            out = o_ref[at, cols]
            gate = g_refs[h][at, :]
            back = dm_ref[at, cols]
            gain = gain_ref[h : h + 1, :]
            sig = jax.nn.sigmoid(gate)
            silu = gate * sig
            inv = lax.rsqrt(jnp.mean(out * out, axis=-1, keepdims=True) + 1e-05)
            hat = out * inv
            dgain_ref[h : h + 1, :] += jnp.sum(back * hat * silu, axis=0, keepdims=True)
            scaled = back * gain
            dg_ref[at, cols] = (scaled * hat * (sig * (1.0 + gate * (1.0 - sig)))).astype(BF16)
            dhat = scaled * silu
            dout = inv * (dhat - hat * jnp.mean(dhat * hat, axis=-1, keepdims=True))
            low = dout
            do_ref[at, cols] = low
            pushed[h, c] = dx(pt_ref[h, c], low)
    held = [state[h] for h in range(heads)]
    for c in reversed(range(group)):
        for h in range(heads):
            ds_ref[h, c] = held[h]
        held = [d3(mt_ref[h, c], held[h]) + pushed[h, c] for h in range(heads)]
    for h in range(heads):
        state[h] = held[h]
        dstart_ref[h] = held[h]


def delta_tail(grad_mixed, outs, raw, gain, reach_turned, steps_turned):
    heads, count = steps_turned.shape[:2]
    tokens = count * CHUNK
    group = min(2, count)
    rows = group * CHUNK
    last = count // group - 1
    square = spec((heads, group, CHUNK, CHUNK), lambda g: (0, last - g, 0, 0))
    tall = spec((heads, group, CHUNK, DV), lambda g: (0, last - g, 0, 0))
    flat = spec((rows, heads * DV), lambda g: (last - g, 0))
    return pl.pallas_call(
        functools.partial(tail_kernel, heads, group),
        grid=(count // group,),
        in_specs=[flat, flat, spec((heads, DV), lambda g: (0, 0)), square, square]
        + gate_specs(heads, rows, lambda g: last - g),
        out_specs=[
            flat,
            flat,
            spec((heads, DV), lambda g: (0, 0)),
            tall,
            spec((heads, DK, DV), lambda g: (0, 0, 0)),
        ],
        out_shape=[
            jax.ShapeDtypeStruct((tokens, heads * DV), F32),
            jax.ShapeDtypeStruct((tokens, heads * DV), BF16),
            jax.ShapeDtypeStruct((heads, DV), F32),
            jax.ShapeDtypeStruct((heads, count, DK, DV), F32),
            jax.ShapeDtypeStruct((heads, DK, DV), F32),
        ],
        scratch_shapes=[pltpu.VMEM((heads, DK, DV), F32)],
        compiler_params=params(),
        cost_estimate=cost(heads * count * 10 * 2 * CHUNK**3 * 8, heads * count * CHUNK * 6000),
        name="delta_tail",
    )(grad_mixed, outs, gain, reach_turned, steps_turned, *([raw] * heads))


def early_kernel(heads, group, at_ref, u_ref, s_ref, do_ref, da_ref, dqd_ref, dua_ref):
    pairs = [(h, c) for c in range(group) for h in range(heads)]
    douts = {
        (h, c): do_ref[c * CHUNK : (c + 1) * CHUNK, h * DV : (h + 1) * DV] for h, c in pairs
    }
    for h, c in pairs:
        da_ref[h, c] = dx(douts[h, c], u_ref[h, c], NT)
    for h, c in pairs:
        dqd_ref[h, c] = dx(douts[h, c], s_ref[h, c], NT)
    for h, c in pairs:
        dua_ref[h, c] = dx(at_ref[h, c], douts[h, c])


def delta_early(scores_turned, u, s, dout):
    heads, count = u.shape[:2]
    group = min(2, count)
    square = spec((heads, group, CHUNK, CHUNK), lambda g: (0, g, 0, 0))
    tall = spec((heads, group, CHUNK, DV), lambda g: (0, g, 0, 0))
    return pl.pallas_call(
        functools.partial(early_kernel, heads, group),
        grid=(count // group,),
        in_specs=[square, tall, tall, spec((group * CHUNK, heads * DV), lambda g: (g, 0))],
        out_specs=[square, square, tall],
        out_shape=[
            jax.ShapeDtypeStruct((heads, count, CHUNK, CHUNK), F32),
            jax.ShapeDtypeStruct((heads, count, CHUNK, DK), F32),
            jax.ShapeDtypeStruct((heads, count, CHUNK, DV), F32),
        ],
        compiler_params=params(),
        cost_estimate=cost(heads * count * 30 * 2 * CHUNK**3, heads * count * CHUNK * 4000),
        name="delta_early",
    )(scores_turned, u, s, dout)


def grads_kernel(
    heads, group, end_ref, qkv_ref, gt_ref, tt_ref, a_ref, lk_ref, u_ref, s_ref,
    ds_ref, back_ref, da_ref, dqd_ref, dua_ref, dqkv_ref, dgt_ref,
):
    row, col = rows_cols()
    lane = lax.broadcasted_iota(jnp.int32, (CHUNK, GATE_LANES), 1)
    pairs = [(h, c) for c in range(group) for h in range(heads)]
    at = {(h, c): slice(c * CHUNK, (c + 1) * CHUNK) for h, c in pairs}
    parts = {(h, c): decay_parts(gt_ref[h, at[h, c], :], row, col) for h, c in pairs}
    keys = {(h, c): qkv_ref[at[h, c], (4 * h + 1) * DK : (4 * h + 2) * DK] for h, c in pairs}
    queries = {(h, c): qkv_ref[at[h, c], 4 * h * DK : (4 * h + 1) * DK] for h, c in pairs}
    vals = {(h, c): qkv_ref[at[h, c], (2 * h + 1) * DV : (2 * h + 2) * DV] for h, c in pairs}
    after = {(h, c): ds_ref[h, c] + d3(back_ref[h, c], end_ref[h]) for h, c in pairs}
    du = {
        (h, c): dua_ref[h, c] + dx(parts[h, c][3] * keys[h, c], after[h, c]) for h, c in pairs
    }
    x = {(h, c): dx(tt_ref[h, c], du[h, c]) for h, c in pairs}
    y = {(h, c): -dx(x[h, c], s_ref[h, c], NT) for h, c in pairs}
    da = {(h, c): da_ref[h, c] for h, c in pairs}
    dqd = {(h, c): dqd_ref[h, c] for h, c in pairs}
    dke = {(h, c): dx(u_ref[h, c], after[h, c], NT) for h, c in pairs}
    dl = {(h, c): dx(x[h, c], u_ref[h, c], NT) for h, c in pairs}
    for h, c in pairs:
        p = (h, c)
        beta, decays, carried, to_end = parts[p]
        key, query = keys[p], queries[p]
        kept = lk_ref[h, c].astype(F32)
        low_grad = jnp.where(row > col, -dl[p], 0.0)
        dg = jnp.sum(s_ref[h, c].astype(F32) * after[p], axis=0, keepdims=True)
        dg = jnp.sum(dg, axis=1, keepdims=True)
        yk = jnp.sum(y[p] * key, axis=-1, keepdims=True)
        dbeta = jnp.sum(x[p] * vals[p], axis=-1, keepdims=True) + carried * yk
        dbeta = dbeta + jnp.sum(low_grad * kept, axis=-1, keepdims=True)
        dcarried = beta * yk + jnp.sum(dqd[p] * query, axis=-1, keepdims=True)
        dend = jnp.sum(dke[p] * key, axis=-1, keepdims=True) * to_end
        scaled = low_grad * beta
        gram = scaled * decays
        score = da[p] * decays
        dqkv_ref[at[p], (2 * h + 1) * DV : (2 * h + 2) * DV] = beta * x[p]
        dqkv_ref[at[p], 4 * h * DK : (4 * h + 1) * DK] = carried * dqd[p] + dx(score, key)
        dqkv_ref[at[p], (4 * h + 1) * DK : (4 * h + 2) * DK] = (
            (beta * carried) * y[p]
            + to_end * dke[p]
            + dx(gram + gram.T, key)
            + dx(score.T, query)
        )
        spread = scaled * kept + da[p] * a_ref[h, c].astype(F32)
        dcum = jnp.sum(spread, axis=-1, keepdims=True)
        dcum = dcum - to_col(jnp.sum(spread, axis=0, keepdims=True), row, col)
        dcum = dcum - dend + dcarried * carried
        tail = jnp.sum(dend, axis=0, keepdims=True) + dg * carried[CHUNK - 1 : CHUNK]
        line = jnp.sum(jnp.where(row >= col, dcum, 0.0), axis=0, keepdims=True) + tail
        dlog = to_col(line, row, col)
        dgt_ref[h, at[p], :] = jnp.where(lane == 0, dlog, jnp.where(lane == 1, dbeta, 0.0))


def delta_grads(grad_end, qkv, gates, inv_turned, scores, kept, u, s, ds, back, early):
    heads, tokens, _ = gates.shape
    count = tokens // CHUNK
    group = min(2, count)
    rows = group * CHUNK
    square = spec((heads, group, CHUNK, CHUNK), lambda g: (0, g, 0, 0))
    tall = spec((heads, group, CHUNK, DV), lambda g: (0, g, 0, 0))
    gate_spec = spec((heads, rows, GATE_LANES), lambda g: (0, g, 0))
    wide = spec((rows, heads * 2 * DV), lambda g: (g, 0))
    return pl.pallas_call(
        functools.partial(grads_kernel, heads, group),
        grid=(count // group,),
        in_specs=[
            spec((heads, DK, DV), lambda g: (0, 0, 0)),
            wide,
            gate_spec,
            square,
            square,
            square,
            tall,
            tall,
            tall,
            square,
            square,
            square,
            tall,
        ],
        out_specs=[wide, gate_spec],
        out_shape=[
            jax.ShapeDtypeStruct((tokens, heads * 2 * DV), F32),
            jax.ShapeDtypeStruct((heads, tokens, GATE_LANES), F32),
        ],
        compiler_params=params(),
        cost_estimate=cost(heads * count * 30 * 2 * CHUNK**3 * 8, heads * count * CHUNK * 12000),
        name="delta_grads",
    )(grad_end, qkv, gates, inv_turned, scores, kept, u, s, ds, back, *early)


def front_act(x, rim, mask_ref, taps):
    extended = jnp.concatenate([rim, x], axis=0)
    conv = taps[0:1] * x
    for lag in range(1, 4):
        moved = pltpu.roll(extended, lag, 0)[8:]
        conv = conv + taps[lag : lag + 1] * (moved * mask_ref[:, 3 + lag : 4 + lag])
    return conv


def front_kernel(x_ref, rim_ref, mask_ref, taps_ref, y_ref, conv_ref):
    conv = front_act(x_ref[...], rim_ref[8:, :], mask_ref, taps_ref[...])
    conv_ref[...] = conv
    act = conv * jax.nn.sigmoid(conv)
    kind = pl.program_id(0) & 3

    @pl.when(kind < 2)
    def _():
        inv = lax.rsqrt(jnp.sum(act * act, axis=-1, keepdims=True) + 1e-06)
        y_ref[...] = act * (inv * jnp.where(kind == 0, DK**-0.5, 1.0))

    @pl.when(kind >= 2)
    def _():
        y_ref[...] = act


def raw_block(c):
    return (c >> 2) * 6 + (c & 3)


def front(raw, rim, masks, taps):
    tokens, cols = raw.shape[0], taps.shape[1]
    block = spec((tokens, DK), lambda c: (0, c))
    return pl.pallas_call(
        front_kernel,
        grid=(cols // DK,),
        in_specs=[
            spec((tokens, DK), lambda c: (0, raw_block(c))),
            spec((16, DK), lambda c: (0, raw_block(c))),
            spec((tokens, 8), lambda c: (0, 0)),
            spec((4, DK), lambda c: (0, c)),
        ],
        out_specs=[block, block],
        out_shape=[jax.ShapeDtypeStruct((tokens, cols), F32)] * 2,
        compiler_params=params(),
        cost_estimate=cost(tokens * cols * 40, tokens * cols * 8),
        name="front",
    )(raw, rim, masks, taps)


def conv_back(kind, conv, back):
    sig = jax.nn.sigmoid(conv)
    if kind < 2:
        act = conv * sig
        inv = lax.rsqrt(jnp.sum(act * act, axis=-1, keepdims=True) + 1e-06)
        unit = act * inv
        back = back * (DK**-0.5 if kind == 0 else 1.0)
        back = inv * (back - unit * jnp.sum(back * unit, axis=-1, keepdims=True))
    return back * (sig * (1.0 + conv * (1.0 - sig)))


def front_back_kernel(
    x_ref, rim_ref, conv_ref, mask_ref, taps_ref, dy_ref, dg_ref, dx_ref, edge_ref, dtaps_ref
):
    tokens = x_ref.shape[0]
    kind = lax.rem(pl.program_id(0), 6)

    @pl.when(kind >= 4)
    def _():
        grad = dg_ref[...]
        dx_ref[...] = grad
        edge_ref[...] = grad[tokens - 16 :].astype(F32)
        dtaps_ref[...] = jnp.zeros((4, DK), F32)

    def through(which):
        taps = taps_ref[...]
        x = x_ref[...]
        dconv = conv_back(which, conv_ref[...], dy_ref[...])
        extended = jnp.concatenate([rim_ref[8:, :], x], axis=0)
        zeros = jnp.zeros((8, DK), F32)
        total = taps[0:1] * dconv
        dtaps_ref[0:1, :] = jnp.sum(dconv * x, axis=0, keepdims=True)
        for lag in range(1, 4):
            part = jnp.concatenate([zeros, dconv * mask_ref[:, 3 + lag : 4 + lag]], axis=0)
            part = pltpu.roll(part, tokens + 8 - lag, 0)
            dtaps_ref[lag : lag + 1, :] = jnp.sum(part * extended, axis=0, keepdims=True)
            total = total + taps[lag : lag + 1] * part[8:]
        dx_ref[...] = total.astype(BF16)
        edge_ref[...] = total[tokens - 16 :]

    for which in range(3):

        @pl.when((kind == which) | ((which == 2) & (kind == 3)))
        def _():
            through(which)


def rim_back_kernel(heads, conv_ref, mask_ref, taps_ref, dy_ref, drim_ref):
    drim_ref[...] = jnp.zeros_like(drim_ref)
    zeros = jnp.zeros((8, DK), F32)
    for h in range(heads):
        for kind in range(4):
            at = slice((4 * h + kind) * DK, (4 * h + kind + 1) * DK)
            taps = taps_ref[:, at]
            dconv = conv_back(kind, conv_ref[:, at], dy_ref[:, at])
            total = zeros
            for lag in range(1, 4):
                part = jnp.concatenate([zeros, dconv * mask_ref[:, 3 + lag : 4 + lag]], axis=0)
                total = total + taps[lag : lag + 1] * pltpu.roll(part, 16 - lag, 0)[:8]
            drim_ref[:, (6 * h + kind) * DK : (6 * h + kind + 1) * DK] = total


def rim_back(conv, masks, taps, dqkv, cols):
    heads = taps.shape[1] // (4 * DK)
    return pl.pallas_call(
        functools.partial(rim_back_kernel, heads),
        out_shape=jax.ShapeDtypeStruct((8, cols), F32),
        compiler_params=params(),
        cost_estimate=cost(1000, 100000),
        name="rim_back",
    )(conv[:8], masks[:8], taps, dqkv[:8])


def act_block(c):
    return lax.div(c, 6) * 4 + jnp.minimum(lax.rem(c, 6), 3)


def gate_block(c):
    return lax.div(c, 6) * 2 + jnp.maximum(lax.rem(c, 6) - 4, 0)


def front_back(raw, rim, conv, masks, taps, dqkv, dg):
    tokens, cols = raw.shape
    block = spec((tokens, DK), lambda c: (0, c))
    act_spec = spec((tokens, DK), lambda c: (0, act_block(c)))
    return pl.pallas_call(
        front_back_kernel,
        grid=(cols // DK,),
        in_specs=[
            block,
            spec((16, DK), lambda c: (0, c)),
            act_spec,
            spec((tokens, 8), lambda c: (0, 0)),
            spec((4, DK), lambda c: (0, act_block(c))),
            act_spec,
            spec((tokens, DK), lambda c: (0, gate_block(c))),
        ],
        out_specs=[
            block,
            spec((16, DK), lambda c: (0, c)),
            spec((4, DK), lambda c: (0, c)),
        ],
        out_shape=[
            jax.ShapeDtypeStruct((tokens, cols), BF16),
            jax.ShapeDtypeStruct((16, cols), F32),
            jax.ShapeDtypeStruct((4, cols), F32),
        ],
        compiler_params=params(),
        cost_estimate=cost(tokens * cols * 80, tokens * cols * 14),
        name="front_back",
    )(raw, rim, conv, masks, taps, dqkv, dg)


def flip(value, bit):
    count = lax.axis_size("mp")
    return lax.ppermute(value, "mp", [(i, i ^ (1 << bit)) for i in range(count)])


def bit_count():
    return lax.axis_size("mp").bit_length() - 1


def exchange(values, bits):
    values = lax.optimization_barrier(tuple(values))
    return lax.optimization_barrier(tuple(flip(v, b) for v, b in zip(values, bits)))


def gather_mp(share):
    bits = bit_count()
    half = share.shape[0] // 2
    orders = (list(range(bits - 1, 0, -1)), list(range(1, bits)))
    held = [share[w * half : (w + 1) * half][None] for w in range(2)]
    rels = [[0], [0]]
    for turn in range(bits - 1):
        now = [order[turn] for order in orders]
        got = exchange(held, now)
        held = [jnp.concatenate([h, g], axis=0) for h, g in zip(held, got)]
        rels = [rel + [r | (1 << bit) for r in rel] for rel, bit in zip(rels, now)]
    got = exchange(held, [0, 0])
    return [(h, g, rel) for h, g, rel in zip(held, got, rels)]


def gathered_specs(found, tile, tiles):
    specs = []
    for which, (held, other, rel) in enumerate(found):
        shape = (held.shape[0], tile, held.shape[2])
        if which == 0:
            index = lambda i, m: (0, jnp.minimum(i, tiles - 1), 0)
        else:
            index = lambda i, m: (0, jnp.maximum(i - tiles, 0), 0)
        specs += [spec(shape, index)] * 2
    return specs


def gathered_args(found):
    return [x for held, other, rel in found for x in (held, other)]


def gathered_blocks(found, refs, which):
    held, other = refs[2 * which], refs[2 * which + 1]
    rel = found[which][2]
    blocks = [(r, held[i].astype(F32)) for i, r in enumerate(rel)]
    return blocks + [(r | 1, other[i].astype(F32)) for i, r in enumerate(rel)]


def place(mp_ref, r, cols):
    return pl.ds(pl.multiple_of((mp_ref[0] ^ r) * cols, cols), cols)


def norm_kernel(rels, cols, tiles, mode, *refs):
    mp_ref, refs = refs[0], refs[1:]
    found = [(None, None, rel) for rel in rels]
    if mode == "plain":
        out_ref = refs[4]
    else:
        gain_ref, out_ref, inv_ref = refs[4:7]
    for which in range(2):

        @pl.when((pl.program_id(0) < tiles) == (which == 0))
        def _():
            blocks = gathered_blocks(found, refs, which)
            if mode == "plain":
                for r, x in blocks:
                    out_ref[:, place(mp_ref, r, cols)] = x.astype(BF16)
                return
            total = sum(jnp.sum(x * x, axis=-1, keepdims=True) for _, x in blocks)
            inv = lax.rsqrt(total * (1.0 / (cols * len(blocks))) + 1e-05)
            for r, x in blocks:
                at = place(mp_ref, r, cols)
                out_ref[:, at] = (x * inv * gain_ref[:, at]).astype(BF16)
            inv_ref[...] = jnp.broadcast_to(inv, inv_ref.shape)


def assemble(found, mp_pos, gain=None):
    half, cols = found[0][0].shape[1:]
    rels = [f[2] for f in found]
    width = cols * 2 * len(rels[0])
    tokens = 2 * half
    tile = min(256, half)
    tiles = half // tile
    mode = "plain" if gain is None else "norm"
    row_spec = spec((tile, width), lambda i, m: (i, 0))
    in_specs = gathered_specs(found, tile, tiles)
    out_specs = [row_spec]
    out_shape = [jax.ShapeDtypeStruct((tokens, width), BF16)]
    args = gathered_args(found)
    if gain is not None:
        in_specs.append(spec((1, width), lambda i, m: (0, 0)))
        args.append(gain.reshape(1, width))
        out_specs.append(spec((tile, 128), lambda i, m: (i, 0)))
        out_shape.append(jax.ShapeDtypeStruct((tokens, 128), F32))
    return pl.pallas_call(
        functools.partial(norm_kernel, rels, cols, tiles, mode),
        grid_spec=pltpu.PrefetchScalarGridSpec(
            num_scalar_prefetch=1,
            grid=(2 * tiles,),
            in_specs=in_specs,
            out_specs=out_specs,
        ),
        out_shape=out_shape,
        compiler_params=params(),
        cost_estimate=cost(tokens * width * 10, tokens * width * 4),
        name="assemble",
    )(mp_pos.reshape(1).astype(jnp.int32), *args)


def norm_back_kernel(rels, cols, tiles, *refs):
    mp_ref, refs = refs[0], refs[1:]
    found = [(None, None, rel) for rel in rels]
    grads, mids = refs[:4], refs[4:8]
    up_ref, gain_ref, own_grad_ref, own_mid_ref, out_ref, own_out_ref, dgain_ref = refs[8:]

    @pl.when(pl.program_id(0) == 0)
    def _():
        dgain_ref[...] = jnp.zeros_like(dgain_ref)

    for which in range(2):

        @pl.when((pl.program_id(0) < tiles) == (which == 0))
        def _():
            grad = gathered_blocks(found, grads, which)
            mid = gathered_blocks(found, mids, which)
            scale = 1.0 / (cols * len(grad))
            total = sum(jnp.sum(x * x, axis=-1, keepdims=True) for _, x in mid)
            inv = lax.rsqrt(total * scale + 1e-05)
            scaled = [(r, g * gain_ref[:, place(mp_ref, r, cols)]) for r, g in grad]
            mean = sum(
                jnp.sum(g * x, axis=-1, keepdims=True) for (_, g), (_, x) in zip(scaled, mid)
            )
            shrink = inv * inv * (mean * scale)
            for (r, g), (_, x) in zip(scaled, mid):
                at = place(mp_ref, r, cols)
                out_ref[:, at] = (up_ref[:, at].astype(F32) + inv * (g - x * shrink)).astype(BF16)
            at = place(mp_ref, 0, cols)
            own_grad, own_mid = own_grad_ref[...], own_mid_ref[...]
            own_out_ref[...] = up_ref[:, at].astype(F32) + inv * (
                own_grad * gain_ref[:, at] - own_mid * shrink
            )
            dgain_ref[...] += jnp.sum(own_grad * own_mid * inv, axis=0, keepdims=True)


def norm_back(found_grad, found_mid, full_grad, gain, own_grad, own_mid, mp_pos):
    half, cols = found_grad[0][0].shape[1:]
    rels = [f[2] for f in found_grad]
    tokens, width = full_grad.shape
    tile = min(256, half)
    tiles = half // tile
    row_spec = spec((tile, width), lambda i, m: (i, 0))
    own_spec = spec((tile, cols), lambda i, m: (i, 0))
    return pl.pallas_call(
        functools.partial(norm_back_kernel, rels, cols, tiles),
        grid_spec=pltpu.PrefetchScalarGridSpec(
            num_scalar_prefetch=1,
            grid=(2 * tiles,),
            in_specs=gathered_specs(found_grad, tile, tiles)
            + gathered_specs(found_mid, tile, tiles)
            + [row_spec, spec((1, width), lambda i, m: (0, 0)), own_spec, own_spec],
            out_specs=[row_spec, own_spec, spec((1, cols), lambda i, m: (0, 0))],
        ),
        out_shape=[
            jax.ShapeDtypeStruct((tokens, width), BF16),
            jax.ShapeDtypeStruct((tokens, cols), F32),
            jax.ShapeDtypeStruct((1, cols), F32),
        ],
        compiler_params=params(),
        cost_estimate=cost(tokens * width * 20, tokens * width * 8),
        name="norm_back",
    )(
        mp_pos.reshape(1).astype(jnp.int32),
        *gathered_args(found_grad),
        *gathered_args(found_mid),
        full_grad,
        gain.reshape(1, width),
        own_grad,
        own_mid,
    )


def block_kernel(turns, mp_ref, *refs):
    out_ref = refs[2 * len(turns)]
    total = None
    for i, turned in enumerate(turns):
        part = d1(refs[2 * i][...], refs[2 * i + 1][...], NN if turned is False else NT)
        total = part if total is None else total + part
    out_ref[0] = total.astype(out_ref.dtype)


def right_index(parity, turned, g, m):
    at = (2 * g + parity) ^ m[0]
    return (at, 0) if turned else (0, at)


def spaced_index(parity, cols, rows, g, m):
    at = ((2 * g + parity) ^ m[0]) * cols
    return (pl.multiple_of(at + lax.div(at, rows) * 16, 16), 0)


def block_products(terms, mp_pos, cols, parity):
    tokens = terms[0][0].shape[0]
    count = lax.axis_size("mp") // 2
    in_specs, args, flops = [], [], 0
    for left, right, turned in terms:
        depth = left.shape[1]
        in_specs.append(spec((tokens, depth), lambda g, m: (0, 0)))
        if turned is None:
            rows = right.shape[0] // lax.axis_size("seq") - 16
            index = functools.partial(spaced_index, parity, cols, rows)
            in_specs.append(pl.BlockSpec((pl.Element(cols), pl.Element(depth)), index))
        else:
            index = functools.partial(right_index, parity, turned)
            in_specs.append(spec((cols, depth) if turned else (depth, cols), index))
        args += [left, right]
        flops += 2 * tokens * depth * cols * count
    return pl.pallas_call(
        functools.partial(block_kernel, [t[2] for t in terms]),
        grid_spec=pltpu.PrefetchScalarGridSpec(
            num_scalar_prefetch=1,
            grid=(count,),
            in_specs=in_specs,
            out_specs=spec((1, tokens, cols), lambda g, m: (g, 0, 0)),
        ),
        out_shape=jax.ShapeDtypeStruct((count, tokens, cols), BF16 if parity else F32),
        compiler_params=params(),
        cost_estimate=cost(flops, tokens * cols * count * 4),
        name="block_products",
    )(mp_pos.reshape(1).astype(jnp.int32), *args)


def reduce_mp(terms, mp_pos, cols):
    sent = flip(block_products(terms, mp_pos, cols, 1), 0)
    kept = block_products(terms, mp_pos, cols, 0)
    bits = bit_count()
    half = kept.shape[1] // 2
    orders = (list(range(1, bits)), list(range(bits - 1, 0, -1)))
    rels = [[2 * i for i in range(kept.shape[0])] for _ in orders]
    helds = []
    for which in range(2):
        at = slice(which * half, (which + 1) * half)
        helds.append({r: kept[i, at] + sent[i, at].astype(F32) for i, r in enumerate(rels[which])})
    for turn in range(bits - 1):
        aways = [[r for r in rels[w] if (r >> orders[w][turn]) & 1] for w in range(2)]
        gots = exchange(
            [jnp.stack([helds[w][r].astype(BF16) for r in aways[w]]) for w in range(2)],
            [orders[w][turn] for w in range(2)],
        )
        for w in range(2):
            bit = orders[w][turn]
            rels[w] = [r for r in rels[w] if not (r >> bit) & 1]
            helds[w] = {
                r: helds[w][r] + gots[w][aways[w].index(r | (1 << bit))].astype(F32) for r in rels[w]
            }
    return jnp.concatenate([helds[0][0], helds[1][0]], axis=0), kept


def sum_mp(value):
    for bit in range(bit_count()):
        value = value + flip(value, bit)
    return value


def sum_seq(value):
    count = lax.axis_size("seq")
    total = value
    for step in range(1, count):
        total = total + lax.ppermute(value, "seq", [(i, (i + step) % count) for i in range(count)])
    return total


def shifted(value, steps):
    count = lax.axis_size("seq")
    first, last = max(0, -steps), min(count, count - steps)
    return lax.ppermute(value, "seq", [(i, i + steps) for i in range(first, last)])


def batched(left, right):
    return jnp.einsum("hde,hev->hdv", left, right, precision=lax.Precision.HIGHEST)


def dot(left, right, dims=NN):
    return lax.dot_general(left, right, dims, preferred_element_type=F32)


TN = (((0,), (0,)), ((), ()))


def first_kernel(
    heads, count, rows, x_ref, rim_ref, w_ref, mask_ref, scale_ref, bias_ref,
    raw_ref, pre_ref, gate_ref, rim_raw_ref,
):
    @pl.when(pl.program_id(0) == 0)
    def _():
        total = None
        for s in range(count):
            at = s * (rows + 16)
            part = d1(rim_ref[:, s * rows : (s + 1) * rows], w_ref[at : at + rows, :])
            total = part if total is None else total + part
        rim_raw_ref[...] = total

    raw, pre = None, None
    for s in range(count):
        at = s * (rows + 16)
        part = x_ref[:, s * rows : (s + 1) * rows]
        left = d1(part, w_ref[at : at + rows, :])
        right = d1(part, w_ref[at + rows : at + rows + 16, :rows], NT)
        raw = left if raw is None else raw + left
        pre = right if pre is None else pre + right
    raw_ref[...] = raw
    pre_ref[...] = pre
    masks = mask_ref[...]
    lane = lax.broadcasted_iota(jnp.int32, masks.shape, 1)
    for h in range(heads):
        x = pre[:, 2 * h : 2 * h + 1] + bias_ref[h]
        soft = jnp.maximum(x, 0.0) + jnp.log1p(jnp.exp(-jnp.abs(x)))
        beta = jax.nn.sigmoid(pre[:, 2 * h + 1 : 2 * h + 2])
        gate_ref[h] = jnp.where(
            lane == 0, -scale_ref[h] * soft, jnp.where(lane == 1, beta, masks)
        )


def project_first(normed, rim, mixer, masks, scale, bias):
    tokens, width = normed.shape
    count = lax.axis_size("seq")
    rows, cols = mixer.shape[0] // count - 16, mixer.shape[1]
    heads = scale.shape[0]
    tile = 256
    scalar = pl.BlockSpec(memory_space=pltpu.SMEM)
    return pl.pallas_call(
        functools.partial(first_kernel, heads, count, rows),
        grid=(tokens // tile,),
        in_specs=[
            spec((tile, width), lambda i: (i, 0)),
            spec((16, width), lambda i: (0, 0)),
            spec(mixer.shape, lambda i: (0, 0)),
            spec((tile, 8), lambda i: (i, 0)),
            scalar,
            scalar,
        ],
        out_specs=[
            spec((tile, cols), lambda i: (i, 0)),
            spec((tile, 16), lambda i: (i, 0)),
            spec((heads, tile, 8), lambda i: (0, i, 0)),
            spec((16, cols), lambda i: (0, 0)),
        ],
        out_shape=[
            jax.ShapeDtypeStruct((tokens, cols), F32),
            jax.ShapeDtypeStruct((tokens, 16), F32),
            jax.ShapeDtypeStruct((heads, tokens, 8), F32),
            jax.ShapeDtypeStruct((16, cols), F32),
        ],
        compiler_params=params(),
        cost_estimate=cost(2 * tokens * width * cols, tokens * width * 2 + width * cols * 2),
        name="project_first",
    )(normed, rim, mixer, masks, scale, bias)


def gates_back_kernel(heads, pre_ref, dg_ref, scale_ref, bias_ref, low_ref, sums_ref):
    pre = pre_ref[...]
    lane = lax.broadcasted_iota(jnp.int32, pre.shape, 1)
    line = lax.broadcasted_iota(jnp.int32, (1, 128), 1)
    low = jnp.zeros(pre.shape, F32)
    for h in range(heads):
        x = pre[:, 2 * h : 2 * h + 1] + bias_ref[h]
        soft = jnp.maximum(x, 0.0) + jnp.log1p(jnp.exp(-jnp.abs(x)))
        beta = jax.nn.sigmoid(pre[:, 2 * h + 1 : 2 * h + 2])
        dlog = dg_ref[h][:, 0:1]
        dx = dlog * (-scale_ref[h] * jax.nn.sigmoid(x))
        db = dg_ref[h][:, 1:2] * (beta * (1.0 - beta))
        low = jnp.where(lane == 2 * h, dx, jnp.where(lane == 2 * h + 1, db, low))
        dscale = jnp.sum(-dlog * soft, axis=0, keepdims=True)
        dbias = jnp.sum(dx, axis=0, keepdims=True)
        sums_ref[h : h + 1, :] = jnp.where(line == 0, dscale, jnp.where(line == 1, dbias, 0.0))
    low_ref[...] = low.astype(BF16)


def gates_back(pre, dgates, scale, bias):
    tokens = pre.shape[0]
    heads = scale.shape[0]
    scalar = pl.BlockSpec(memory_space=pltpu.SMEM)
    whole = pl.BlockSpec(memory_space=pltpu.VMEM)
    return pl.pallas_call(
        functools.partial(gates_back_kernel, heads),
        in_specs=[whole, whole, scalar, scalar],
        out_specs=[whole, whole],
        out_shape=[
            jax.ShapeDtypeStruct((tokens, 16), BF16),
            jax.ShapeDtypeStruct((heads, 128), F32),
        ],
        compiler_params=params(),
        cost_estimate=cost(tokens * 1000, tokens * 1024),
        name="gates_back",
    )(pre, dgates, scale, bias)


def unpack(value, units):
    whole = units // 128 * 128
    rest = value[:, 2 * whole :]
    tail = units - whole
    gate = jnp.concatenate([value[:, :whole], rest[:, :tail]], axis=1)
    return gate, jnp.concatenate([value[:, whole : 2 * whole], rest[:, tail:]], axis=1)


def pack(gate, up):
    whole = gate.shape[1] // 128 * 128
    return jnp.concatenate(
        [gate[:, :whole], up[:, :whole], gate[:, whole:], up[:, whole:]], axis=1
    )


def ffn_kernel(units, x_ref, dy_ref, gu_ref, down_ref, hid_ref, dgu_ref):
    gate, up = unpack(d1(x_ref[...], gu_ref[...]), units)
    back = d1(dy_ref[...], down_ref[...], NT)
    sig = jax.nn.sigmoid(gate)
    silu = gate * sig
    hid_ref[...] = (silu * up).astype(BF16)
    dgu_ref[...] = pack(
        (back * up * sig * (1.0 + gate * (1.0 - sig))), (back * silu)
    ).astype(BF16)


def ffn(normed2, full_grad, gu_full, down_full):
    tokens, width = normed2.shape
    units = down_full.shape[0]
    tile = 256
    row_spec = spec((tile, width), lambda i: (i, 0))
    return pl.pallas_call(
        functools.partial(ffn_kernel, units),
        grid=(tokens // tile,),
        in_specs=[
            row_spec,
            row_spec,
            spec((width, 2 * units), lambda i: (0, 0)),
            spec((units, width), lambda i: (0, 0)),
        ],
        out_specs=[
            spec((tile, units), lambda i: (i, 0)),
            spec((tile, 2 * units), lambda i: (i, 0)),
        ],
        out_shape=[
            jax.ShapeDtypeStruct((tokens, units), BF16),
            jax.ShapeDtypeStruct((tokens, 2 * units), BF16),
        ],
        compiler_params=params(),
        cost_estimate=cost(6 * tokens * width * units, tokens * width * 4 + width * units * 6),
        name="ffn",
    )(normed2, full_grad, gu_full, down_full)


def after(value, *earlier):
    return lax.optimization_barrier((value, earlier))[0]


def ring_gather(value):
    pairs = [(shifted(value, 1), shifted(value, -1))]
    for _ in range(2, lax.axis_size("seq")):
        pairs.append((shifted(pairs[-1][0], 1), shifted(pairs[-1][1], -1)))
    return pairs


def together(*values):
    return lax.optimization_barrier(values)


def join_ring(own, pairs, axis):
    seq_count = lax.axis_size("seq")
    seq_pos = lax.axis_index("seq")
    size = own.shape[axis]
    shape = list(own.shape)
    shape[axis] = size * seq_count
    full = jnp.zeros(tuple(shape), own.dtype)
    full = lax.dynamic_update_slice_in_dim(full, own, seq_pos * size, axis)
    for j in range(1, seq_count):
        piece = jnp.where(seq_pos >= j, pairs[j - 1][0], pairs[seq_count - j - 1][1])
        at = lax.rem(seq_pos - j + seq_count, seq_count) * size
        full = lax.dynamic_update_slice_in_dim(full, piece, at, axis)
    return full


def chain(steps, ends, sign):
    total = shifted(ends.astype(BF16), sign).astype(F32)
    for _ in range(lax.axis_size("seq") - 2):
        total = shifted((batched(steps, total) + ends).astype(BF16), sign).astype(F32)
    return total


def scatter_seq(value, axis):
    return lax.psum_scatter(value, "seq", scatter_dimension=axis, tiled=True).astype(F32)


def shards(
    residual,
    attn_gain,
    w_mixer,
    w_gates,
    conv_taps,
    decay_scale,
    dt_bias,
    head_gain,
    w_out,
    ffn_gain,
    w_gate,
    w_up,
    w_down,
    out_grad,
    doc_ids,
):
    tokens, cols = residual.shape
    seq_count = lax.axis_size("seq")
    mp_count = lax.axis_size("mp")
    seq_pos = lax.axis_index("seq")
    mp_pos = lax.axis_index("mp")
    rows, heads = w_mixer.shape[:2]
    width = rows * seq_count

    padded = jnp.concatenate([jnp.full((3,), -1, jnp.int32), doc_ids])
    window = lax.dynamic_slice_in_dim(padded, seq_pos * tokens, tokens + 3)
    ids = window[3:]
    prior = jnp.repeat(window[2 : 2 + tokens].reshape(-1, CHUNK)[:, 0], CHUNK)
    same = [(window[3 - j : 3 - j + tokens] == ids).astype(F32) for j in range(1, 4)]
    ids_f, prior_f = ids.astype(F32), prior.astype(F32)
    zero = jnp.zeros((tokens,), F32)
    masks = jnp.stack([zero] * 2 + [ids_f, prior_f] + same + [zero], axis=1)

    units = w_gate.shape[1]
    mix_cols = heads * (2 * DK + 2 * DV)
    gate_part = jnp.pad(
        w_gates.reshape(rows, 2 * heads).T, ((0, 16 - 2 * heads), (0, mix_cols - rows))
    )
    mixer_part = jnp.concatenate([w_mixer.reshape(rows, mix_cols), gate_part])
    do_part = jnp.concatenate([w_out, w_down])
    gu_part = pack(w_gate, w_up)
    mixer_full = lax.all_gather(mixer_part, "seq", axis=0, tiled=True)
    found_res = gather_mp(residual)
    do_full = lax.all_gather(after(do_part, found_res[0][0]), "seq", axis=1, tiled=True)

    normed, inv1 = assemble(found_res, mp_pos, attn_gain)
    gu_full = lax.all_gather(after(gu_part, normed), "seq", axis=0, tiled=True)
    found_og = gather_mp(after(out_grad, normed))
    full_grad = assemble(found_og, mp_pos)[0]
    mixer_full = after(mixer_full, full_grad)
    rim_normed = shifted(normed[tokens - 16 :], 1)
    raw, gate_pre, gates, rim = project_first(
        normed, rim_normed, mixer_full, masks, decay_scale, dt_bias
    )
    taps = conv_taps.reshape(4, heads * 2 * DV)
    qkv, conv = front(raw, rim, masks, taps)

    inverse, inv_turned, scores, scores_turned, kept, wkeys, reach, reach_turned, steps, steps_turned = (
        delta_prep(qkv, gates)
    )
    trans, back = delta_trans(steps, steps_turned)
    pseudo, local_out, states, state_end = delta_values(qkv, gates, inverse, scores, steps)
    start = chain(trans[:, -1], state_end, 1)
    mixed, outs, held, corrected = delta_output(
        start, states, trans, reach, wkeys, pseudo, local_out, raw, head_gain
    )

    out_full, down_full = do_full[: w_out.shape[0]], do_full[w_out.shape[0] :]
    branch, _ = reduce_mp([(mixed, out_full, False)], mp_pos, cols)
    middle = residual.astype(F32) + branch
    found_mid = gather_mp(middle.astype(BF16))
    normed2, _ = assemble(found_mid, mp_pos, ffn_gain)
    hidden, grad_gu = ffn(normed2, full_grad, gu_full, down_full)
    part_gu = dot(normed2, grad_gu, TN).astype(BF16)
    grad_gu = after(grad_gu, part_gu)
    grad_normed2, kept_gn2 = reduce_mp([(grad_gu, gu_full, True)], mp_pos, cols)
    dw_gu = lax.psum_scatter(part_gu, "seq", scatter_dimension=0, tiled=True)
    part_down = dot(after(hidden, kept_gn2), full_grad, TN).astype(BF16)
    found_gn2 = gather_mp(grad_normed2.astype(BF16))

    grad_branch, grad_middle, dffn_gain = norm_back(
        found_gn2, found_mid, full_grad, ffn_gain, grad_normed2, middle, mp_pos
    )
    grad_mixed = dot(grad_branch, out_full, NT)

    dout, dg_raw, dhead_gain, dstates, dstart = delta_tail(
        grad_mixed, outs, raw, head_gain, reach_turned, steps_turned
    )
    part_out = dot(mixed, after(grad_branch, dstart), TN).astype(BF16)
    part_do = jnp.concatenate([part_out, part_down])
    dw_do = lax.psum_scatter(part_do, "seq", scatter_dimension=1, tiled=True)
    early = delta_early(scores_turned, corrected, held, after(dout, dstart))
    grad_end = chain(back[:, 0], dstart, -1)
    grad_end = after(grad_end, part_do, early)
    dqkv, dgates = delta_grads(
        grad_end, qkv, gates, inv_turned, scores, kept, corrected, held, dstates, back[:, 1:],
        early,
    )
    drim = rim_back(conv, masks, taps, dqkv, mix_cols)
    came = shifted(drim, -1)
    dproj, edge, dtaps = front_back(raw, rim, conv, masks, taps, after(dqkv, drim), dg_raw)
    edge = jnp.concatenate([edge[:8], edge[8:] + came])
    dproj = lax.dynamic_update_slice_in_dim(dproj, edge.astype(BF16), tokens - 16, 0)
    dgate_low, gate_sums = gates_back(gate_pre, dgates, decay_scale, dt_bias)

    part_mixer = dot(normed, dproj, TN).astype(BF16)
    dw_mixer = lax.psum_scatter(part_mixer, "seq", scatter_dimension=0, tiled=True)
    dproj, dgate_low = after((dproj, dgate_low), part_mixer)
    part_gates = dot(dgate_low, normed, TN)
    gates_full = jnp.swapaxes(
        mixer_full.reshape(seq_count, rows + 16, mix_cols)[:, rows:, :rows], 0, 1
    ).reshape(16, width)
    grad_normed, kept_gn = reduce_mp(
        [(dproj, mixer_full, None), (dgate_low, gates_full, False)], mp_pos, cols
    )
    ffn_part, _ = reduce_mp([(after(hidden, kept_gn), down_full, False)], mp_pos, cols)
    output = (middle + ffn_part).astype(BF16)
    own_gain = lax.dynamic_slice_in_dim(attn_gain, mp_pos * cols, cols)
    own_res = residual.astype(F32)
    inv1 = inv1[:, :1]
    scaled = grad_normed * own_gain
    mean = jnp.sum(scaled * own_res, axis=-1).reshape(-1, 128)
    mean = sum_mp(mean).reshape(tokens, 1) * (1.0 / width)
    grad_residual = grad_middle + inv1 * (scaled - own_res * (inv1 * inv1 * mean))
    dattn_gain = jnp.sum(grad_normed * own_res * inv1, axis=0)

    dw_gate, dw_up = unpack(dw_gu, units)

    dtaps = dtaps.reshape(4, heads, 2 * DK + 2 * DV)[:, :, : 2 * DK + DV]
    small = [
        dattn_gain, dffn_gain, dhead_gain, gate_sums[:, 0], gate_sums[:, 1], dtaps,
        part_gates[: 2 * heads],
    ]
    packed = jnp.concatenate([value.reshape(-1) for value in small])
    packed = jnp.pad(packed, (0, -packed.shape[0] % 1024)).reshape(-1, 128)
    packed = sum_seq(packed).reshape(-1)
    sums, at = [], 0
    for value in small:
        sums.append(packed[at : at + value.size].reshape(value.shape))
        at += value.size
    gains = jnp.stack([sums[0], sums[1].reshape(-1)])
    gains = lax.dynamic_update_slice(jnp.zeros((2, width), F32), gains, (0, mp_pos * cols))
    gains = sum_mp(gains)
    dw_gates = lax.dynamic_slice_in_dim(sums[6], seq_pos * rows, rows, 1)
    return (
        output,
        grad_residual,
        gains[0],
        dw_mixer.astype(F32).reshape(rows, heads, 2 * DK + 2 * DV),
        dw_gates.T.reshape(rows, heads, 2),
        sums[5],
        sums[3],
        sums[4],
        sums[2],
        dw_do[: w_out.shape[0]].astype(F32),
        gains[1],
        dw_gate.astype(F32),
        dw_up.astype(F32),
        dw_do[w_out.shape[0] :].astype(F32),
    )


def solution(mesh):
    in_specs = (
        P("seq", "mp"),
        P(),
        P("seq", "mp", None),
        P("seq", "mp", None),
        P(None, "mp", None),
        P("mp"),
        P("mp"),
        P("mp", None),
        P("mp", "seq"),
        P(),
        P("seq", "mp"),
        P("seq", "mp"),
        P("mp", "seq"),
        P("seq", "mp"),
        P(),
    )
    out_specs = (
        P("seq", "mp"),
        P("seq", "mp"),
        P(),
        P("seq", "mp", None),
        P("seq", "mp", None),
        P(None, "mp", None),
        P("mp"),
        P("mp"),
        P("mp", None),
        P("mp", "seq"),
        P(),
        P("seq", "mp"),
        P("seq", "mp"),
        P("mp", "seq"),
    )
    return jax.shard_map(shards, mesh=mesh, in_specs=in_specs, out_specs=out_specs, check_vma=False)
```

```python
import functools
import jax
import jax.numpy as jnp
from jax import lax
from jax.experimental import pallas as pl
from jax.experimental.pallas import tpu as pltpu
from jax.sharding import PartitionSpec as P

DK = 128
DV = 256
CHUNK = 128
GATE_LANES = 8
F32 = jnp.float32
BF16 = jnp.bfloat16
NN = (((1,), (0,)), ((), ()))
NT = (((1,), (1,)), ((), ()))
VMEM_LIMIT = 48 * 1024 * 1024


def d1(left, right, dims=NN):
    return lax.dot_general(
        left.astype(BF16), right.astype(BF16), dims, preferred_element_type=F32
    )


def dx(left, right, dims=NN):
    if left.dtype == BF16 and right.dtype == BF16:
        return d1(left, right, dims)
    return d3(left.astype(F32), right.astype(F32), dims)


def split(value):
    high = value.astype(BF16)
    return high, (value - high.astype(F32)).astype(BF16)


def d3(left, right, dims=NN):
    lh, ll = split(left)
    rh, rl = split(right)
    return d1(lh, rh, dims) + (d1(lh, rl, dims) + d1(ll, rh, dims))


def params():
    return pltpu.CompilerParams(vmem_limit_bytes=VMEM_LIMIT)


def cost(flops, nbytes):
    return pl.CostEstimate(flops=int(flops) // 100, bytes_accessed=int(nbytes) // 100, transcendentals=0)


def spec(shape, index_map):
    return pl.BlockSpec(shape, index_map)


def rows_cols():
    row = lax.broadcasted_iota(jnp.int32, (CHUNK, CHUNK), 0)
    col = lax.broadcasted_iota(jnp.int32, (CHUNK, CHUNK), 1)
    return row, col


def to_row(column, row, col):
    return jnp.sum(jnp.where(row == col, column, 0.0), axis=0, keepdims=True)


def to_col(line, row, col):
    return jnp.sum(jnp.where(row == col, line, 0.0), axis=1, keepdims=True)


def decay_parts(gates, row, col):
    log_decay, beta, ids, prior = (gates[:, i : i + 1] for i in range(4))
    cum_row = jnp.sum(jnp.where(row <= col, log_decay, 0.0), axis=0, keepdims=True)
    cum_col = to_col(cum_row, row, col)
    same = ids == to_row(ids, row, col)
    inside = (row >= col) & same
    decays = jnp.where(inside, jnp.exp(jnp.where(inside, cum_col - cum_row, 0.0)), 0.0)
    carried = jnp.where(ids == prior, jnp.exp(cum_col), 0.0)
    last_ids = ids[CHUNK - 1 : CHUNK]
    last_cum = cum_col[CHUNK - 1 : CHUNK]
    to_end = jnp.where(ids == last_ids, jnp.exp(last_cum - cum_col), 0.0)
    return beta, decays, carried, to_end


def invert(lowers, row, col):
    eye = jnp.where(row == col, 1.0, 0.0)
    found = None
    shift = 0
    while (1 << shift) < CHUNK:
        mask = ((row >> (shift + 1)) == (col >> (shift + 1))) & (
            (row >> shift) > (col >> shift)
        )
        masked = [jnp.where(mask, lower, 0.0) for lower in lowers]
        if found is None:
            found = [eye - m for m in masked]
        else:
            low = [x.astype(BF16) for x in found]
            inner = [d1(m, x) for m, x in zip(masked, low)]
            outer = [d1(x, y) for x, y in zip(low, inner)]
            found = [x - y for x, y in zip(found, outer)]
        shift += 1
    rest = [d3(lower, x) for lower, x in zip(lowers, found)]
    rest = [(eye - x) - r for x, r in zip(found, rest)]
    return [x + d1(x, r) for x, r in zip(found, rest)]


def prep_kernel(
    group, qk_ref, gt_ref, t_ref, tt_ref, a_ref, at_ref, lk_ref, w_ref, p_ref, pt_ref, m_ref, mt_ref
):
    row, col = rows_cols()
    queries, keys, parts = [], [], []
    for c in range(group):
        block = qk_ref[c * CHUNK : (c + 1) * CHUNK, :]
        queries.append(block[:, :DK])
        keys.append(block[:, DK:])
        parts.append(decay_parts(gt_ref[0, c * CHUNK : (c + 1) * CHUNK, :], row, col))
    gram = [d3(k, k, NT) for k in keys]
    scores = [dx(q, k, NT) for q, k in zip(queries, keys)]
    kept = [jnp.where(row > col, p[1] * g, 0.0) for p, g in zip(parts, gram)]
    lowers = [x * p[0] for x, p in zip(kept, parts)]
    inverses = invert(lowers, row, col)
    eye = jnp.where(row == col, 1.0, 0.0)
    for c in range(group):
        beta, decays, carried, to_end = parts[c]
        inverse = inverses[c]
        t_ref[0, c] = inverse
        tt_ref[0, c] = inverses[c].T
        score = decays * scores[c]
        a_ref[0, c] = score
        at_ref[0, c] = score.T
        lk_ref[0, c] = kept[c]
        wkeys = dx(inverse, (beta * carried) * keys[c])
        w_ref[0, c] = wkeys
        reach = carried * queries[c] - dx(score, wkeys)
        p_ref[0, c] = reach
        pt_ref[0, c] = reach.T
        end_keys = to_end * keys[c]
        step = carried[CHUNK - 1 : CHUNK] * eye - dx(end_keys.T, wkeys)
        m_ref[0, c] = step
        mt_ref[0, c] = step.T


def delta_prep(qk, gates):
    heads, tokens, _ = gates.shape
    count = tokens // CHUNK
    group = min(4, count)
    rows = group * CHUNK
    low = jax.ShapeDtypeStruct((heads, count, CHUNK, CHUNK), F32)
    wide = jax.ShapeDtypeStruct((heads, count, DK, DK), F32)
    out_spec = spec((1, group, CHUNK, CHUNK), lambda h, g: (h, g, 0, 0))
    return pl.pallas_call(
        functools.partial(prep_kernel, group),
        grid=(heads, count // group),
        in_specs=[
            spec((rows, 2 * DK), lambda h, g: (g, 2 * h)),
            spec((1, rows, GATE_LANES), lambda h, g: (h, g, 0)),
        ],
        out_specs=[out_spec] * 10,
        out_shape=[low] * 8 + [wide] * 2,
        compiler_params=params(),
        cost_estimate=cost(heads * count * 40 * 2 * CHUNK**3 * 8, heads * count * CHUNK * CHUNK * 24),
        name="delta_prep",
    )(qk, gates)


def trans_kernel(heads, count, m_ref, mt_ref, fwd_ref, back_ref):
    row, col = rows_cols()
    eye = jnp.where(row == col, 1.0, 0.0)
    fwd = [eye] * heads
    back = [eye] * heads
    for h in range(heads):
        fwd_ref[h, 0] = eye
        back_ref[h, count] = eye
    for c in range(count):
        if c == 0:
            fwd = [m_ref[h, 0] for h in range(heads)]
            back = [mt_ref[h, count - 1] for h in range(heads)]
        else:
            fwd = [d3(m_ref[h, c], fwd[h]) for h in range(heads)]
            back = [d3(mt_ref[h, count - 1 - c], back[h]) for h in range(heads)]
        for h in range(heads):
            fwd_ref[h, c + 1] = fwd[h]
            back_ref[h, count - 1 - c] = back[h]


def delta_trans(steps, steps_turned):
    heads, count = steps.shape[:2]
    shape = jax.ShapeDtypeStruct((heads, count + 1, DK, DK), F32)
    return pl.pallas_call(
        functools.partial(trans_kernel, heads, count),
        out_shape=[shape, shape],
        compiler_params=params(),
        cost_estimate=cost(heads * count * 6 * 2 * DK**3 * 8, heads * count * DK * DK * 16),
        name="delta_trans",
    )(steps, steps_turned)


def values_kernel(
    heads, group, qkv_ref, gt_ref, t_ref, a_ref, m_ref, ut_ref, o_ref, s_ref, end_ref, state
):
    @pl.when(pl.program_id(0) == 0)
    def _():
        state[...] = jnp.zeros_like(state)

    row, col = rows_cols()
    pairs = [(h, c) for c in range(group) for h in range(heads)]
    offsets = {}
    for h, c in pairs:
        at = slice(c * CHUNK, (c + 1) * CHUNK)
        beta, _, _, to_end = decay_parts(gt_ref[h, at, :], row, col)
        pseudo = dx(t_ref[h, c], beta * qkv_ref[at, (2 * h + 1) * DV : (2 * h + 2) * DV])
        ut_ref[h, c] = pseudo
        o_ref[at, h * DV : (h + 1) * DV] = dx(a_ref[h, c], pseudo)
        end_keys = to_end * qkv_ref[at, (4 * h + 1) * DK : (4 * h + 2) * DK]
        offsets[h, c] = dx(end_keys.T, pseudo)
    held = [state[h] for h in range(heads)]
    for c in range(group):
        for h in range(heads):
            s_ref[h, c] = held[h]
        held = [d3(m_ref[h, c], held[h]) + offsets[h, c] for h in range(heads)]
    for h in range(heads):
        state[h] = held[h]
        end_ref[h] = held[h]


def delta_values(qkv, gates, inverse, scores, steps):
    heads, tokens, _ = gates.shape
    count = tokens // CHUNK
    group = min(4, count)
    rows = group * CHUNK
    square = spec((heads, group, CHUNK, CHUNK), lambda g: (0, g, 0, 0))
    tall = spec((heads, group, CHUNK, DV), lambda g: (0, g, 0, 0))
    return pl.pallas_call(
        functools.partial(values_kernel, heads, group),
        grid=(count // group,),
        in_specs=[
            spec((rows, heads * 2 * DV), lambda g: (g, 0)),
            spec((heads, rows, GATE_LANES), lambda g: (0, g, 0)),
            square,
            square,
            square,
        ],
        out_specs=[
            tall,
            spec((rows, heads * DV), lambda g: (g, 0)),
            tall,
            spec((heads, DK, DV), lambda g: (0, 0, 0)),
        ],
        out_shape=[
            jax.ShapeDtypeStruct((heads, count, CHUNK, DV), F32),
            jax.ShapeDtypeStruct((tokens, heads * DV), F32),
            jax.ShapeDtypeStruct((heads, count, DK, DV), F32),
            jax.ShapeDtypeStruct((heads, DK, DV), F32),
        ],
        scratch_shapes=[pltpu.VMEM((heads, DK, DV), F32)],
        compiler_params=params(),
        cost_estimate=cost(heads * count * 12 * 2 * CHUNK**3 * 8, heads * count * CHUNK * 4000),
        name="delta_values",
    )(qkv, gates, inverse, scores, steps)


def output_kernel(
    heads, group, start_ref, s0_ref, tc_ref, p_ref, w_ref, ut_ref, o0_ref, gain_ref, *refs
):
    g_ref, mixed_ref, o_ref, s_ref, u_ref = refs
    for c in range(group):
        for h in range(heads):
            at = slice(c * CHUNK, (c + 1) * CHUNK)
            cols = slice(h * DV, (h + 1) * DV)
            held = s0_ref[h, c] + d3(tc_ref[h, c], start_ref[h])
            low = held
            s_ref[h, c] = low
            u_ref[h, c] = (ut_ref[h, c].astype(F32) - dx(w_ref[h, c], low))
            out = o0_ref[at, cols] + dx(p_ref[h, c], low)
            o_ref[at, cols] = out
            gate = g_ref[at, cols]
            inv = lax.rsqrt(jnp.mean(out * out, axis=-1, keepdims=True) + 1e-05)
            mixed = out * inv * gain_ref[h : h + 1, :] * (gate * jax.nn.sigmoid(gate))
            mixed_ref[at, cols] = mixed.astype(BF16)


def delta_output(start, states, trans, reach, wkeys, pseudo, local_out, raw, gain):
    heads, count = states.shape[:2]
    tokens = count * CHUNK
    group = min(2, count)
    rows = group * CHUNK
    square = spec((heads, group, CHUNK, CHUNK), lambda g: (0, g, 0, 0))
    tall = spec((heads, group, CHUNK, DV), lambda g: (0, g, 0, 0))
    flat = spec((rows, heads * DV), lambda g: (g, 0))
    low = jax.ShapeDtypeStruct((heads, count, CHUNK, DV), F32)
    return pl.pallas_call(
        functools.partial(output_kernel, heads, group),
        grid=(count // group,),
        in_specs=[
            spec((heads, DK, DV), lambda g: (0, 0, 0)),
            tall,
            square,
            square,
            square,
            tall,
            flat,
            spec((heads, DV), lambda g: (0, 0)),
        ]
        + [flat],
        out_specs=[flat, flat, tall, tall],
        out_shape=[
            jax.ShapeDtypeStruct((tokens, heads * DV), BF16),
            jax.ShapeDtypeStruct((tokens, heads * DV), F32),
            low,
            low,
        ],
        compiler_params=params(),
        cost_estimate=cost(heads * count * 10 * 2 * CHUNK**3 * 8, heads * count * CHUNK * 6000),
        name="delta_output",
    )(start, states, trans, reach, wkeys, pseudo, local_out, gain, raw)


def tail_kernel(
    heads, group, dm_ref, o_ref, gain_ref, pt_ref, mt_ref, *refs
):
    g_ref, do_ref, dg_ref, dgain_ref, ds_ref, dstart_ref, state = refs

    @pl.when(pl.program_id(0) == 0)
    def _():
        state[...] = jnp.zeros_like(state)
        dgain_ref[...] = jnp.zeros_like(dgain_ref)

    pushed = {}
    for c in range(group):
        for h in range(heads):
            at = slice(c * CHUNK, (c + 1) * CHUNK)
            cols = slice(h * DV, (h + 1) * DV)
            out = o_ref[at, cols]
            gate = g_ref[at, cols]
            back = dm_ref[at, cols]
            gain = gain_ref[h : h + 1, :]
            sig = jax.nn.sigmoid(gate)
            silu = gate * sig
            inv = lax.rsqrt(jnp.mean(out * out, axis=-1, keepdims=True) + 1e-05)
            hat = out * inv
            dgain_ref[h : h + 1, :] += jnp.sum(back * hat * silu, axis=0, keepdims=True)
            scaled = back * gain
            dg_ref[at, cols] = (scaled * hat * (sig * (1.0 + gate * (1.0 - sig)))).astype(BF16)
            dhat = scaled * silu
            dout = inv * (dhat - hat * jnp.mean(dhat * hat, axis=-1, keepdims=True))
            low = dout
            do_ref[at, cols] = low
            pushed[h, c] = dx(pt_ref[h, c], low)
    held = [state[h] for h in range(heads)]
    for c in reversed(range(group)):
        for h in range(heads):
            ds_ref[h, c] = held[h]
        held = [d3(mt_ref[h, c], held[h]) + pushed[h, c] for h in range(heads)]
    for h in range(heads):
        state[h] = held[h]
        dstart_ref[h] = held[h]


def delta_tail(grad_mixed, outs, raw, gain, reach_turned, steps_turned):
    heads, count = steps_turned.shape[:2]
    tokens = count * CHUNK
    group = min(2, count)
    rows = group * CHUNK
    last = count // group - 1
    square = spec((heads, group, CHUNK, CHUNK), lambda g: (0, last - g, 0, 0))
    tall = spec((heads, group, CHUNK, DV), lambda g: (0, last - g, 0, 0))
    flat = spec((rows, heads * DV), lambda g: (last - g, 0))
    return pl.pallas_call(
        functools.partial(tail_kernel, heads, group),
        grid=(count // group,),
        in_specs=[flat, flat, spec((heads, DV), lambda g: (0, 0)), square, square]
        + [flat],
        out_specs=[
            flat,
            flat,
            spec((heads, DV), lambda g: (0, 0)),
            tall,
            spec((heads, DK, DV), lambda g: (0, 0, 0)),
        ],
        out_shape=[
            jax.ShapeDtypeStruct((tokens, heads * DV), F32),
            jax.ShapeDtypeStruct((tokens, heads * DV), BF16),
            jax.ShapeDtypeStruct((heads, DV), F32),
            jax.ShapeDtypeStruct((heads, count, DK, DV), F32),
            jax.ShapeDtypeStruct((heads, DK, DV), F32),
        ],
        scratch_shapes=[pltpu.VMEM((heads, DK, DV), F32)],
        compiler_params=params(),
        cost_estimate=cost(heads * count * 10 * 2 * CHUNK**3 * 8, heads * count * CHUNK * 6000),
        name="delta_tail",
    )(grad_mixed, outs, gain, reach_turned, steps_turned, raw)


def early_kernel(heads, group, at_ref, u_ref, s_ref, do_ref, da_ref, dqd_ref, dua_ref):
    pairs = [(h, c) for c in range(group) for h in range(heads)]
    douts = {
        (h, c): do_ref[c * CHUNK : (c + 1) * CHUNK, h * DV : (h + 1) * DV] for h, c in pairs
    }
    for h, c in pairs:
        da_ref[h, c] = dx(douts[h, c], u_ref[h, c], NT)
    for h, c in pairs:
        dqd_ref[h, c] = dx(douts[h, c], s_ref[h, c], NT)
    for h, c in pairs:
        dua_ref[h, c] = dx(at_ref[h, c], douts[h, c])


def delta_early(scores_turned, u, s, dout):
    heads, count = u.shape[:2]
    group = min(2, count)
    square = spec((heads, group, CHUNK, CHUNK), lambda g: (0, g, 0, 0))
    tall = spec((heads, group, CHUNK, DV), lambda g: (0, g, 0, 0))
    return pl.pallas_call(
        functools.partial(early_kernel, heads, group),
        grid=(count // group,),
        in_specs=[square, tall, tall, spec((group * CHUNK, heads * DV), lambda g: (g, 0))],
        out_specs=[square, square, tall],
        out_shape=[
            jax.ShapeDtypeStruct((heads, count, CHUNK, CHUNK), F32),
            jax.ShapeDtypeStruct((heads, count, CHUNK, DK), F32),
            jax.ShapeDtypeStruct((heads, count, CHUNK, DV), F32),
        ],
        compiler_params=params(),
        cost_estimate=cost(heads * count * 30 * 2 * CHUNK**3, heads * count * CHUNK * 4000),
        name="delta_early",
    )(scores_turned, u, s, dout)


def grads_kernel(
    heads, group, end_ref, qkv_ref, gt_ref, tt_ref, a_ref, lk_ref, u_ref, s_ref,
    ds_ref, back_ref, da_ref, dqd_ref, dua_ref, dqkv_ref, dgt_ref,
):
    row, col = rows_cols()
    lane = lax.broadcasted_iota(jnp.int32, (CHUNK, GATE_LANES), 1)
    pairs = [(h, c) for c in range(group) for h in range(heads)]
    at = {(h, c): slice(c * CHUNK, (c + 1) * CHUNK) for h, c in pairs}
    parts = {(h, c): decay_parts(gt_ref[h, at[h, c], :], row, col) for h, c in pairs}
    keys = {(h, c): qkv_ref[at[h, c], (4 * h + 1) * DK : (4 * h + 2) * DK] for h, c in pairs}
    queries = {(h, c): qkv_ref[at[h, c], 4 * h * DK : (4 * h + 1) * DK] for h, c in pairs}
    vals = {(h, c): qkv_ref[at[h, c], (2 * h + 1) * DV : (2 * h + 2) * DV] for h, c in pairs}
    after = {(h, c): ds_ref[h, c] + d3(back_ref[h, c], end_ref[h]) for h, c in pairs}
    du = {
        (h, c): dua_ref[h, c] + dx(parts[h, c][3] * keys[h, c], after[h, c]) for h, c in pairs
    }
    x = {(h, c): dx(tt_ref[h, c], du[h, c]) for h, c in pairs}
    y = {(h, c): -dx(x[h, c], s_ref[h, c], NT) for h, c in pairs}
    da = {(h, c): da_ref[h, c] for h, c in pairs}
    dqd = {(h, c): dqd_ref[h, c] for h, c in pairs}
    dke = {(h, c): dx(u_ref[h, c], after[h, c], NT) for h, c in pairs}
    dl = {(h, c): dx(x[h, c], u_ref[h, c], NT) for h, c in pairs}
    for h, c in pairs:
        p = (h, c)
        beta, decays, carried, to_end = parts[p]
        key, query = keys[p], queries[p]
        kept = lk_ref[h, c].astype(F32)
        low_grad = jnp.where(row > col, -dl[p], 0.0)
        dg = jnp.sum(s_ref[h, c].astype(F32) * after[p], axis=0, keepdims=True)
        dg = jnp.sum(dg, axis=1, keepdims=True)
        yk = jnp.sum(y[p] * key, axis=-1, keepdims=True)
        dbeta = jnp.sum(x[p] * vals[p], axis=-1, keepdims=True) + carried * yk
        dbeta = dbeta + jnp.sum(low_grad * kept, axis=-1, keepdims=True)
        dcarried = beta * yk + jnp.sum(dqd[p] * query, axis=-1, keepdims=True)
        dend = jnp.sum(dke[p] * key, axis=-1, keepdims=True) * to_end
        scaled = low_grad * beta
        gram = scaled * decays
        score = da[p] * decays
        dqkv_ref[at[p], (2 * h + 1) * DV : (2 * h + 2) * DV] = beta * x[p]
        dqkv_ref[at[p], 4 * h * DK : (4 * h + 1) * DK] = carried * dqd[p] + dx(score, key)
        dqkv_ref[at[p], (4 * h + 1) * DK : (4 * h + 2) * DK] = (
            (beta * carried) * y[p]
            + to_end * dke[p]
            + dx(gram + gram.T, key)
            + dx(score.T, query)
        )
        spread = scaled * kept + da[p] * a_ref[h, c].astype(F32)
        dcum = jnp.sum(spread, axis=-1, keepdims=True)
        dcum = dcum - to_col(jnp.sum(spread, axis=0, keepdims=True), row, col)
        dcum = dcum - dend + dcarried * carried
        tail = jnp.sum(dend, axis=0, keepdims=True) + dg * carried[CHUNK - 1 : CHUNK]
        line = jnp.sum(jnp.where(row >= col, dcum, 0.0), axis=0, keepdims=True) + tail
        dlog = to_col(line, row, col)
        dgt_ref[h, at[p], :] = jnp.where(lane == 0, dlog, jnp.where(lane == 1, dbeta, 0.0))


def delta_grads(grad_end, qkv, gates, inv_turned, scores, kept, u, s, ds, back, early):
    heads, tokens, _ = gates.shape
    count = tokens // CHUNK
    group = min(2, count)
    rows = group * CHUNK
    square = spec((heads, group, CHUNK, CHUNK), lambda g: (0, g, 0, 0))
    tall = spec((heads, group, CHUNK, DV), lambda g: (0, g, 0, 0))
    gate_spec = spec((heads, rows, GATE_LANES), lambda g: (0, g, 0))
    wide = spec((rows, heads * 2 * DV), lambda g: (g, 0))
    return pl.pallas_call(
        functools.partial(grads_kernel, heads, group),
        grid=(count // group,),
        in_specs=[
            spec((heads, DK, DV), lambda g: (0, 0, 0)),
            wide,
            gate_spec,
            square,
            square,
            square,
            tall,
            tall,
            tall,
            square,
            square,
            square,
            tall,
        ],
        out_specs=[wide, gate_spec],
        out_shape=[
            jax.ShapeDtypeStruct((tokens, heads * 2 * DV), F32),
            jax.ShapeDtypeStruct((heads, tokens, GATE_LANES), F32),
        ],
        compiler_params=params(),
        cost_estimate=cost(heads * count * 30 * 2 * CHUNK**3 * 8, heads * count * CHUNK * 12000),
        name="delta_grads",
    )(grad_end, qkv, gates, inv_turned, scores, kept, u, s, ds, back, *early)


def front_act(x, rim, mask_ref, taps):
    extended = jnp.concatenate([rim, x], axis=0)
    conv = taps[0:1] * x
    for lag in range(1, 4):
        moved = pltpu.roll(extended, lag, 0)[8:]
        conv = conv + taps[lag : lag + 1] * (moved * mask_ref[:, 3 + lag : 4 + lag])
    return conv


def front_kernel(x_ref, rim_ref, mask_ref, taps_ref, y_ref, conv_ref):
    conv = front_act(x_ref[...], rim_ref[8:, :], mask_ref, taps_ref[...])
    conv_ref[...] = conv
    act = conv * jax.nn.sigmoid(conv)
    kind = pl.program_id(0) & 3

    @pl.when(kind < 2)
    def _():
        inv = lax.rsqrt(jnp.sum(act * act, axis=-1, keepdims=True) + 1e-06)
        y_ref[...] = act * (inv * jnp.where(kind == 0, DK**-0.5, 1.0))

    @pl.when(kind >= 2)
    def _():
        y_ref[...] = act


def front(raw, rim, masks, taps):
    tokens, cols = raw.shape[0], taps.shape[1]
    block = spec((tokens, DK), lambda c: (0, c))
    return pl.pallas_call(
        front_kernel,
        grid=(cols // DK,),
        in_specs=[
            spec((tokens, DK), lambda c: (0, c)),
            spec((16, DK), lambda c: (0, c)),
            spec((tokens, 8), lambda c: (0, 0)),
            spec((4, DK), lambda c: (0, c)),
        ],
        out_specs=[block, block],
        out_shape=[jax.ShapeDtypeStruct((tokens, cols), F32)] * 2,
        compiler_params=params(),
        cost_estimate=cost(tokens * cols * 40, tokens * cols * 8),
        name="front",
    )(raw, rim, masks, taps)


def conv_back(kind, conv, back):
    sig = jax.nn.sigmoid(conv)
    if kind < 2:
        act = conv * sig
        inv = lax.rsqrt(jnp.sum(act * act, axis=-1, keepdims=True) + 1e-06)
        unit = act * inv
        back = back * (DK**-0.5 if kind == 0 else 1.0)
        back = inv * (back - unit * jnp.sum(back * unit, axis=-1, keepdims=True))
    return back * (sig * (1.0 + conv * (1.0 - sig)))


def front_back_kernel(
    x_ref, rim_ref, conv_ref, mask_ref, taps_ref, dy_ref, dg_ref, dx_ref, edge_ref, dtaps_ref
):
    tokens = x_ref.shape[0]
    kind = lax.rem(pl.program_id(0), 6)

    @pl.when(kind >= 4)
    def _():
        grad = dg_ref[...]
        dx_ref[...] = grad
        edge_ref[...] = grad[tokens - 16 :].astype(F32)
        dtaps_ref[...] = jnp.zeros((4, DK), F32)

    def through(which):
        taps = taps_ref[...]
        x = x_ref[...]
        dconv = conv_back(which, conv_ref[...], dy_ref[...])
        extended = jnp.concatenate([rim_ref[8:, :], x], axis=0)
        zeros = jnp.zeros((8, DK), F32)
        total = taps[0:1] * dconv
        dtaps_ref[0:1, :] = jnp.sum(dconv * x, axis=0, keepdims=True)
        for lag in range(1, 4):
            part = jnp.concatenate([zeros, dconv * mask_ref[:, 3 + lag : 4 + lag]], axis=0)
            part = pltpu.roll(part, tokens + 8 - lag, 0)
            dtaps_ref[lag : lag + 1, :] = jnp.sum(part * extended, axis=0, keepdims=True)
            total = total + taps[lag : lag + 1] * part[8:]
        dx_ref[...] = total.astype(BF16)
        edge_ref[...] = total[tokens - 16 :]

    for which in range(3):

        @pl.when((kind == which) | ((which == 2) & (kind == 3)))
        def _():
            through(which)


def rim_back_kernel(heads, conv_ref, mask_ref, taps_ref, dy_ref, drim_ref):
    zeros = jnp.zeros((8, DK), F32)
    for h in range(heads):
        for kind in range(4):
            at = slice((4 * h + kind) * DK, (4 * h + kind + 1) * DK)
            taps = taps_ref[:, at]
            dconv = conv_back(kind, conv_ref[:, at], dy_ref[:, at])
            total = zeros
            for lag in range(1, 4):
                part = jnp.concatenate([zeros, dconv * mask_ref[:, 3 + lag : 4 + lag]], axis=0)
                total = total + taps[lag : lag + 1] * pltpu.roll(part, 16 - lag, 0)[:8]
            drim_ref[:, at] = total


def rim_back(conv, masks, taps, dqkv):
    cols = taps.shape[1]
    heads = cols // (4 * DK)
    return pl.pallas_call(
        functools.partial(rim_back_kernel, heads),
        out_shape=jax.ShapeDtypeStruct((8, cols), F32),
        compiler_params=params(),
        cost_estimate=cost(1000, 100000),
        name="rim_back",
    )(conv[:8], masks[:8], taps, dqkv[:8])


def act_block(c):
    return lax.div(c, 6) * 4 + jnp.minimum(lax.rem(c, 6), 3)


def gate_block(c):
    return lax.div(c, 6) * 2 + jnp.maximum(lax.rem(c, 6) - 4, 0)


def front_back(raw, rim, conv, masks, taps, dqkv, dg):
    tokens, cols = raw.shape[0], raw.shape[1] + dg.shape[1]
    block = spec((tokens, DK), lambda c: (0, c))
    act_spec = spec((tokens, DK), lambda c: (0, act_block(c)))
    return pl.pallas_call(
        front_back_kernel,
        grid=(cols // DK,),
        in_specs=[
            act_spec,
            spec((16, DK), lambda c: (0, act_block(c))),
            act_spec,
            spec((tokens, 8), lambda c: (0, 0)),
            spec((4, DK), lambda c: (0, act_block(c))),
            act_spec,
            spec((tokens, DK), lambda c: (0, gate_block(c))),
        ],
        out_specs=[
            block,
            spec((16, DK), lambda c: (0, c)),
            spec((4, DK), lambda c: (0, c)),
        ],
        out_shape=[
            jax.ShapeDtypeStruct((tokens, cols), BF16),
            jax.ShapeDtypeStruct((16, cols), F32),
            jax.ShapeDtypeStruct((4, cols), F32),
        ],
        compiler_params=params(),
        cost_estimate=cost(tokens * cols * 80, tokens * cols * 14),
        name="front_back",
    )(raw, rim, conv, masks, taps, dqkv, dg)


def flip(value, bit):
    count = lax.axis_size("mp")
    return lax.ppermute(value, "mp", [(i, i ^ (1 << bit)) for i in range(count)])


def bit_count():
    return lax.axis_size("mp").bit_length() - 1


def exchange(values, bits):
    values = lax.optimization_barrier(tuple(values))
    return lax.optimization_barrier(tuple(flip(v, b) for v, b in zip(values, bits)))


def gather_mp(share):
    bits = bit_count()
    half = share.shape[0] // 2
    orders = (list(range(bits - 1, 0, -1)), list(range(1, bits)))
    held = [share[w * half : (w + 1) * half][None] for w in range(2)]
    rels = [[0], [0]]
    for turn in range(bits - 1):
        now = [order[turn] for order in orders]
        got = exchange(held, now)
        held = [jnp.concatenate([h, g], axis=0) for h, g in zip(held, got)]
        rels = [rel + [r | (1 << bit) for r in rel] for rel, bit in zip(rels, now)]
    got = exchange(held, [0, 0])
    return [(h, g, rel) for h, g, rel in zip(held, got, rels)]


def gathered_specs(found, tile, tiles):
    specs = []
    for which, (held, other, rel) in enumerate(found):
        shape = (held.shape[0], tile, held.shape[2])
        if which == 0:
            index = lambda i, m: (0, jnp.minimum(i, tiles - 1), 0)
        else:
            index = lambda i, m: (0, jnp.maximum(i - tiles, 0), 0)
        specs += [spec(shape, index)] * 2
    return specs


def gathered_args(found):
    return [x for held, other, rel in found for x in (held, other)]


def gathered_blocks(found, refs, which):
    held, other = refs[2 * which], refs[2 * which + 1]
    rel = found[which][2]
    blocks = [(r, held[i].astype(F32)) for i, r in enumerate(rel)]
    return blocks + [(r | 1, other[i].astype(F32)) for i, r in enumerate(rel)]


def place(mp_ref, r, cols):
    return pl.ds(pl.multiple_of((mp_ref[0] ^ r) * cols, cols), cols)


def norm_kernel(rels, cols, tiles, mode, *refs):
    mp_ref, refs = refs[0], refs[1:]
    found = [(None, None, rel) for rel in rels]
    if mode == "plain":
        out_ref = refs[4]
    else:
        gain_ref, out_ref, inv_ref = refs[4:7]
    for which in range(2):

        @pl.when((pl.program_id(0) < tiles) == (which == 0))
        def _():
            blocks = gathered_blocks(found, refs, which)
            if mode == "plain":
                for r, x in blocks:
                    out_ref[:, place(mp_ref, r, cols)] = x.astype(BF16)
                return
            total = sum(jnp.sum(x * x, axis=-1, keepdims=True) for _, x in blocks)
            inv = lax.rsqrt(total * (1.0 / (cols * len(blocks))) + 1e-05)
            for r, x in blocks:
                at = place(mp_ref, r, cols)
                out_ref[:, at] = (x * inv * gain_ref[:, at]).astype(BF16)
            inv_ref[...] = jnp.broadcast_to(inv, inv_ref.shape)


def assemble(found, mp_pos, gain=None):
    half, cols = found[0][0].shape[1:]
    rels = [f[2] for f in found]
    width = cols * 2 * len(rels[0])
    tokens = 2 * half
    tile = min(256, half)
    tiles = half // tile
    mode = "plain" if gain is None else "norm"
    row_spec = spec((tile, width), lambda i, m: (i, 0))
    in_specs = gathered_specs(found, tile, tiles)
    out_specs = [row_spec]
    out_shape = [jax.ShapeDtypeStruct((tokens, width), BF16)]
    args = gathered_args(found)
    if gain is not None:
        in_specs.append(spec((1, width), lambda i, m: (0, 0)))
        args.append(gain.reshape(1, width))
        out_specs.append(spec((tile, 128), lambda i, m: (i, 0)))
        out_shape.append(jax.ShapeDtypeStruct((tokens, 128), F32))
    return pl.pallas_call(
        functools.partial(norm_kernel, rels, cols, tiles, mode),
        grid_spec=pltpu.PrefetchScalarGridSpec(
            num_scalar_prefetch=1,
            grid=(2 * tiles,),
            in_specs=in_specs,
            out_specs=out_specs,
        ),
        out_shape=out_shape,
        compiler_params=params(),
        cost_estimate=cost(tokens * width * 10, tokens * width * 4),
        name="assemble",
    )(mp_pos.reshape(1).astype(jnp.int32), *args)


def norm_back_kernel(rels, cols, tiles, *refs):
    mp_ref, refs = refs[0], refs[1:]
    found = [(None, None, rel) for rel in rels]
    grads, mids = refs[:4], refs[4:8]
    up_ref, gain_ref, own_grad_ref, own_mid_ref, out_ref, own_out_ref, dgain_ref = refs[8:]

    @pl.when(pl.program_id(0) == 0)
    def _():
        dgain_ref[...] = jnp.zeros_like(dgain_ref)

    for which in range(2):

        @pl.when((pl.program_id(0) < tiles) == (which == 0))
        def _():
            grad = gathered_blocks(found, grads, which)
            mid = gathered_blocks(found, mids, which)
            scale = 1.0 / (cols * len(grad))
            total = sum(jnp.sum(x * x, axis=-1, keepdims=True) for _, x in mid)
            inv = lax.rsqrt(total * scale + 1e-05)
            scaled = [(r, g * gain_ref[:, place(mp_ref, r, cols)]) for r, g in grad]
            mean = sum(
                jnp.sum(g * x, axis=-1, keepdims=True) for (_, g), (_, x) in zip(scaled, mid)
            )
            shrink = inv * inv * (mean * scale)
            for (r, g), (_, x) in zip(scaled, mid):
                at = place(mp_ref, r, cols)
                out_ref[:, at] = (up_ref[:, at].astype(F32) + inv * (g - x * shrink)).astype(BF16)
            at = place(mp_ref, 0, cols)
            own_grad, own_mid = own_grad_ref[...], own_mid_ref[...]
            own_out_ref[...] = up_ref[:, at].astype(F32) + inv * (
                own_grad * gain_ref[:, at] - own_mid * shrink
            )
            dgain_ref[...] += jnp.sum(own_grad * own_mid * inv, axis=0, keepdims=True)


def norm_back(found_grad, found_mid, full_grad, gain, own_grad, own_mid, mp_pos):
    half, cols = found_grad[0][0].shape[1:]
    rels = [f[2] for f in found_grad]
    tokens, width = full_grad.shape
    tile = min(256, half)
    tiles = half // tile
    row_spec = spec((tile, width), lambda i, m: (i, 0))
    own_spec = spec((tile, cols), lambda i, m: (i, 0))
    return pl.pallas_call(
        functools.partial(norm_back_kernel, rels, cols, tiles),
        grid_spec=pltpu.PrefetchScalarGridSpec(
            num_scalar_prefetch=1,
            grid=(2 * tiles,),
            in_specs=gathered_specs(found_grad, tile, tiles)
            + gathered_specs(found_mid, tile, tiles)
            + [row_spec, spec((1, width), lambda i, m: (0, 0)), own_spec, own_spec],
            out_specs=[row_spec, own_spec, spec((1, cols), lambda i, m: (0, 0))],
        ),
        out_shape=[
            jax.ShapeDtypeStruct((tokens, width), BF16),
            jax.ShapeDtypeStruct((tokens, cols), F32),
            jax.ShapeDtypeStruct((1, cols), F32),
        ],
        compiler_params=params(),
        cost_estimate=cost(tokens * width * 20, tokens * width * 8),
        name="norm_back",
    )(
        mp_pos.reshape(1).astype(jnp.int32),
        *gathered_args(found_grad),
        *gathered_args(found_mid),
        full_grad,
        gain.reshape(1, width),
        own_grad,
        own_mid,
    )


def block_kernel(terms, mp_ref, *refs):
    out_ref = refs[2 * terms]
    total = None
    for i in range(terms):
        part = d1(refs[2 * i][...], refs[2 * i + 1][...], NT)
        total = part if total is None else total + part
    out_ref[0] = total.astype(out_ref.dtype)


def left_index(start, g, m):
    return (0, start)


def right_index(parity, cols, rows, start, g, m):
    at = ((2 * g + parity) ^ m[0]) * cols
    if rows:
        at = at + lax.div(at, rows) * 16
    return (pl.multiple_of(at, 16), start)


def block_products(terms, mp_pos, cols, parity):
    tokens = terms[0][0].shape[0]
    count = lax.axis_size("mp") // 2
    in_specs, args, flops = [], [], 0
    for left, left_start, right, right_start, depth, rows in terms:
        in_specs.append(
            pl.BlockSpec(
                (pl.Element(tokens), pl.Element(depth)), functools.partial(left_index, left_start)
            )
        )
        index = functools.partial(right_index, parity, cols, rows, right_start)
        in_specs.append(pl.BlockSpec((pl.Element(cols), pl.Element(depth)), index))
        args += [left, right]
        flops += 2 * tokens * depth * cols * count
    return pl.pallas_call(
        functools.partial(block_kernel, len(terms)),
        grid_spec=pltpu.PrefetchScalarGridSpec(
            num_scalar_prefetch=1,
            grid=(count,),
            in_specs=in_specs,
            out_specs=spec((1, tokens, cols), lambda g, m: (g, 0, 0)),
        ),
        out_shape=jax.ShapeDtypeStruct((count, tokens, cols), BF16 if parity else F32),
        compiler_params=params(),
        cost_estimate=cost(flops, tokens * cols * count * 4),
        name="block_products",
    )(mp_pos.reshape(1).astype(jnp.int32), *args)


def reduce_mp(terms, mp_pos, cols):
    sent = flip(block_products(terms, mp_pos, cols, 1), 0)
    kept = block_products(terms, mp_pos, cols, 0)
    bits = bit_count()
    half = kept.shape[1] // 2
    orders = (list(range(1, bits)), list(range(bits - 1, 0, -1)))
    rels = [[2 * i for i in range(kept.shape[0])] for _ in orders]
    helds = []
    for which in range(2):
        at = slice(which * half, (which + 1) * half)
        helds.append({r: kept[i, at] + sent[i, at].astype(F32) for i, r in enumerate(rels[which])})
    for turn in range(bits - 1):
        aways = [[r for r in rels[w] if (r >> orders[w][turn]) & 1] for w in range(2)]
        gots = exchange(
            [jnp.stack([helds[w][r].astype(BF16) for r in aways[w]]) for w in range(2)],
            [orders[w][turn] for w in range(2)],
        )
        for w in range(2):
            bit = orders[w][turn]
            rels[w] = [r for r in rels[w] if not (r >> bit) & 1]
            helds[w] = {
                r: helds[w][r] + gots[w][aways[w].index(r | (1 << bit))].astype(F32) for r in rels[w]
            }
    return jnp.concatenate([helds[0][0], helds[1][0]], axis=0), kept


def sum_mp(value):
    for bit in range(bit_count()):
        value = value + flip(value, bit)
    return value


def sum_seq(value):
    count = lax.axis_size("seq")
    total = value
    for step in range(1, count):
        total = total + lax.ppermute(value, "seq", [(i, (i + step) % count) for i in range(count)])
    return total


def shifted(value, steps):
    count = lax.axis_size("seq")
    first, last = max(0, -steps), min(count, count - steps)
    return lax.ppermute(value, "seq", [(i, i + steps) for i in range(first, last)])


def batched(left, right):
    return jnp.einsum("hde,hev->hdv", left, right, precision=lax.Precision.HIGHEST)


def dot(left, right, dims=NN):
    return lax.dot_general(left, right, dims, preferred_element_type=F32)


TN = (((0,), (0,)), ((), ()))


def first_kernel(
    heads, count, rows, x_ref, rim_ref, w_ref, mask_ref, scale_ref, bias_ref,
    raw_ref, pre_ref, gate_ref, rim_raw_ref,
):
    @pl.when(pl.program_id(0) == 0)
    def _():
        total = None
        for s in range(count):
            at = s * (rows + 16)
            part = d1(rim_ref[:, s * rows : (s + 1) * rows], w_ref[at : at + rows, :])
            total = part if total is None else total + part
        rim_raw_ref[...] = total

    raw, pre = None, None
    for s in range(count):
        at = s * (rows + 16)
        part = x_ref[:, s * rows : (s + 1) * rows]
        left = d1(part, w_ref[at : at + rows, :])
        right = d1(part, w_ref[at + rows : at + rows + 16, :rows], NT)
        raw = left if raw is None else raw + left
        pre = right if pre is None else pre + right
    raw_ref[...] = raw
    pre_ref[...] = pre
    masks = mask_ref[...]
    lane = lax.broadcasted_iota(jnp.int32, masks.shape, 1)
    for h in range(heads):
        x = pre[:, 2 * h : 2 * h + 1] + bias_ref[h]
        soft = jnp.maximum(x, 0.0) + jnp.log1p(jnp.exp(-jnp.abs(x)))
        beta = jax.nn.sigmoid(pre[:, 2 * h + 1 : 2 * h + 2])
        gate_ref[h] = jnp.where(
            lane == 0, -scale_ref[h] * soft, jnp.where(lane == 1, beta, masks)
        )


def project_first(normed, rim, mixer, masks, scale, bias):
    tokens, width = normed.shape
    count = lax.axis_size("seq")
    rows, cols = mixer.shape[0] // count - 16, mixer.shape[1]
    heads = scale.shape[0]
    tile = 256
    scalar = pl.BlockSpec(memory_space=pltpu.SMEM)
    return pl.pallas_call(
        functools.partial(first_kernel, heads, count, rows),
        grid=(tokens // tile,),
        in_specs=[
            spec((tile, width), lambda i: (i, 0)),
            spec((16, width), lambda i: (0, 0)),
            spec(mixer.shape, lambda i: (0, 0)),
            spec((tile, 8), lambda i: (i, 0)),
            scalar,
            scalar,
        ],
        out_specs=[
            spec((tile, cols), lambda i: (i, 0)),
            spec((tile, 16), lambda i: (i, 0)),
            spec((heads, tile, 8), lambda i: (0, i, 0)),
            spec((16, cols), lambda i: (0, 0)),
        ],
        out_shape=[
            jax.ShapeDtypeStruct((tokens, cols), F32),
            jax.ShapeDtypeStruct((tokens, 16), F32),
            jax.ShapeDtypeStruct((heads, tokens, 8), F32),
            jax.ShapeDtypeStruct((16, cols), F32),
        ],
        compiler_params=params(),
        cost_estimate=cost(2 * tokens * width * cols, tokens * width * 2 + width * cols * 2),
        name="project_first",
    )(normed, rim, mixer, masks, scale, bias)


def gates_back_kernel(heads, pre_ref, dg_ref, scale_ref, bias_ref, low_ref, sums_ref):
    pre = pre_ref[...]
    lane = lax.broadcasted_iota(jnp.int32, pre.shape, 1)
    line = lax.broadcasted_iota(jnp.int32, (1, 128), 1)
    low = jnp.zeros(pre.shape, F32)
    for h in range(heads):
        x = pre[:, 2 * h : 2 * h + 1] + bias_ref[h]
        soft = jnp.maximum(x, 0.0) + jnp.log1p(jnp.exp(-jnp.abs(x)))
        beta = jax.nn.sigmoid(pre[:, 2 * h + 1 : 2 * h + 2])
        dlog = dg_ref[h][:, 0:1]
        dx = dlog * (-scale_ref[h] * jax.nn.sigmoid(x))
        db = dg_ref[h][:, 1:2] * (beta * (1.0 - beta))
        low = jnp.where(lane == 2 * h, dx, jnp.where(lane == 2 * h + 1, db, low))
        dscale = jnp.sum(-dlog * soft, axis=0, keepdims=True)
        dbias = jnp.sum(dx, axis=0, keepdims=True)
        sums_ref[h : h + 1, :] = jnp.where(line == 0, dscale, jnp.where(line == 1, dbias, 0.0))
    low_ref[...] = low.astype(BF16)


def gates_back(pre, dgates, scale, bias):
    tokens = pre.shape[0]
    heads = scale.shape[0]
    scalar = pl.BlockSpec(memory_space=pltpu.SMEM)
    whole = pl.BlockSpec(memory_space=pltpu.VMEM)
    return pl.pallas_call(
        functools.partial(gates_back_kernel, heads),
        in_specs=[whole, whole, scalar, scalar],
        out_specs=[whole, whole],
        out_shape=[
            jax.ShapeDtypeStruct((tokens, 16), BF16),
            jax.ShapeDtypeStruct((heads, 128), F32),
        ],
        compiler_params=params(),
        cost_estimate=cost(tokens * 1000, tokens * 1024),
        name="gates_back",
    )(pre, dgates, scale, bias)


def unpack(value, units):
    whole = units // 128 * 128
    rest = value[:, 2 * whole :]
    tail = units - whole
    gate = jnp.concatenate([value[:, :whole], rest[:, :tail]], axis=1)
    return gate, jnp.concatenate([value[:, whole : 2 * whole], rest[:, tail:]], axis=1)


def pack(gate, up):
    whole = gate.shape[1] // 128 * 128
    return jnp.concatenate(
        [gate[:, :whole], up[:, :whole], gate[:, whole:], up[:, whole:]], axis=1
    )


def ffn_kernel(units, x_ref, back_ref, gu_ref, hid_ref, dgu_ref):
    gate, up = unpack(d1(x_ref[...], gu_ref[...]), units)
    back = back_ref[...]
    sig = jax.nn.sigmoid(gate)
    silu = gate * sig
    hid_ref[...] = (silu * up).astype(BF16)
    dgu_ref[...] = pack(
        (back * up * sig * (1.0 + gate * (1.0 - sig))), (back * silu)
    ).astype(BF16)


def ffn(normed2, grad_hidden, gu_full):
    tokens, width = normed2.shape
    units = grad_hidden.shape[1]
    tile = 256
    row_spec = spec((tile, width), lambda i: (i, 0))
    return pl.pallas_call(
        functools.partial(ffn_kernel, units),
        grid=(tokens // tile,),
        in_specs=[
            row_spec,
            spec((tile, units), lambda i: (i, 0)),
            spec((width, 2 * units), lambda i: (0, 0)),
        ],
        out_specs=[
            spec((tile, units), lambda i: (i, 0)),
            spec((tile, 2 * units), lambda i: (i, 0)),
        ],
        out_shape=[
            jax.ShapeDtypeStruct((tokens, units), BF16),
            jax.ShapeDtypeStruct((tokens, 2 * units), BF16),
        ],
        compiler_params=params(),
        cost_estimate=cost(6 * tokens * width * units, tokens * width * 4 + width * units * 6),
        name="ffn",
    )(normed2, grad_hidden, gu_full)


def after(value, *earlier):
    return lax.optimization_barrier((value, earlier))[0]


def together(*values):
    return lax.optimization_barrier(values)


def chain(steps, ends, sign):
    total = shifted(ends.astype(BF16), sign).astype(F32)
    for _ in range(lax.axis_size("seq") - 2):
        total = shifted((batched(steps, total) + ends).astype(BF16), sign).astype(F32)
    return total


def scatter_seq(value, axis):
    return lax.psum_scatter(value, "seq", scatter_dimension=axis, tiled=True).astype(F32)


def shards(
    residual,
    attn_gain,
    w_mixer,
    w_gates,
    conv_taps,
    decay_scale,
    dt_bias,
    head_gain,
    w_out,
    ffn_gain,
    w_gate,
    w_up,
    w_down,
    out_grad,
    doc_ids,
):
    tokens, cols = residual.shape
    seq_count = lax.axis_size("seq")
    mp_count = lax.axis_size("mp")
    seq_pos = lax.axis_index("seq")
    mp_pos = lax.axis_index("mp")
    rows, heads = w_mixer.shape[:2]
    width = rows * seq_count

    padded = jnp.concatenate([jnp.full((3,), -1, jnp.int32), doc_ids])
    window = lax.dynamic_slice_in_dim(padded, seq_pos * tokens, tokens + 3)
    ids = window[3:]
    prior = jnp.repeat(window[2 : 2 + tokens].reshape(-1, CHUNK)[:, 0], CHUNK)
    same = [(window[3 - j : 3 - j + tokens] == ids).astype(F32) for j in range(1, 4)]
    ids_f, prior_f = ids.astype(F32), prior.astype(F32)
    zero = jnp.zeros((tokens,), F32)
    masks = jnp.stack([zero] * 2 + [ids_f, prior_f] + same + [zero], axis=1)

    units = w_gate.shape[1]
    feats = w_out.shape[0]
    act_cols, gate_cols = heads * 2 * DV, heads * DV
    gate_part = jnp.pad(
        w_gates.reshape(rows, 2 * heads).T, ((0, 16 - 2 * heads), (0, act_cols - rows))
    )
    act_part = w_mixer[:, :, : 2 * DV].reshape(rows, act_cols)
    act_full = lax.all_gather(
        jnp.concatenate([act_part, gate_part]), "seq", axis=0, tiled=True
    )
    found_res = gather_mp(residual)
    god_part = jnp.concatenate(
        [w_mixer[:, :, 2 * DV :].reshape(rows, gate_cols), w_out.T, w_down.T], axis=1
    )
    god_full = lax.all_gather(after(god_part, found_res[0][0]), "seq", axis=0, tiled=True)
    gu_part = pack(w_gate, w_up)

    normed, inv1 = assemble(found_res, mp_pos, attn_gain)
    rim_normed = shifted(normed[tokens - 16 :], 1)
    found_og = gather_mp(after(out_grad, normed))
    full_grad = assemble(found_og, mp_pos)[0]
    act_full = after(act_full, full_grad)
    raw, gate_pre, gates, rim = project_first(
        normed, rim_normed, act_full, masks, decay_scale, dt_bias
    )
    gu_full = lax.all_gather(after(gu_part, raw), "seq", axis=0, tiled=True)
    taps = conv_taps.reshape(4, act_cols)
    qkv, conv = front(raw, rim, masks, taps)

    inverse, inv_turned, scores, scores_turned, kept, wkeys, reach, reach_turned, steps, steps_turned = (
        delta_prep(qkv, gates)
    )
    trans, back = delta_trans(steps, steps_turned)
    pseudo, local_out, states, state_end = delta_values(qkv, gates, inverse, scores, steps)
    start = chain(trans[:, -1], state_end, 1)
    god_full = after(god_full, state_end)
    raw_gate = dot(normed, god_full[:, :gate_cols])
    out_turned = god_full[:, gate_cols : gate_cols + feats]
    down_turned = god_full[:, gate_cols + feats :]
    gates_full = jnp.swapaxes(
        act_full.reshape(seq_count, rows + 16, act_cols)[:, rows:, :rows], 0, 1
    ).reshape(16, width).T
    mixed, outs, held, corrected = delta_output(
        start, states, trans, reach, wkeys, pseudo, local_out, raw_gate, head_gain
    )

    mixed, out_turned, down_turned, gates_full = together(
        mixed, out_turned, down_turned, gates_full
    )
    branch, _ = reduce_mp([(mixed, 0, god_full, gate_cols, feats, 0)], mp_pos, cols)
    middle = residual.astype(F32) + branch
    found_mid = gather_mp(middle.astype(BF16))
    normed2, _ = assemble(found_mid, mp_pos, ffn_gain)
    grad_hidden = dot(full_grad, after(down_turned, branch))
    gu_full = after(gu_full, grad_hidden, normed2)
    hidden, grad_gu = ffn(normed2, grad_hidden, gu_full)
    part_gu = dot(normed2, grad_gu, TN).astype(BF16)
    grad_gu = after(grad_gu, part_gu)
    grad_normed2, kept_gn2 = reduce_mp(
        [(grad_gu, 0, gu_full, 0, 2 * units, 0)], mp_pos, cols
    )
    dw_gu = lax.psum_scatter(part_gu, "seq", scatter_dimension=0, tiled=True)
    part_down = dot(after(hidden, kept_gn2), full_grad, TN).astype(BF16)
    found_gn2 = gather_mp(grad_normed2.astype(BF16))

    grad_branch, grad_middle, dffn_gain = norm_back(
        found_gn2, found_mid, full_grad, ffn_gain, grad_normed2, middle, mp_pos
    )
    grad_mixed = dot(grad_branch, out_turned)

    dout, dg_raw, dhead_gain, dstates, dstart = delta_tail(
        grad_mixed, outs, raw_gate, head_gain, reach_turned, steps_turned
    )
    part_out = dot(mixed, after(grad_branch, dstart), TN).astype(BF16)
    part_do = jnp.concatenate([part_out, part_down])
    dw_do = lax.psum_scatter(part_do, "seq", scatter_dimension=1, tiled=True)
    early = delta_early(scores_turned, corrected, held, after(dout, dstart))
    grad_end = chain(back[:, 0], dstart, -1)
    grad_end = after(grad_end, part_do, early)
    dqkv, dgates = delta_grads(
        grad_end, qkv, gates, inv_turned, scores, kept, corrected, held, dstates, back[:, 1:],
        early,
    )
    drim = rim_back(conv, masks, taps, dqkv)
    came = shifted(drim, -1)
    dproj, edge, dtaps = front_back(raw, rim, conv, masks, taps, after(dqkv, drim), dg_raw)
    came = jnp.pad(came.reshape(8, heads, 2 * DV), ((0, 0), (0, 0), (0, DV))).reshape(8, -1)
    edge = jnp.concatenate([edge[:8], edge[8:] + came])
    dproj = lax.dynamic_update_slice_in_dim(dproj, edge.astype(BF16), tokens - 16, 0)
    dgate_low, gate_sums = gates_back(gate_pre, dgates, decay_scale, dt_bias)

    part_mixer = dot(normed, dproj, TN).astype(BF16)
    dw_mixer = lax.psum_scatter(part_mixer, "seq", scatter_dimension=0, tiled=True)
    dproj, dgate_low = after((dproj, dgate_low), part_mixer)
    part_gates = dot(dgate_low, normed, TN)
    terms = [(dgate_low, 0, gates_full, 0, 16, 0)]
    for h in range(heads):
        terms.append((dproj, 3 * h * DV, act_full, 2 * h * DV, 2 * DV, rows))
        terms.append((dproj, (3 * h + 2) * DV, god_full, h * DV, DV, 0))
    grad_normed, kept_gn = reduce_mp(terms, mp_pos, cols)
    ffn_part, _ = reduce_mp(
        [(after(hidden, kept_gn), 0, down_turned, 0, units, 0)], mp_pos, cols
    )
    output = (middle + ffn_part).astype(BF16)
    own_gain = lax.dynamic_slice_in_dim(attn_gain, mp_pos * cols, cols)
    own_res = residual.astype(F32)
    inv1 = inv1[:, :1]
    scaled = grad_normed * own_gain
    mean = jnp.sum(scaled * own_res, axis=-1).reshape(-1, 128)
    mean = sum_mp(mean).reshape(tokens, 1) * (1.0 / width)
    grad_residual = grad_middle + inv1 * (scaled - own_res * (inv1 * inv1 * mean))
    dattn_gain = jnp.sum(grad_normed * own_res * inv1, axis=0)

    dw_gate, dw_up = unpack(dw_gu, units)

    dtaps = dtaps.reshape(4, heads, 2 * DK + 2 * DV)[:, :, : 2 * DK + DV]
    small = [
        dattn_gain, dffn_gain, dhead_gain, gate_sums[:, 0], gate_sums[:, 1], dtaps,
        part_gates[: 2 * heads],
    ]
    packed = jnp.concatenate([value.reshape(-1) for value in small])
    packed = jnp.pad(packed, (0, -packed.shape[0] % 1024)).reshape(-1, 128)
    packed = sum_seq(packed).reshape(-1)
    sums, at = [], 0
    for value in small:
        sums.append(packed[at : at + value.size].reshape(value.shape))
        at += value.size
    gains = jnp.stack([sums[0], sums[1].reshape(-1)])
    gains = lax.dynamic_update_slice(jnp.zeros((2, width), F32), gains, (0, mp_pos * cols))
    gains = sum_mp(gains)
    dw_gates = lax.dynamic_slice_in_dim(sums[6], seq_pos * rows, rows, 1)
    return (
        output,
        grad_residual,
        gains[0],
        dw_mixer.astype(F32).reshape(rows, heads, 2 * DK + 2 * DV),
        dw_gates.T.reshape(rows, heads, 2),
        sums[5],
        sums[3],
        sums[4],
        sums[2],
        dw_do[: w_out.shape[0]].astype(F32),
        gains[1],
        dw_gate.astype(F32),
        dw_up.astype(F32),
        dw_do[w_out.shape[0] :].astype(F32),
    )


def solution(mesh):
    in_specs = (
        P("seq", "mp"),
        P(),
        P("seq", "mp", None),
        P("seq", "mp", None),
        P(None, "mp", None),
        P("mp"),
        P("mp"),
        P("mp", None),
        P("mp", "seq"),
        P(),
        P("seq", "mp"),
        P("seq", "mp"),
        P("mp", "seq"),
        P("seq", "mp"),
        P(),
    )
    out_specs = (
        P("seq", "mp"),
        P("seq", "mp"),
        P(),
        P("seq", "mp", None),
        P("seq", "mp", None),
        P(None, "mp", None),
        P("mp"),
        P("mp"),
        P("mp", None),
        P("mp", "seq"),
        P(),
        P("seq", "mp"),
        P("seq", "mp"),
        P("mp", "seq"),
    )
    return jax.shard_map(shards, mesh=mesh, in_specs=in_specs, out_specs=out_specs, check_vma=False)
```

```python
import functools
import jax
import jax.numpy as jnp
from jax import lax
from jax.experimental import pallas as pl
from jax.experimental.pallas import tpu as pltpu
from jax.sharding import PartitionSpec as P

DK = 128
DV = 256
CHUNK = 128
GATE_LANES = 8
F32 = jnp.float32
BF16 = jnp.bfloat16
NN = (((1,), (0,)), ((), ()))
NT = (((1,), (1,)), ((), ()))
VMEM_LIMIT = 48 * 1024 * 1024


def d1(left, right, dims=NN):
    return lax.dot_general(
        left.astype(BF16), right.astype(BF16), dims, preferred_element_type=F32
    )


def dx(left, right, dims=NN):
    if left.dtype == BF16 and right.dtype == BF16:
        return d1(left, right, dims)
    return d3(left.astype(F32), right.astype(F32), dims)


def split(value):
    high = value.astype(BF16)
    return high, (value - high.astype(F32)).astype(BF16)


def d3(left, right, dims=NN):
    lh, ll = split(left)
    rh, rl = split(right)
    return d1(lh, rh, dims) + (d1(lh, rl, dims) + d1(ll, rh, dims))


def params():
    return pltpu.CompilerParams(vmem_limit_bytes=VMEM_LIMIT)


def cost(flops, nbytes):
    return pl.CostEstimate(flops=int(flops) // 100, bytes_accessed=int(nbytes) // 100, transcendentals=0)


def spec(shape, index_map):
    return pl.BlockSpec(shape, index_map)


def rows_cols():
    row = lax.broadcasted_iota(jnp.int32, (CHUNK, CHUNK), 0)
    col = lax.broadcasted_iota(jnp.int32, (CHUNK, CHUNK), 1)
    return row, col


def to_row(column, row, col):
    return jnp.sum(jnp.where(row == col, column, 0.0), axis=0, keepdims=True)


def to_col(line, row, col):
    return jnp.sum(jnp.where(row == col, line, 0.0), axis=1, keepdims=True)


def decay_parts(gates, row, col):
    log_decay, beta, ids, prior = (gates[:, i : i + 1] for i in range(4))
    cum_row = jnp.sum(jnp.where(row <= col, log_decay, 0.0), axis=0, keepdims=True)
    cum_col = to_col(cum_row, row, col)
    same = ids == to_row(ids, row, col)
    inside = (row >= col) & same
    decays = jnp.where(inside, jnp.exp(jnp.where(inside, cum_col - cum_row, 0.0)), 0.0)
    carried = jnp.where(ids == prior, jnp.exp(cum_col), 0.0)
    last_ids = ids[CHUNK - 1 : CHUNK]
    last_cum = cum_col[CHUNK - 1 : CHUNK]
    to_end = jnp.where(ids == last_ids, jnp.exp(last_cum - cum_col), 0.0)
    return beta, decays, carried, to_end


def invert(lowers, row, col):
    eye = jnp.where(row == col, 1.0, 0.0)
    found = None
    shift = 0
    while (1 << shift) < CHUNK:
        mask = ((row >> (shift + 1)) == (col >> (shift + 1))) & (
            (row >> shift) > (col >> shift)
        )
        masked = [jnp.where(mask, lower, 0.0) for lower in lowers]
        if found is None:
            found = [eye - m for m in masked]
        else:
            low = [x.astype(BF16) for x in found]
            inner = [d1(m, x) for m, x in zip(masked, low)]
            outer = [d1(x, y) for x, y in zip(low, inner)]
            found = [x - y for x, y in zip(found, outer)]
        shift += 1
    rest = [d3(lower, x) for lower, x in zip(lowers, found)]
    rest = [(eye - x) - r for x, r in zip(found, rest)]
    return [x + d1(x, r) for x, r in zip(found, rest)]


def prep_kernel(
    group, qk_ref, gt_ref, t_ref, tt_ref, a_ref, at_ref, lk_ref, w_ref, p_ref, pt_ref, m_ref, mt_ref
):
    row, col = rows_cols()
    queries, keys, parts = [], [], []
    for c in range(group):
        block = qk_ref[c * CHUNK : (c + 1) * CHUNK, :]
        queries.append(block[:, :DK])
        keys.append(block[:, DK:])
        parts.append(decay_parts(gt_ref[0, c * CHUNK : (c + 1) * CHUNK, :], row, col))
    gram = [d3(k, k, NT) for k in keys]
    scores = [dx(q, k, NT) for q, k in zip(queries, keys)]
    kept = [jnp.where(row > col, p[1] * g, 0.0) for p, g in zip(parts, gram)]
    lowers = [x * p[0] for x, p in zip(kept, parts)]
    inverses = invert(lowers, row, col)
    eye = jnp.where(row == col, 1.0, 0.0)
    for c in range(group):
        beta, decays, carried, to_end = parts[c]
        inverse = inverses[c]
        t_ref[0, c] = inverse
        tt_ref[0, c] = inverses[c].T
        score = decays * scores[c]
        a_ref[0, c] = score
        at_ref[0, c] = score.T
        lk_ref[0, c] = kept[c]
        wkeys = dx(inverse, (beta * carried) * keys[c])
        w_ref[0, c] = wkeys
        reach = carried * queries[c] - dx(score, wkeys)
        p_ref[0, c] = reach
        pt_ref[0, c] = reach.T
        end_keys = to_end * keys[c]
        step = carried[CHUNK - 1 : CHUNK] * eye - dx(end_keys.T, wkeys)
        m_ref[0, c] = step
        mt_ref[0, c] = step.T


def delta_prep(qk, gates):
    heads, tokens, _ = gates.shape
    count = tokens // CHUNK
    group = min(4, count)
    rows = group * CHUNK
    low = jax.ShapeDtypeStruct((heads, count, CHUNK, CHUNK), F32)
    wide = jax.ShapeDtypeStruct((heads, count, DK, DK), F32)
    out_spec = spec((1, group, CHUNK, CHUNK), lambda h, g: (h, g, 0, 0))
    return pl.pallas_call(
        functools.partial(prep_kernel, group),
        grid=(heads, count // group),
        in_specs=[
            spec((rows, 2 * DK), lambda h, g: (g, 2 * h)),
            spec((1, rows, GATE_LANES), lambda h, g: (h, g, 0)),
        ],
        out_specs=[out_spec] * 10,
        out_shape=[low] * 8 + [wide] * 2,
        compiler_params=params(),
        cost_estimate=cost(heads * count * 40 * 2 * CHUNK**3 * 8, heads * count * CHUNK * CHUNK * 24),
        name="delta_prep",
    )(qk, gates)


def trans_kernel(heads, count, m_ref, mt_ref, fwd_ref, back_ref):
    row, col = rows_cols()
    eye = jnp.where(row == col, 1.0, 0.0)
    fwd = [eye] * heads
    back = [eye] * heads
    for h in range(heads):
        fwd_ref[h, 0] = eye
        back_ref[h, count] = eye
    for c in range(count):
        if c == 0:
            fwd = [m_ref[h, 0] for h in range(heads)]
            back = [mt_ref[h, count - 1] for h in range(heads)]
        else:
            fwd = [d3(m_ref[h, c], fwd[h]) for h in range(heads)]
            back = [d3(mt_ref[h, count - 1 - c], back[h]) for h in range(heads)]
        for h in range(heads):
            fwd_ref[h, c + 1] = fwd[h]
            back_ref[h, count - 1 - c] = back[h]


def delta_trans(steps, steps_turned):
    heads, count = steps.shape[:2]
    shape = jax.ShapeDtypeStruct((heads, count + 1, DK, DK), F32)
    return pl.pallas_call(
        functools.partial(trans_kernel, heads, count),
        out_shape=[shape, shape],
        compiler_params=params(),
        cost_estimate=cost(heads * count * 6 * 2 * DK**3 * 8, heads * count * DK * DK * 16),
        name="delta_trans",
    )(steps, steps_turned)


def values_kernel(
    heads, group, qkv_ref, gt_ref, t_ref, a_ref, m_ref, ut_ref, o_ref, s_ref, end_ref, state
):
    @pl.when(pl.program_id(0) == 0)
    def _():
        state[...] = jnp.zeros_like(state)

    row, col = rows_cols()
    pairs = [(h, c) for c in range(group) for h in range(heads)]
    offsets = {}
    for h, c in pairs:
        at = slice(c * CHUNK, (c + 1) * CHUNK)
        beta, _, _, to_end = decay_parts(gt_ref[h, at, :], row, col)
        pseudo = dx(t_ref[h, c], beta * qkv_ref[at, (2 * h + 1) * DV : (2 * h + 2) * DV])
        ut_ref[h, c] = pseudo
        o_ref[at, h * DV : (h + 1) * DV] = dx(a_ref[h, c], pseudo)
        end_keys = to_end * qkv_ref[at, (4 * h + 1) * DK : (4 * h + 2) * DK]
        offsets[h, c] = dx(end_keys.T, pseudo)
    held = [state[h] for h in range(heads)]
    for c in range(group):
        for h in range(heads):
            s_ref[h, c] = held[h]
        held = [d3(m_ref[h, c], held[h]) + offsets[h, c] for h in range(heads)]
    for h in range(heads):
        state[h] = held[h]
        end_ref[h] = held[h]


def delta_values(qkv, gates, inverse, scores, steps):
    heads, tokens, _ = gates.shape
    count = tokens // CHUNK
    group = min(4, count)
    rows = group * CHUNK
    square = spec((heads, group, CHUNK, CHUNK), lambda g: (0, g, 0, 0))
    tall = spec((heads, group, CHUNK, DV), lambda g: (0, g, 0, 0))
    return pl.pallas_call(
        functools.partial(values_kernel, heads, group),
        grid=(count // group,),
        in_specs=[
            spec((rows, heads * 2 * DV), lambda g: (g, 0)),
            spec((heads, rows, GATE_LANES), lambda g: (0, g, 0)),
            square,
            square,
            square,
        ],
        out_specs=[
            tall,
            spec((rows, heads * DV), lambda g: (g, 0)),
            tall,
            spec((heads, DK, DV), lambda g: (0, 0, 0)),
        ],
        out_shape=[
            jax.ShapeDtypeStruct((heads, count, CHUNK, DV), F32),
            jax.ShapeDtypeStruct((tokens, heads * DV), F32),
            jax.ShapeDtypeStruct((heads, count, DK, DV), F32),
            jax.ShapeDtypeStruct((heads, DK, DV), F32),
        ],
        scratch_shapes=[pltpu.VMEM((heads, DK, DV), F32)],
        compiler_params=params(),
        cost_estimate=cost(heads * count * 12 * 2 * CHUNK**3 * 8, heads * count * CHUNK * 4000),
        name="delta_values",
    )(qkv, gates, inverse, scores, steps)


def output_kernel(
    heads, group, start_ref, s0_ref, tc_ref, p_ref, w_ref, ut_ref, o0_ref, gain_ref, *refs
):
    g_ref, mixed_ref, o_ref, s_ref, u_ref = refs
    for c in range(group):
        for h in range(heads):
            at = slice(c * CHUNK, (c + 1) * CHUNK)
            cols = slice(h * DV, (h + 1) * DV)
            held = s0_ref[h, c] + d3(tc_ref[h, c], start_ref[h])
            low = held
            s_ref[h, c] = low
            u_ref[h, c] = (ut_ref[h, c].astype(F32) - dx(w_ref[h, c], low))
            out = o0_ref[at, cols] + dx(p_ref[h, c], low)
            o_ref[at, cols] = out
            gate = g_ref[at, cols]
            inv = lax.rsqrt(jnp.mean(out * out, axis=-1, keepdims=True) + 1e-05)
            mixed = out * inv * gain_ref[h : h + 1, :] * (gate * jax.nn.sigmoid(gate))
            mixed_ref[at, cols] = mixed.astype(BF16)


def delta_output(start, states, trans, reach, wkeys, pseudo, local_out, raw, gain):
    heads, count = states.shape[:2]
    tokens = count * CHUNK
    group = min(2, count)
    rows = group * CHUNK
    square = spec((heads, group, CHUNK, CHUNK), lambda g: (0, g, 0, 0))
    tall = spec((heads, group, CHUNK, DV), lambda g: (0, g, 0, 0))
    flat = spec((rows, heads * DV), lambda g: (g, 0))
    low = jax.ShapeDtypeStruct((heads, count, CHUNK, DV), F32)
    return pl.pallas_call(
        functools.partial(output_kernel, heads, group),
        grid=(count // group,),
        in_specs=[
            spec((heads, DK, DV), lambda g: (0, 0, 0)),
            tall,
            square,
            square,
            square,
            tall,
            flat,
            spec((heads, DV), lambda g: (0, 0)),
        ]
        + [flat],
        out_specs=[flat, flat, tall, tall],
        out_shape=[
            jax.ShapeDtypeStruct((tokens, heads * DV), BF16),
            jax.ShapeDtypeStruct((tokens, heads * DV), F32),
            low,
            low,
        ],
        compiler_params=params(),
        cost_estimate=cost(heads * count * 10 * 2 * CHUNK**3 * 8, heads * count * CHUNK * 6000),
        name="delta_output",
    )(start, states, trans, reach, wkeys, pseudo, local_out, gain, raw)


def tail_kernel(
    heads, group, dm_ref, o_ref, gain_ref, pt_ref, mt_ref, *refs
):
    g_ref, do_ref, dg_ref, dgain_ref, ds_ref, dstart_ref, state = refs

    @pl.when(pl.program_id(0) == 0)
    def _():
        state[...] = jnp.zeros_like(state)
        dgain_ref[...] = jnp.zeros_like(dgain_ref)

    pushed = {}
    for c in range(group):
        for h in range(heads):
            at = slice(c * CHUNK, (c + 1) * CHUNK)
            cols = slice(h * DV, (h + 1) * DV)
            out = o_ref[at, cols]
            gate = g_ref[at, cols]
            back = dm_ref[at, cols]
            gain = gain_ref[h : h + 1, :]
            sig = jax.nn.sigmoid(gate)
            silu = gate * sig
            inv = lax.rsqrt(jnp.mean(out * out, axis=-1, keepdims=True) + 1e-05)
            hat = out * inv
            dgain_ref[h : h + 1, :] += jnp.sum(back * hat * silu, axis=0, keepdims=True)
            scaled = back * gain
            dg_ref[at, cols] = (scaled * hat * (sig * (1.0 + gate * (1.0 - sig)))).astype(BF16)
            dhat = scaled * silu
            dout = inv * (dhat - hat * jnp.mean(dhat * hat, axis=-1, keepdims=True))
            low = dout
            do_ref[at, cols] = low
            pushed[h, c] = dx(pt_ref[h, c], low)
    held = [state[h] for h in range(heads)]
    for c in reversed(range(group)):
        for h in range(heads):
            ds_ref[h, c] = held[h]
        held = [d3(mt_ref[h, c], held[h]) + pushed[h, c] for h in range(heads)]
    for h in range(heads):
        state[h] = held[h]
        dstart_ref[h] = held[h]


def delta_tail(grad_mixed, outs, raw, gain, reach_turned, steps_turned):
    heads, count = steps_turned.shape[:2]
    tokens = count * CHUNK
    group = min(2, count)
    rows = group * CHUNK
    last = count // group - 1
    square = spec((heads, group, CHUNK, CHUNK), lambda g: (0, last - g, 0, 0))
    tall = spec((heads, group, CHUNK, DV), lambda g: (0, last - g, 0, 0))
    flat = spec((rows, heads * DV), lambda g: (last - g, 0))
    return pl.pallas_call(
        functools.partial(tail_kernel, heads, group),
        grid=(count // group,),
        in_specs=[flat, flat, spec((heads, DV), lambda g: (0, 0)), square, square]
        + [flat],
        out_specs=[
            flat,
            flat,
            spec((heads, DV), lambda g: (0, 0)),
            tall,
            spec((heads, DK, DV), lambda g: (0, 0, 0)),
        ],
        out_shape=[
            jax.ShapeDtypeStruct((tokens, heads * DV), F32),
            jax.ShapeDtypeStruct((tokens, heads * DV), BF16),
            jax.ShapeDtypeStruct((heads, DV), F32),
            jax.ShapeDtypeStruct((heads, count, DK, DV), F32),
            jax.ShapeDtypeStruct((heads, DK, DV), F32),
        ],
        scratch_shapes=[pltpu.VMEM((heads, DK, DV), F32)],
        compiler_params=params(),
        cost_estimate=cost(heads * count * 10 * 2 * CHUNK**3 * 8, heads * count * CHUNK * 6000),
        name="delta_tail",
    )(grad_mixed, outs, gain, reach_turned, steps_turned, raw)


def early_kernel(heads, group, at_ref, u_ref, s_ref, do_ref, da_ref, dqd_ref, dua_ref):
    pairs = [(h, c) for c in range(group) for h in range(heads)]
    douts = {
        (h, c): do_ref[c * CHUNK : (c + 1) * CHUNK, h * DV : (h + 1) * DV] for h, c in pairs
    }
    for h, c in pairs:
        da_ref[h, c] = dx(douts[h, c], u_ref[h, c], NT)
    for h, c in pairs:
        dqd_ref[h, c] = dx(douts[h, c], s_ref[h, c], NT)
    for h, c in pairs:
        dua_ref[h, c] = dx(at_ref[h, c], douts[h, c])


def delta_early(scores_turned, u, s, dout):
    heads, count = u.shape[:2]
    group = min(2, count)
    square = spec((heads, group, CHUNK, CHUNK), lambda g: (0, g, 0, 0))
    tall = spec((heads, group, CHUNK, DV), lambda g: (0, g, 0, 0))
    return pl.pallas_call(
        functools.partial(early_kernel, heads, group),
        grid=(count // group,),
        in_specs=[square, tall, tall, spec((group * CHUNK, heads * DV), lambda g: (g, 0))],
        out_specs=[square, square, tall],
        out_shape=[
            jax.ShapeDtypeStruct((heads, count, CHUNK, CHUNK), F32),
            jax.ShapeDtypeStruct((heads, count, CHUNK, DK), F32),
            jax.ShapeDtypeStruct((heads, count, CHUNK, DV), F32),
        ],
        compiler_params=params(),
        cost_estimate=cost(heads * count * 30 * 2 * CHUNK**3, heads * count * CHUNK * 4000),
        name="delta_early",
    )(scores_turned, u, s, dout)


def grads_kernel(
    heads, group, end_ref, qkv_ref, gt_ref, tt_ref, a_ref, lk_ref, u_ref, s_ref,
    ds_ref, back_ref, da_ref, dqd_ref, dua_ref, dqkv_ref, dgt_ref,
):
    row, col = rows_cols()
    lane = lax.broadcasted_iota(jnp.int32, (CHUNK, GATE_LANES), 1)
    pairs = [(h, c) for c in range(group) for h in range(heads)]
    at = {(h, c): slice(c * CHUNK, (c + 1) * CHUNK) for h, c in pairs}
    parts = {(h, c): decay_parts(gt_ref[h, at[h, c], :], row, col) for h, c in pairs}
    keys = {(h, c): qkv_ref[at[h, c], (4 * h + 1) * DK : (4 * h + 2) * DK] for h, c in pairs}
    queries = {(h, c): qkv_ref[at[h, c], 4 * h * DK : (4 * h + 1) * DK] for h, c in pairs}
    vals = {(h, c): qkv_ref[at[h, c], (2 * h + 1) * DV : (2 * h + 2) * DV] for h, c in pairs}
    after = {(h, c): ds_ref[h, c] + d3(back_ref[h, c], end_ref[h]) for h, c in pairs}
    du = {
        (h, c): dua_ref[h, c] + dx(parts[h, c][3] * keys[h, c], after[h, c]) for h, c in pairs
    }
    x = {(h, c): dx(tt_ref[h, c], du[h, c]) for h, c in pairs}
    y = {(h, c): -dx(x[h, c], s_ref[h, c], NT) for h, c in pairs}
    da = {(h, c): da_ref[h, c] for h, c in pairs}
    dqd = {(h, c): dqd_ref[h, c] for h, c in pairs}
    dke = {(h, c): dx(u_ref[h, c], after[h, c], NT) for h, c in pairs}
    dl = {(h, c): dx(x[h, c], u_ref[h, c], NT) for h, c in pairs}
    for h, c in pairs:
        p = (h, c)
        beta, decays, carried, to_end = parts[p]
        key, query = keys[p], queries[p]
        kept = lk_ref[h, c].astype(F32)
        low_grad = jnp.where(row > col, -dl[p], 0.0)
        dg = jnp.sum(s_ref[h, c].astype(F32) * after[p], axis=0, keepdims=True)
        dg = jnp.sum(dg, axis=1, keepdims=True)
        yk = jnp.sum(y[p] * key, axis=-1, keepdims=True)
        dbeta = jnp.sum(x[p] * vals[p], axis=-1, keepdims=True) + carried * yk
        dbeta = dbeta + jnp.sum(low_grad * kept, axis=-1, keepdims=True)
        dcarried = beta * yk + jnp.sum(dqd[p] * query, axis=-1, keepdims=True)
        dend = jnp.sum(dke[p] * key, axis=-1, keepdims=True) * to_end
        scaled = low_grad * beta
        gram = scaled * decays
        score = da[p] * decays
        dqkv_ref[at[p], (2 * h + 1) * DV : (2 * h + 2) * DV] = beta * x[p]
        dqkv_ref[at[p], 4 * h * DK : (4 * h + 1) * DK] = carried * dqd[p] + dx(score, key)
        dqkv_ref[at[p], (4 * h + 1) * DK : (4 * h + 2) * DK] = (
            (beta * carried) * y[p]
            + to_end * dke[p]
            + dx(gram + gram.T, key)
            + dx(score.T, query)
        )
        spread = scaled * kept + da[p] * a_ref[h, c].astype(F32)
        dcum = jnp.sum(spread, axis=-1, keepdims=True)
        dcum = dcum - to_col(jnp.sum(spread, axis=0, keepdims=True), row, col)
        dcum = dcum - dend + dcarried * carried
        tail = jnp.sum(dend, axis=0, keepdims=True) + dg * carried[CHUNK - 1 : CHUNK]
        line = jnp.sum(jnp.where(row >= col, dcum, 0.0), axis=0, keepdims=True) + tail
        dlog = to_col(line, row, col)
        dgt_ref[h, at[p], :] = jnp.where(lane == 0, dlog, jnp.where(lane == 1, dbeta, 0.0))


def delta_grads(grad_end, qkv, gates, inv_turned, scores, kept, u, s, ds, back, early):
    heads, tokens, _ = gates.shape
    count = tokens // CHUNK
    group = min(2, count)
    rows = group * CHUNK
    square = spec((heads, group, CHUNK, CHUNK), lambda g: (0, g, 0, 0))
    tall = spec((heads, group, CHUNK, DV), lambda g: (0, g, 0, 0))
    gate_spec = spec((heads, rows, GATE_LANES), lambda g: (0, g, 0))
    wide = spec((rows, heads * 2 * DV), lambda g: (g, 0))
    return pl.pallas_call(
        functools.partial(grads_kernel, heads, group),
        grid=(count // group,),
        in_specs=[
            spec((heads, DK, DV), lambda g: (0, 0, 0)),
            wide,
            gate_spec,
            square,
            square,
            square,
            tall,
            tall,
            tall,
            square,
            square,
            square,
            tall,
        ],
        out_specs=[wide, gate_spec],
        out_shape=[
            jax.ShapeDtypeStruct((tokens, heads * 2 * DV), F32),
            jax.ShapeDtypeStruct((heads, tokens, GATE_LANES), F32),
        ],
        compiler_params=params(),
        cost_estimate=cost(heads * count * 30 * 2 * CHUNK**3 * 8, heads * count * CHUNK * 12000),
        name="delta_grads",
    )(grad_end, qkv, gates, inv_turned, scores, kept, u, s, ds, back, *early)


def front_act(x, rim, mask_ref, taps):
    extended = jnp.concatenate([rim, x], axis=0)
    conv = taps[0:1] * x
    for lag in range(1, 4):
        moved = pltpu.roll(extended, lag, 0)[8:]
        conv = conv + taps[lag : lag + 1] * (moved * mask_ref[:, 3 + lag : 4 + lag])
    return conv


def front_kernel(x_ref, rim_ref, mask_ref, taps_ref, y_ref, conv_ref):
    conv = front_act(x_ref[...], rim_ref[8:, :], mask_ref, taps_ref[...])
    conv_ref[...] = conv
    act = conv * jax.nn.sigmoid(conv)
    kind = pl.program_id(0) & 3

    @pl.when(kind < 2)
    def _():
        inv = lax.rsqrt(jnp.sum(act * act, axis=-1, keepdims=True) + 1e-06)
        y_ref[...] = act * (inv * jnp.where(kind == 0, DK**-0.5, 1.0))

    @pl.when(kind >= 2)
    def _():
        y_ref[...] = act


def front(raw, rim, masks, taps):
    tokens, cols = raw.shape[0], taps.shape[1]
    block = spec((tokens, DK), lambda c: (0, c))
    return pl.pallas_call(
        front_kernel,
        grid=(cols // DK,),
        in_specs=[
            spec((tokens, DK), lambda c: (0, c)),
            spec((16, DK), lambda c: (0, c)),
            spec((tokens, 8), lambda c: (0, 0)),
            spec((4, DK), lambda c: (0, c)),
        ],
        out_specs=[block, block],
        out_shape=[jax.ShapeDtypeStruct((tokens, cols), F32)] * 2,
        compiler_params=params(),
        cost_estimate=cost(tokens * cols * 40, tokens * cols * 8),
        name="front",
    )(raw, rim, masks, taps)


def conv_back(kind, conv, back):
    sig = jax.nn.sigmoid(conv)
    if kind < 2:
        act = conv * sig
        inv = lax.rsqrt(jnp.sum(act * act, axis=-1, keepdims=True) + 1e-06)
        unit = act * inv
        back = back * (DK**-0.5 if kind == 0 else 1.0)
        back = inv * (back - unit * jnp.sum(back * unit, axis=-1, keepdims=True))
    return back * (sig * (1.0 + conv * (1.0 - sig)))


def front_back_kernel(
    x_ref, rim_ref, conv_ref, mask_ref, taps_ref, dy_ref, dg_ref, dx_ref, edge_ref, dtaps_ref
):
    tokens = x_ref.shape[0]
    kind = lax.rem(pl.program_id(0), 6)

    @pl.when(kind >= 4)
    def _():
        grad = dg_ref[...]
        dx_ref[...] = grad
        edge_ref[...] = grad[tokens - 16 :].astype(F32)
        dtaps_ref[...] = jnp.zeros((4, DK), F32)

    def through(which):
        taps = taps_ref[...]
        x = x_ref[...]
        dconv = conv_back(which, conv_ref[...], dy_ref[...])
        extended = jnp.concatenate([rim_ref[8:, :], x], axis=0)
        zeros = jnp.zeros((8, DK), F32)
        total = taps[0:1] * dconv
        dtaps_ref[0:1, :] = jnp.sum(dconv * x, axis=0, keepdims=True)
        for lag in range(1, 4):
            part = jnp.concatenate([zeros, dconv * mask_ref[:, 3 + lag : 4 + lag]], axis=0)
            part = pltpu.roll(part, tokens + 8 - lag, 0)
            dtaps_ref[lag : lag + 1, :] = jnp.sum(part * extended, axis=0, keepdims=True)
            total = total + taps[lag : lag + 1] * part[8:]
        dx_ref[...] = total.astype(BF16)
        edge_ref[...] = total[tokens - 16 :]

    for which in range(3):

        @pl.when((kind == which) | ((which == 2) & (kind == 3)))
        def _():
            through(which)


def rim_back_kernel(heads, conv_ref, mask_ref, taps_ref, dy_ref, drim_ref):
    zeros = jnp.zeros((8, DK), F32)
    for h in range(heads):
        for kind in range(4):
            at = slice((4 * h + kind) * DK, (4 * h + kind + 1) * DK)
            taps = taps_ref[:, at]
            dconv = conv_back(kind, conv_ref[:, at], dy_ref[:, at])
            total = zeros
            for lag in range(1, 4):
                part = jnp.concatenate([zeros, dconv * mask_ref[:, 3 + lag : 4 + lag]], axis=0)
                total = total + taps[lag : lag + 1] * pltpu.roll(part, 16 - lag, 0)[:8]
            drim_ref[:, at] = total


def rim_back(conv, masks, taps, dqkv):
    cols = taps.shape[1]
    heads = cols // (4 * DK)
    return pl.pallas_call(
        functools.partial(rim_back_kernel, heads),
        out_shape=jax.ShapeDtypeStruct((8, cols), F32),
        compiler_params=params(),
        cost_estimate=cost(1000, 100000),
        name="rim_back",
    )(conv[:8], masks[:8], taps, dqkv[:8])


def act_block(c):
    return lax.div(c, 6) * 4 + jnp.minimum(lax.rem(c, 6), 3)


def gate_block(c):
    return lax.div(c, 6) * 2 + jnp.maximum(lax.rem(c, 6) - 4, 0)


def front_back(raw, rim, conv, masks, taps, dqkv, dg):
    tokens, cols = raw.shape[0], raw.shape[1] + dg.shape[1]
    block = spec((tokens, DK), lambda c: (0, c))
    act_spec = spec((tokens, DK), lambda c: (0, act_block(c)))
    return pl.pallas_call(
        front_back_kernel,
        grid=(cols // DK,),
        in_specs=[
            act_spec,
            spec((16, DK), lambda c: (0, act_block(c))),
            act_spec,
            spec((tokens, 8), lambda c: (0, 0)),
            spec((4, DK), lambda c: (0, act_block(c))),
            act_spec,
            spec((tokens, DK), lambda c: (0, gate_block(c))),
        ],
        out_specs=[
            block,
            spec((16, DK), lambda c: (0, c)),
            spec((4, DK), lambda c: (0, c)),
        ],
        out_shape=[
            jax.ShapeDtypeStruct((tokens, cols), BF16),
            jax.ShapeDtypeStruct((16, cols), F32),
            jax.ShapeDtypeStruct((4, cols), F32),
        ],
        compiler_params=params(),
        cost_estimate=cost(tokens * cols * 80, tokens * cols * 14),
        name="front_back",
    )(raw, rim, conv, masks, taps, dqkv, dg)


def flip(value, bit):
    count = lax.axis_size("mp")
    return lax.ppermute(value, "mp", [(i, i ^ (1 << bit)) for i in range(count)])


def bit_count():
    return lax.axis_size("mp").bit_length() - 1


def exchange(values, bits):
    values = lax.optimization_barrier(tuple(values))
    return lax.optimization_barrier(tuple(flip(v, b) for v, b in zip(values, bits)))


def gather_mp(share):
    bits = bit_count()
    half = share.shape[0] // 2
    orders = (list(range(bits - 1, 0, -1)), list(range(1, bits)))
    held = [share[w * half : (w + 1) * half][None] for w in range(2)]
    rels = [[0], [0]]
    for turn in range(bits - 1):
        now = [order[turn] for order in orders]
        got = exchange(held, now)
        held = [jnp.concatenate([h, g], axis=0) for h, g in zip(held, got)]
        rels = [rel + [r | (1 << bit) for r in rel] for rel, bit in zip(rels, now)]
    got = exchange(held, [0, 0])
    return [(h, g, rel) for h, g, rel in zip(held, got, rels)]


def gathered_specs(found, tile, tiles):
    specs = []
    for which, (held, other, rel) in enumerate(found):
        shape = (held.shape[0], tile, held.shape[2])
        if which == 0:
            index = lambda i, m: (0, jnp.minimum(i, tiles - 1), 0)
        else:
            index = lambda i, m: (0, jnp.maximum(i - tiles, 0), 0)
        specs += [spec(shape, index)] * 2
    return specs


def gathered_args(found):
    return [x for held, other, rel in found for x in (held, other)]


def gathered_blocks(found, refs, which):
    held, other = refs[2 * which], refs[2 * which + 1]
    rel = found[which][2]
    blocks = [(r, held[i].astype(F32)) for i, r in enumerate(rel)]
    return blocks + [(r | 1, other[i].astype(F32)) for i, r in enumerate(rel)]


def place(mp_ref, r, cols):
    return pl.ds(pl.multiple_of((mp_ref[0] ^ r) * cols, cols), cols)


def norm_kernel(rels, cols, tiles, mode, *refs):
    mp_ref, refs = refs[0], refs[1:]
    found = [(None, None, rel) for rel in rels]
    if mode == "plain":
        out_ref = refs[4]
    else:
        gain_ref, out_ref, inv_ref = refs[4:7]
    for which in range(2):

        @pl.when((pl.program_id(0) < tiles) == (which == 0))
        def _():
            blocks = gathered_blocks(found, refs, which)
            if mode == "plain":
                for r, x in blocks:
                    out_ref[:, place(mp_ref, r, cols)] = x.astype(BF16)
                return
            total = sum(jnp.sum(x * x, axis=-1, keepdims=True) for _, x in blocks)
            inv = lax.rsqrt(total * (1.0 / (cols * len(blocks))) + 1e-05)
            for r, x in blocks:
                at = place(mp_ref, r, cols)
                out_ref[:, at] = (x * inv * gain_ref[:, at]).astype(BF16)
            inv_ref[...] = jnp.broadcast_to(inv, inv_ref.shape)


def assemble(found, mp_pos, gain=None):
    half, cols = found[0][0].shape[1:]
    rels = [f[2] for f in found]
    width = cols * 2 * len(rels[0])
    tokens = 2 * half
    tile = min(256, half)
    tiles = half // tile
    mode = "plain" if gain is None else "norm"
    row_spec = spec((tile, width), lambda i, m: (i, 0))
    in_specs = gathered_specs(found, tile, tiles)
    out_specs = [row_spec]
    out_shape = [jax.ShapeDtypeStruct((tokens, width), BF16)]
    args = gathered_args(found)
    if gain is not None:
        in_specs.append(spec((1, width), lambda i, m: (0, 0)))
        args.append(gain.reshape(1, width))
        out_specs.append(spec((tile, 128), lambda i, m: (i, 0)))
        out_shape.append(jax.ShapeDtypeStruct((tokens, 128), F32))
    return pl.pallas_call(
        functools.partial(norm_kernel, rels, cols, tiles, mode),
        grid_spec=pltpu.PrefetchScalarGridSpec(
            num_scalar_prefetch=1,
            grid=(2 * tiles,),
            in_specs=in_specs,
            out_specs=out_specs,
        ),
        out_shape=out_shape,
        compiler_params=params(),
        cost_estimate=cost(tokens * width * 10, tokens * width * 4),
        name="assemble",
    )(mp_pos.reshape(1).astype(jnp.int32), *args)


def norm_back_kernel(rels, cols, tiles, *refs):
    mp_ref, refs = refs[0], refs[1:]
    found = [(None, None, rel) for rel in rels]
    grads, mids = refs[:4], refs[4:8]
    up_ref, gain_ref, own_grad_ref, own_mid_ref, out_ref, own_out_ref, dgain_ref = refs[8:]

    @pl.when(pl.program_id(0) == 0)
    def _():
        dgain_ref[...] = jnp.zeros_like(dgain_ref)

    for which in range(2):

        @pl.when((pl.program_id(0) < tiles) == (which == 0))
        def _():
            grad = gathered_blocks(found, grads, which)
            mid = gathered_blocks(found, mids, which)
            scale = 1.0 / (cols * len(grad))
            total = sum(jnp.sum(x * x, axis=-1, keepdims=True) for _, x in mid)
            inv = lax.rsqrt(total * scale + 1e-05)
            scaled = [(r, g * gain_ref[:, place(mp_ref, r, cols)]) for r, g in grad]
            mean = sum(
                jnp.sum(g * x, axis=-1, keepdims=True) for (_, g), (_, x) in zip(scaled, mid)
            )
            shrink = inv * inv * (mean * scale)
            for (r, g), (_, x) in zip(scaled, mid):
                at = place(mp_ref, r, cols)
                out_ref[:, at] = (up_ref[:, at].astype(F32) + inv * (g - x * shrink)).astype(BF16)
            at = place(mp_ref, 0, cols)
            own_grad, own_mid = own_grad_ref[...], own_mid_ref[...]
            own_out_ref[...] = up_ref[:, at].astype(F32) + inv * (
                own_grad * gain_ref[:, at] - own_mid * shrink
            )
            dgain_ref[...] += jnp.sum(own_grad * own_mid * inv, axis=0, keepdims=True)


def norm_back(found_grad, found_mid, full_grad, gain, own_grad, own_mid, mp_pos):
    half, cols = found_grad[0][0].shape[1:]
    rels = [f[2] for f in found_grad]
    tokens, width = full_grad.shape
    tile = min(256, half)
    tiles = half // tile
    row_spec = spec((tile, width), lambda i, m: (i, 0))
    own_spec = spec((tile, cols), lambda i, m: (i, 0))
    return pl.pallas_call(
        functools.partial(norm_back_kernel, rels, cols, tiles),
        grid_spec=pltpu.PrefetchScalarGridSpec(
            num_scalar_prefetch=1,
            grid=(2 * tiles,),
            in_specs=gathered_specs(found_grad, tile, tiles)
            + gathered_specs(found_mid, tile, tiles)
            + [row_spec, spec((1, width), lambda i, m: (0, 0)), own_spec, own_spec],
            out_specs=[row_spec, own_spec, spec((1, cols), lambda i, m: (0, 0))],
        ),
        out_shape=[
            jax.ShapeDtypeStruct((tokens, width), BF16),
            jax.ShapeDtypeStruct((tokens, cols), F32),
            jax.ShapeDtypeStruct((1, cols), F32),
        ],
        compiler_params=params(),
        cost_estimate=cost(tokens * width * 20, tokens * width * 8),
        name="norm_back",
    )(
        mp_pos.reshape(1).astype(jnp.int32),
        *gathered_args(found_grad),
        *gathered_args(found_mid),
        full_grad,
        gain.reshape(1, width),
        own_grad,
        own_mid,
    )


def block_kernel(terms, mp_ref, *refs):
    out_ref = refs[2 * terms]
    total = None
    for i in range(terms):
        part = d1(refs[2 * i][...], refs[2 * i + 1][...], NT)
        total = part if total is None else total + part
    out_ref[0] = total.astype(out_ref.dtype)


def left_index(start, g, m):
    return (0, start)


def right_index(parity, cols, rows, start, g, m):
    at = ((2 * g + parity) ^ m[0]) * cols
    if rows:
        at = at + lax.div(at, rows) * 16
    return (pl.multiple_of(at, 16), start)


def block_products(terms, mp_pos, cols, parity):
    tokens = terms[0][0].shape[0]
    count = lax.axis_size("mp") // 2
    in_specs, args, flops = [], [], 0
    for left, left_start, right, right_start, depth, rows in terms:
        in_specs.append(
            pl.BlockSpec(
                (pl.Element(tokens), pl.Element(depth)), functools.partial(left_index, left_start)
            )
        )
        index = functools.partial(right_index, parity, cols, rows, right_start)
        in_specs.append(pl.BlockSpec((pl.Element(cols), pl.Element(depth)), index))
        args += [left, right]
        flops += 2 * tokens * depth * cols * count
    return pl.pallas_call(
        functools.partial(block_kernel, len(terms)),
        grid_spec=pltpu.PrefetchScalarGridSpec(
            num_scalar_prefetch=1,
            grid=(count,),
            in_specs=in_specs,
            out_specs=spec((1, tokens, cols), lambda g, m: (g, 0, 0)),
        ),
        out_shape=jax.ShapeDtypeStruct((count, tokens, cols), BF16 if parity else F32),
        compiler_params=params(),
        cost_estimate=cost(flops, tokens * cols * count * 4),
        name="block_products",
    )(mp_pos.reshape(1).astype(jnp.int32), *args)


def reduce_mp(terms, mp_pos, cols):
    sent = flip(block_products(terms, mp_pos, cols, 1), 0)
    kept = block_products(terms, mp_pos, cols, 0)
    bits = bit_count()
    half = kept.shape[1] // 2
    orders = (list(range(1, bits)), list(range(bits - 1, 0, -1)))
    rels = [[2 * i for i in range(kept.shape[0])] for _ in orders]
    helds = []
    for which in range(2):
        at = slice(which * half, (which + 1) * half)
        helds.append({r: kept[i, at] + sent[i, at].astype(F32) for i, r in enumerate(rels[which])})
    for turn in range(bits - 1):
        aways = [[r for r in rels[w] if (r >> orders[w][turn]) & 1] for w in range(2)]
        gots = exchange(
            [jnp.stack([helds[w][r].astype(BF16) for r in aways[w]]) for w in range(2)],
            [orders[w][turn] for w in range(2)],
        )
        for w in range(2):
            bit = orders[w][turn]
            rels[w] = [r for r in rels[w] if not (r >> bit) & 1]
            helds[w] = {
                r: helds[w][r] + gots[w][aways[w].index(r | (1 << bit))].astype(F32) for r in rels[w]
            }
    return jnp.concatenate([helds[0][0], helds[1][0]], axis=0), kept


def sum_mp(value):
    for bit in range(bit_count()):
        value = value + flip(value, bit)
    return value


def sum_seq(value):
    count = lax.axis_size("seq")
    total = value
    for step in range(1, count):
        total = total + lax.ppermute(value, "seq", [(i, (i + step) % count) for i in range(count)])
    return total


def shifted(value, steps):
    count = lax.axis_size("seq")
    first, last = max(0, -steps), min(count, count - steps)
    return lax.ppermute(value, "seq", [(i, i + steps) for i in range(first, last)])


def batched(left, right):
    return jnp.einsum("hde,hev->hdv", left, right, precision=lax.Precision.HIGHEST)


def dot(left, right, dims=NN):
    return lax.dot_general(left, right, dims, preferred_element_type=F32)


TN = (((0,), (0,)), ((), ()))


def first_kernel(
    heads, count, rows, x_ref, rim_ref, w_ref, mask_ref, scale_ref, bias_ref,
    raw_ref, pre_ref, gate_ref, rim_raw_ref,
):
    @pl.when(pl.program_id(0) == 0)
    def _():
        total = None
        for s in range(count):
            at = s * (rows + 16)
            part = d1(rim_ref[:, s * rows : (s + 1) * rows], w_ref[at : at + rows, :])
            total = part if total is None else total + part
        rim_raw_ref[...] = total

    raw, pre = None, None
    for s in range(count):
        at = s * (rows + 16)
        part = x_ref[:, s * rows : (s + 1) * rows]
        left = d1(part, w_ref[at : at + rows, :])
        right = d1(part, w_ref[at + rows : at + rows + 16, :rows], NT)
        raw = left if raw is None else raw + left
        pre = right if pre is None else pre + right
    raw_ref[...] = raw
    pre_ref[...] = pre
    masks = mask_ref[...]
    lane = lax.broadcasted_iota(jnp.int32, masks.shape, 1)
    for h in range(heads):
        x = pre[:, 2 * h : 2 * h + 1] + bias_ref[h]
        soft = jnp.maximum(x, 0.0) + jnp.log1p(jnp.exp(-jnp.abs(x)))
        beta = jax.nn.sigmoid(pre[:, 2 * h + 1 : 2 * h + 2])
        gate_ref[h] = jnp.where(
            lane == 0, -scale_ref[h] * soft, jnp.where(lane == 1, beta, masks)
        )


def project_first(normed, rim, mixer, masks, scale, bias):
    tokens, width = normed.shape
    count = lax.axis_size("seq")
    rows, cols = mixer.shape[0] // count - 16, mixer.shape[1]
    heads = scale.shape[0]
    tile = 256
    scalar = pl.BlockSpec(memory_space=pltpu.SMEM)
    return pl.pallas_call(
        functools.partial(first_kernel, heads, count, rows),
        grid=(tokens // tile,),
        in_specs=[
            spec((tile, width), lambda i: (i, 0)),
            spec((16, width), lambda i: (0, 0)),
            spec(mixer.shape, lambda i: (0, 0)),
            spec((tile, 8), lambda i: (i, 0)),
            scalar,
            scalar,
        ],
        out_specs=[
            spec((tile, cols), lambda i: (i, 0)),
            spec((tile, 16), lambda i: (i, 0)),
            spec((heads, tile, 8), lambda i: (0, i, 0)),
            spec((16, cols), lambda i: (0, 0)),
        ],
        out_shape=[
            jax.ShapeDtypeStruct((tokens, cols), F32),
            jax.ShapeDtypeStruct((tokens, 16), F32),
            jax.ShapeDtypeStruct((heads, tokens, 8), F32),
            jax.ShapeDtypeStruct((16, cols), F32),
        ],
        compiler_params=params(),
        cost_estimate=cost(2 * tokens * width * cols, tokens * width * 2 + width * cols * 2),
        name="project_first",
    )(normed, rim, mixer, masks, scale, bias)


def gates_back_kernel(heads, pre_ref, dg_ref, scale_ref, bias_ref, low_ref, sums_ref):
    pre = pre_ref[...]
    lane = lax.broadcasted_iota(jnp.int32, pre.shape, 1)
    line = lax.broadcasted_iota(jnp.int32, (1, 128), 1)
    low = jnp.zeros(pre.shape, F32)
    for h in range(heads):
        x = pre[:, 2 * h : 2 * h + 1] + bias_ref[h]
        soft = jnp.maximum(x, 0.0) + jnp.log1p(jnp.exp(-jnp.abs(x)))
        beta = jax.nn.sigmoid(pre[:, 2 * h + 1 : 2 * h + 2])
        dlog = dg_ref[h][:, 0:1]
        dx = dlog * (-scale_ref[h] * jax.nn.sigmoid(x))
        db = dg_ref[h][:, 1:2] * (beta * (1.0 - beta))
        low = jnp.where(lane == 2 * h, dx, jnp.where(lane == 2 * h + 1, db, low))
        dscale = jnp.sum(-dlog * soft, axis=0, keepdims=True)
        dbias = jnp.sum(dx, axis=0, keepdims=True)
        sums_ref[h : h + 1, :] = jnp.where(line == 0, dscale, jnp.where(line == 1, dbias, 0.0))
    low_ref[...] = low.astype(BF16)


def gates_back(pre, dgates, scale, bias):
    tokens = pre.shape[0]
    heads = scale.shape[0]
    scalar = pl.BlockSpec(memory_space=pltpu.SMEM)
    whole = pl.BlockSpec(memory_space=pltpu.VMEM)
    return pl.pallas_call(
        functools.partial(gates_back_kernel, heads),
        in_specs=[whole, whole, scalar, scalar],
        out_specs=[whole, whole],
        out_shape=[
            jax.ShapeDtypeStruct((tokens, 16), BF16),
            jax.ShapeDtypeStruct((heads, 128), F32),
        ],
        compiler_params=params(),
        cost_estimate=cost(tokens * 1000, tokens * 1024),
        name="gates_back",
    )(pre, dgates, scale, bias)


def unpack(value, units):
    whole = units // 128 * 128
    rest = value[:, 2 * whole :]
    tail = units - whole
    gate = jnp.concatenate([value[:, :whole], rest[:, :tail]], axis=1)
    return gate, jnp.concatenate([value[:, whole : 2 * whole], rest[:, tail:]], axis=1)


def pack(gate, up):
    whole = gate.shape[1] // 128 * 128
    return jnp.concatenate(
        [gate[:, :whole], up[:, :whole], gate[:, whole:], up[:, whole:]], axis=1
    )


def ffn_kernel(units, x_ref, back_ref, gu_ref, hid_ref, dgu_ref):
    gate, up = unpack(d1(x_ref[...], gu_ref[...]), units)
    back = back_ref[...]
    sig = jax.nn.sigmoid(gate)
    silu = gate * sig
    hid_ref[...] = (silu * up).astype(BF16)
    dgu_ref[...] = pack(
        (back * up * sig * (1.0 + gate * (1.0 - sig))), (back * silu)
    ).astype(BF16)


def ffn(normed2, grad_hidden, gu_full):
    tokens, width = normed2.shape
    units = grad_hidden.shape[1]
    tile = 256
    row_spec = spec((tile, width), lambda i: (i, 0))
    return pl.pallas_call(
        functools.partial(ffn_kernel, units),
        grid=(tokens // tile,),
        in_specs=[
            row_spec,
            spec((tile, units), lambda i: (i, 0)),
            spec((width, 2 * units), lambda i: (0, 0)),
        ],
        out_specs=[
            spec((tile, units), lambda i: (i, 0)),
            spec((tile, 2 * units), lambda i: (i, 0)),
        ],
        out_shape=[
            jax.ShapeDtypeStruct((tokens, units), BF16),
            jax.ShapeDtypeStruct((tokens, 2 * units), BF16),
        ],
        compiler_params=params(),
        cost_estimate=cost(6 * tokens * width * units, tokens * width * 4 + width * units * 6),
        name="ffn",
    )(normed2, grad_hidden, gu_full)


def after(value, *earlier):
    return lax.optimization_barrier((value, earlier))[0]


def together(*values):
    return lax.optimization_barrier(values)


def chain(steps, ends, sign):
    total = shifted(ends.astype(BF16), sign).astype(F32)
    for _ in range(lax.axis_size("seq") - 2):
        total = shifted((batched(steps, total) + ends).astype(BF16), sign).astype(F32)
    return total


def scatter_seq(value, axis):
    return lax.psum_scatter(value, "seq", scatter_dimension=axis, tiled=True).astype(F32)


def shards(
    residual,
    attn_gain,
    w_mixer,
    w_gates,
    conv_taps,
    decay_scale,
    dt_bias,
    head_gain,
    w_out,
    ffn_gain,
    w_gate,
    w_up,
    w_down,
    out_grad,
    doc_ids,
):
    tokens, cols = residual.shape
    seq_count = lax.axis_size("seq")
    mp_count = lax.axis_size("mp")
    seq_pos = lax.axis_index("seq")
    mp_pos = lax.axis_index("mp")
    rows, heads = w_mixer.shape[:2]
    width = rows * seq_count

    padded = jnp.concatenate([jnp.full((3,), -1, jnp.int32), doc_ids])
    window = lax.dynamic_slice_in_dim(padded, seq_pos * tokens, tokens + 3)
    ids = window[3:]
    prior = jnp.repeat(window[2 : 2 + tokens].reshape(-1, CHUNK)[:, 0], CHUNK)
    same = [(window[3 - j : 3 - j + tokens] == ids).astype(F32) for j in range(1, 4)]
    ids_f, prior_f = ids.astype(F32), prior.astype(F32)
    zero = jnp.zeros((tokens,), F32)
    masks = jnp.stack([zero] * 2 + [ids_f, prior_f] + same + [zero], axis=1)

    units = w_gate.shape[1]
    feats = w_out.shape[0]
    act_cols, gate_cols = heads * 2 * DV, heads * DV
    gate_part = jnp.pad(
        w_gates.reshape(rows, 2 * heads).T, ((0, 16 - 2 * heads), (0, act_cols - rows))
    )
    act_part = w_mixer[:, :, : 2 * DV].reshape(rows, act_cols)
    act_full = lax.all_gather(
        jnp.concatenate([act_part, gate_part]), "seq", axis=0, tiled=True
    )
    found_res = gather_mp(residual)
    god_part = jnp.concatenate(
        [w_mixer[:, :, 2 * DV :].reshape(rows, gate_cols), w_out.T, w_down.T], axis=1
    )
    god_full = lax.all_gather(after(god_part, found_res[0][0]), "seq", axis=0, tiled=True)
    gu_part = pack(w_gate, w_up)

    normed, inv1 = assemble(found_res, mp_pos, attn_gain)
    rim_normed = shifted(normed[tokens - 16 :], 1)
    found_og = gather_mp(after(out_grad, normed))
    full_grad = assemble(found_og, mp_pos)[0]
    act_full = after(act_full, full_grad)
    raw, gate_pre, gates, rim = project_first(
        normed, rim_normed, act_full, masks, decay_scale, dt_bias
    )
    gu_full = lax.all_gather(after(gu_part, raw), "seq", axis=0, tiled=True)
    taps = conv_taps.reshape(4, act_cols)
    qkv, conv = front(raw, rim, masks, taps)

    inverse, inv_turned, scores, scores_turned, kept, wkeys, reach, reach_turned, steps, steps_turned = (
        delta_prep(qkv, gates)
    )
    trans, back = delta_trans(steps, steps_turned)
    pseudo, local_out, states, state_end = delta_values(qkv, gates, inverse, scores, steps)
    start = chain(trans[:, -1], state_end, 1)
    god_full = after(god_full, state_end)
    raw_gate = dot(normed, god_full[:, :gate_cols])
    out_turned = god_full[:, gate_cols : gate_cols + feats]
    down_turned = god_full[:, gate_cols + feats :]
    gates_full = jnp.swapaxes(
        act_full.reshape(seq_count, rows + 16, act_cols)[:, rows:, :rows], 0, 1
    ).reshape(16, width).T
    mixed, outs, held, corrected = delta_output(
        start, states, trans, reach, wkeys, pseudo, local_out, raw_gate, head_gain
    )

    mixed, out_turned, down_turned, gates_full = together(
        mixed, out_turned, down_turned, gates_full
    )
    branch, _ = reduce_mp([(mixed, 0, god_full, gate_cols, feats, 0)], mp_pos, cols)
    middle = residual.astype(F32) + branch
    found_mid = gather_mp(middle)
    normed2, _ = assemble(found_mid, mp_pos, ffn_gain)
    grad_hidden = dot(full_grad, after(down_turned, branch))
    gu_full = after(gu_full, grad_hidden, normed2)
    hidden, grad_gu = ffn(normed2, grad_hidden, gu_full)
    part_gu = dot(normed2, grad_gu, TN).astype(BF16)
    grad_gu = after(grad_gu, part_gu)
    grad_normed2, kept_gn2 = reduce_mp(
        [(grad_gu, 0, gu_full, 0, 2 * units, 0)], mp_pos, cols
    )
    dw_gu = lax.psum_scatter(part_gu, "seq", scatter_dimension=0, tiled=True)
    part_down = dot(after(hidden, kept_gn2), full_grad, TN).astype(BF16)
    found_gn2 = gather_mp(grad_normed2)

    grad_branch, grad_middle, dffn_gain = norm_back(
        found_gn2, found_mid, full_grad, ffn_gain, grad_normed2, middle, mp_pos
    )
    grad_mixed = dot(grad_branch, out_turned)

    dout, dg_raw, dhead_gain, dstates, dstart = delta_tail(
        grad_mixed, outs, raw_gate, head_gain, reach_turned, steps_turned
    )
    part_out = dot(mixed, after(grad_branch, dstart), TN).astype(BF16)
    part_do = jnp.concatenate([part_out, part_down])
    dw_do = lax.psum_scatter(part_do, "seq", scatter_dimension=1, tiled=True)
    early = delta_early(scores_turned, corrected, held, after(dout, dstart))
    grad_end = chain(back[:, 0], dstart, -1)
    grad_end = after(grad_end, part_do, early)
    dqkv, dgates = delta_grads(
        grad_end, qkv, gates, inv_turned, scores, kept, corrected, held, dstates, back[:, 1:],
        early,
    )
    drim = rim_back(conv, masks, taps, dqkv)
    came = shifted(drim, -1)
    dproj, edge, dtaps = front_back(raw, rim, conv, masks, taps, after(dqkv, drim), dg_raw)
    came = jnp.pad(came.reshape(8, heads, 2 * DV), ((0, 0), (0, 0), (0, DV))).reshape(8, -1)
    edge = jnp.concatenate([edge[:8], edge[8:] + came])
    dproj = lax.dynamic_update_slice_in_dim(dproj, edge.astype(BF16), tokens - 16, 0)
    dgate_low, gate_sums = gates_back(gate_pre, dgates, decay_scale, dt_bias)

    part_mixer = dot(normed, dproj, TN).astype(BF16)
    dw_mixer = lax.psum_scatter(part_mixer, "seq", scatter_dimension=0, tiled=True)
    dproj, dgate_low = after((dproj, dgate_low), part_mixer)
    part_gates = dot(dgate_low, normed, TN)
    terms = [(dgate_low, 0, gates_full, 0, 16, 0)]
    for h in range(heads):
        terms.append((dproj, 3 * h * DV, act_full, 2 * h * DV, 2 * DV, rows))
        terms.append((dproj, (3 * h + 2) * DV, god_full, h * DV, DV, 0))
    grad_normed, kept_gn = reduce_mp(terms, mp_pos, cols)
    ffn_part, _ = reduce_mp(
        [(after(hidden, kept_gn), 0, down_turned, 0, units, 0)], mp_pos, cols
    )
    output = (middle + ffn_part).astype(BF16)
    own_gain = lax.dynamic_slice_in_dim(attn_gain, mp_pos * cols, cols)
    own_res = residual.astype(F32)
    inv1 = inv1[:, :1]
    scaled = grad_normed * own_gain
    mean = jnp.sum(scaled * own_res, axis=-1).reshape(-1, 128)
    mean = sum_mp(mean).reshape(tokens, 1) * (1.0 / width)
    grad_residual = grad_middle + inv1 * (scaled - own_res * (inv1 * inv1 * mean))
    dattn_gain = jnp.sum(grad_normed * own_res * inv1, axis=0)

    dw_gate, dw_up = unpack(dw_gu, units)

    dtaps = dtaps.reshape(4, heads, 2 * DK + 2 * DV)[:, :, : 2 * DK + DV]
    small = [
        dattn_gain, dffn_gain, dhead_gain, gate_sums[:, 0], gate_sums[:, 1], dtaps,
        part_gates[: 2 * heads],
    ]
    packed = jnp.concatenate([value.reshape(-1) for value in small])
    packed = jnp.pad(packed, (0, -packed.shape[0] % 1024)).reshape(-1, 128)
    packed = sum_seq(packed).reshape(-1)
    sums, at = [], 0
    for value in small:
        sums.append(packed[at : at + value.size].reshape(value.shape))
        at += value.size
    gains = jnp.stack([sums[0], sums[1].reshape(-1)])
    gains = lax.dynamic_update_slice(jnp.zeros((2, width), F32), gains, (0, mp_pos * cols))
    gains = sum_mp(gains)
    dw_gates = lax.dynamic_slice_in_dim(sums[6], seq_pos * rows, rows, 1)
    return (
        output,
        grad_residual,
        gains[0],
        dw_mixer.astype(F32).reshape(rows, heads, 2 * DK + 2 * DV),
        dw_gates.T.reshape(rows, heads, 2),
        sums[5],
        sums[3],
        sums[4],
        sums[2],
        dw_do[: w_out.shape[0]].astype(F32),
        gains[1],
        dw_gate.astype(F32),
        dw_up.astype(F32),
        dw_do[w_out.shape[0] :].astype(F32),
    )


def solution(mesh):
    in_specs = (
        P("seq", "mp"),
        P(),
        P("seq", "mp", None),
        P("seq", "mp", None),
        P(None, "mp", None),
        P("mp"),
        P("mp"),
        P("mp", None),
        P("mp", "seq"),
        P(),
        P("seq", "mp"),
        P("seq", "mp"),
        P("mp", "seq"),
        P("seq", "mp"),
        P(),
    )
    out_specs = (
        P("seq", "mp"),
        P("seq", "mp"),
        P(),
        P("seq", "mp", None),
        P("seq", "mp", None),
        P(None, "mp", None),
        P("mp"),
        P("mp"),
        P("mp", None),
        P("mp", "seq"),
        P(),
        P("seq", "mp"),
        P("seq", "mp"),
        P("mp", "seq"),
    )
    return jax.shard_map(shards, mesh=mesh, in_specs=in_specs, out_specs=out_specs, check_vma=False)
```
